32 devices in a mesh: segment: 2 (over core), lon: 4 (over z), lat: 4 (over y, x).
Axes of the slice: x: 2, y: 2, z: 4, core: 2. Of those that a mesh axis runs over, the one named last changes fastest.
Arguments:
- dec_cot: bfloat16 [2, 64, 96, 128], P('segment', 'lon', 'lat'), may hold values from -6 to 6
- saved_conv: bfloat16 [2, 4, 64, 96, 256], P('segment', None, 'lon', 'lat'), may hold values from -6 to 6
- dec_weight: bfloat16 [256, 128], replicated, may hold values from -0.5 to 0.5
- w_in: bfloat16 [4, 256, 512], replicated, may hold values from -0.375 to 0.375
- w_out: bfloat16 [4, 512, 256], replicated, may hold values from -0.25 to 0.25
- conv_taps: float32 [4, 5, 256], replicated, may hold values from -3 to 3
- dilation: int32 [4], replicated, may hold values from 1 to 48, as said below
Outputs:
- in_adjoint: bfloat16 [2, 64, 96, 256], P('segment', 'lon', 'lat')
The draws below stay inside these ranges and needn't reach their ends.
Inputs may be any that keep to these rules, and one draw needn't show every extreme that they name: Every layer's dilation lies in 1 to 48; at least one layer has exactly 48.
All inputs are finite; a program needn't handle non-finite values.
Results may differ from the reference program's by a relative error of at most 0.013.
Values may be sent and summed in bfloat16 or wider, within the bound.
No kernel may reach another device: no remote copies, remote signals or barrier semaphores. Data moves between devices by JAX's collectives and lax.ppermute only.
A program may use at most 64 MiB of HBM per device.

```python
import jax
import jax.numpy as jnp
from jax import lax

C = 256
H = 512
V = 128
LAYERS = 4
CL = 16
NLON = 64
NLAT = 96
N_SEGMENT = 2


def draw_dilation(key, part):
    first_key, second_key = jax.random.split(jax.random.fold_in(key, 11))
    values = jax.random.randint(first_key, (LAYERS,), 1, 3 * CL + 1)
    chosen = jax.random.randint(second_key, (), 0, LAYERS)
    return jnp.where(jnp.arange(LAYERS) == chosen, 3 * CL, values).astype(jnp.int32)


def shard_levels(own_key, extent, shards, low, top_value):
    def one(position, parts):
        steps = jax.random.uniform(jax.random.fold_in(jax.random.fold_in(own_key, 6), position), (parts,), jnp.float32, low / len(shards), top_value / len(shards))
        return jnp.repeat(jnp.exp(steps), extent[position] // parts).reshape((-1,) + (1,) * (len(extent) - position - 1))

    gain = one(*shards[0])
    for cut in shards[1:]:
        gain = gain * one(*cut)
    return gain


def noise(stream_key, shape, width, bound, cuts=(), kind=jnp.bfloat16):
    gain = shard_levels(stream_key, shape, cuts, -0.22, 0.18) if cuts else 1.0
    result = jax.random.normal(stream_key, shape, jnp.float32) * width * gain
    return jnp.minimum(jnp.maximum(result, -bound), bound).astype(kind)


def setup_inputs(seed: int = 0) -> dict:
    seeds = jax.random.split(jax.random.key(seed), 8)
    dec_cot = noise(seeds[0], (N_SEGMENT, NLON, NLAT, V), 1.0, 6.0, ((0, 2), (1, 4), (2, 4)))
    saved_conv = noise(seeds[1], (N_SEGMENT, LAYERS, NLON, NLAT, C), 1.0, 6.0, ((0, 2), (2, 4), (3, 4)))
    dec_weight = noise(seeds[2], (C, V), V ** -0.5, 0.5)
    w_in = noise(seeds[3], (LAYERS, C, H), C ** -0.5, 0.375)
    w_out = noise(seeds[4], (LAYERS, H, C), H ** -0.5, 0.25)
    conv_taps = noise(seeds[5], (LAYERS, 5, C), 0.5, 3.0, (), jnp.float32)
    dilation = draw_dilation(jax.random.fold_in(seeds[7], 71), 0)
    return {"dec_cot": dec_cot, "saved_conv": saved_conv, "dec_weight": dec_weight, "w_in": w_in, "w_out": w_out, "conv_taps": conv_taps, "dilation": dilation}


def gelu_slope(hidden):
    normal_cdf = 0.5 * (1.0 + jax.scipy.special.erf(hidden * 0.7071067811865476))
    density = jnp.exp(-0.5 * hidden * hidden) * 0.3989422804014327
    return normal_cdf + hidden * density


def reference(dec_cot, saved_conv, dec_weight, w_in, w_out, conv_taps, dilation):
    results = []
    for slot_index in range(2):
        handed_cot = dec_cot[1 - slot_index].reshape(-1, V)
        handed = jnp.dot(handed_cot, dec_weight.T, preferred_element_type=jnp.float32).astype(jnp.bfloat16)
        gradient = lax.optimization_barrier(handed).astype(jnp.float32)
        for layer_index in reversed(range(LAYERS)):
            conv_out = saved_conv[slot_index, layer_index].reshape(-1, C)
            hidden = jnp.dot(conv_out, w_in[layer_index], preferred_element_type=jnp.float32)
            cot_low = gradient.astype(jnp.bfloat16)
            act_grad = jnp.dot(cot_low, w_out[layer_index].T, preferred_element_type=jnp.float32)
            pre_grad = (act_grad * gelu_slope(hidden)).astype(jnp.bfloat16)
            conv_grad = jnp.dot(pre_grad, w_in[layer_index].T, preferred_element_type=jnp.float32).astype(jnp.bfloat16)
            field = conv_grad.reshape(NLON, NLAT, C).astype(jnp.float32)
            taps_now = conv_taps[layer_index]
            offset = dilation[layer_index]
            lat_padded = jnp.pad(field, ((0, 0), (1, 1), (0, 0)))
            zonal = taps_now[0] * jnp.roll(field, -offset, axis=0) + taps_now[2] * jnp.roll(field, offset, axis=0)
            zonal = lax.optimization_barrier(zonal.astype(jnp.bfloat16)).astype(jnp.float32)
            tapped = zonal + taps_now[1] * field + taps_now[3] * lat_padded[:, 2:] + taps_now[4] * lat_padded[:, :-2]
            gradient = gradient + tapped.reshape(-1, C)
        results.append(gradient.reshape(NLON, NLAT, C).astype(jnp.bfloat16))
    return jnp.stack(results)
```

```python
import functools

import jax
import jax.numpy as jnp
from jax import lax
from jax.experimental import pallas as pl
from jax.experimental.pallas import tpu as pltpu
from jax.sharding import PartitionSpec as P

AXES = ("segment", "lon", "lat")


def with_halo(cells, sides, width):
    for axis, dim in sides:
        count = lax.axis_size(axis)
        ends = count - 1
        head = lax.slice_in_dim(cells, 0, width, axis=dim)
        tail = lax.slice_in_dim(cells, cells.shape[dim] - width, cells.shape[dim], axis=dim)
        cells = jnp.concatenate(
            [
                lax.ppermute(tail, axis, [(i, (i + 1) % count) for i in range(ends)]),
                cells,
                lax.ppermute(head, axis, [((i + 1) % count, i) for i in range(ends)]),
            ],
            axis=dim,
        )
    return cells


def from_behind(value, axis, steps):
    count = lax.axis_size(axis)
    pairs = [(source, (source + steps) % count) for source in range(count)]
    return lax.ppermute(value, axis, pairs)


def partner(block, axis):
    count = lax.axis_size(axis)
    return lax.ppermute(block, axis, [(i, i ^ 1) for i in range(count) if i ^ 1 < count])


def gelu_slope(hidden):
    normal_cdf = 0.5 * (1.0 + lax.erf(hidden * 0.7071067811865476))
    density = jnp.exp(-0.5 * hidden * hidden) * 0.3989422804014327
    return normal_cdf + hidden * density


def tap_adjoint(conv_grad, taps_now, offset):
    lon_cells = conv_grad.shape[0]
    lat_padded = with_halo(conv_grad, (("lat", 1),), 1)
    meridional = taps_now[3] * lat_padded[:, 2:] + taps_now[4] * lat_padded[:, :-2]
    centre = taps_now[1] * conv_grad
    rim_width = 3 * lon_cells
    pieces = []
    for distance in (3, 2, 1, 0, -1, -2, -3):
        pieces.append(conv_grad if distance == 0 else from_behind(conv_grad, "lon", distance))
    padded = jnp.concatenate(pieces, axis=0)
    ahead_cells = lax.dynamic_slice_in_dim(padded, rim_width + offset, lon_cells, 0)
    behind = lax.dynamic_slice_in_dim(padded, rim_width - offset, lon_cells, 0)
    zonal_sum = taps_now[0] * ahead_cells + taps_now[2] * behind
    zonal_sum = lax.optimization_barrier(zonal_sum.astype(jnp.bfloat16)).astype(jnp.float32)
    return zonal_sum + centre + meridional


def by_exchange(dec_cot, saved_conv, dec_weight, w_in, w_out, conv_taps, dilation):
    lon_cells, lat_rows, chans = saved_conv.shape[2:]
    own_cot = dec_cot[0].reshape(-1, dec_cot.shape[3])
    projected = jnp.einsum(
        "nv,cv->nc", own_cot, dec_weight, preferred_element_type=jnp.float32
    ).astype(jnp.bfloat16)
    gradient = lax.optimization_barrier(partner(projected, "segment")).astype(jnp.float32)
    for layer in reversed(range(w_in.shape[0])):
        conv_out = saved_conv[0, layer].reshape(-1, chans)
        hidden = jnp.dot(conv_out, w_in[layer], preferred_element_type=jnp.float32)
        act_grad = jnp.einsum(
            "nc,hc->nh",
            gradient.astype(jnp.bfloat16),
            w_out[layer],
            preferred_element_type=jnp.float32,
        )
        pre_grad = (act_grad * gelu_slope(hidden)).astype(jnp.bfloat16)
        conv_grad = jnp.einsum(
            "nh,ch->nc", pre_grad, w_in[layer], preferred_element_type=jnp.float32
        ).astype(jnp.bfloat16)
        tapped = tap_adjoint(
            conv_grad.reshape(lon_cells, lat_rows, chans), conv_taps[layer], dilation[layer]
        )
        gradient = gradient + tapped.reshape(-1, chans)
    return gradient.reshape(1, lon_cells, lat_rows, chans).astype(jnp.bfloat16)


def routed(value, hop):
    cores, cols, rows = (lax.axis_size(a) for a in AXES)
    pairs = []
    for c in range(cores):
        for z in range(cols):
            for j in range(rows):
                to = hop(c, z, j)
                if to is not None and 0 <= to[2] < rows:
                    pairs.append(((c * cols + z) * rows + j, (to[0] * cols + to[1]) * rows + to[2]))
    return lax.ppermute(value, AXES, pairs)


def row_chunks(low, high):
    count = max(1, (high - low) // 4)
    edges = [low + (high - low) * i // count for i in range(count + 1)]
    return list(zip(edges[:-1], edges[1:]))


def layer_kernel(layer, first, last, lat_size, *refs):
    refs = list(refs)
    offset_ref, row_ref = refs[:2]
    pieces = refs[2:6]
    refs = refs[6:]
    if first:
        cots, refs = refs[:4], refs[4:]
        dec_ref, refs = refs[0], refs[1:]
    else:
        grad_in, refs = refs[0], refs[1:]
    w_in, w_out, taps = refs[:3]
    out, cg = refs[3:5]
    cells = pieces[0].shape[1]
    lon = 4 * cells
    chans = w_in.shape[0]
    halves = [(h, slice(h * 128, (h + 1) * 128)) for h in range(chans // 128)]
    window = pieces[0].shape[0]
    offset = offset_ref[0]
    if first:
        grad = refs[5]
    for r0, r1 in row_chunks(0, window):
        count = (r1 - r0) * lon
        conv_out = jnp.concatenate([p[r0:r1] for p in pieces], axis=1).reshape(count, chans)
        hidden = jnp.dot(conv_out, w_in[...], preferred_element_type=jnp.float32)
        if first:
            cot = jnp.concatenate([p[r0:r1] for p in cots], axis=1).reshape(count, -1)
            handed = lax.dot_general(
                cot, dec_ref[...], (((1,), (1,)), ((), ())), preferred_element_type=jnp.float32
            ).astype(jnp.bfloat16)
            grad[r0:r1] = handed.astype(jnp.float32).reshape(r1 - r0, lon, chans)
            low = handed
        else:
            low = grad_in[r0:r1].reshape(count, chans).astype(jnp.bfloat16)
        act = lax.dot_general(
            low, w_out[...], (((1,), (1,)), ((), ())), preferred_element_type=jnp.float32
        )
        pre = (act * gelu_slope(hidden)).astype(jnp.bfloat16)
        conv_grad = lax.dot_general(
            pre, w_in[...], (((1,), (1,)), ((), ())), preferred_element_type=jnp.float32
        ).reshape(r1 - r0, lon, chans)
        for r in range(r0, r1):
            rows_here = conv_grad[r - r0]
            if r < layer + 1 or r >= window - (layer + 1):
                place = row_ref[0] + (r - layer - 1)
                inside = jnp.where((place >= 0) & (place < lat_size), 1.0, 0.0).astype(jnp.float32)
                rows_here = rows_here * inside
            for h, lanes in halves:
                cg[r, h, 0:lon] = rows_here[:, lanes]
                cg[r, h, lon : 2 * lon] = rows_here[:, lanes]

    def tap(r, carry):
        for h, lanes in halves:
            t = [taps[k : k + 1, lanes] for k in range(5)]
            total = t[0] * cg[r, h, pl.ds(offset, lon)] + t[2] * cg[r, h, pl.ds(lon - offset, lon)]
            total += t[1] * cg[r, h, 0:lon] + t[3] * cg[r + 1, h, 0:lon] + t[4] * cg[r - 1, h, 0:lon]
            if first:
                total += grad[r, :, lanes]
            else:
                total += grad_in[r, :, lanes]
            if last:
                out[r - 1, :, lanes] = total.astype(jnp.bfloat16)
            else:
                out[r - 1, :, lanes] = total
        return carry

    lax.fori_loop(1, window - 1, tap, 0, unroll=2)


def run_layer(layer, layers, lat_size, offset, row, pieces, cots, dec_weight, gradient, w_in, w_out, taps):
    first, last = layer == layers - 1, layer == 0
    window, cells, chans = pieces[0].shape
    lon = 4 * cells
    smem = pl.BlockSpec(memory_space=pltpu.SMEM)
    vmem = pl.BlockSpec(memory_space=pltpu.VMEM)
    args = [offset, row, *pieces]
    args += [*cots, dec_weight] if first else [gradient]
    args += [w_in, w_out, taps]
    if last:
        out = jax.ShapeDtypeStruct((window - 2, lon, chans), jnp.bfloat16)
    else:
        out = jax.ShapeDtypeStruct((window - 2, lon, chans), jnp.float32)
    scratch = [pltpu.VMEM((window, chans // 128, 2 * lon, 128), jnp.float32)]
    if first:
        scratch.append(pltpu.VMEM((window, lon, chans), jnp.float32))
    work = window * lon
    return pl.pallas_call(
        functools.partial(layer_kernel, layer, first, last, lat_size),
        out_shape=out,
        in_specs=[smem, smem] + [vmem] * (len(args) - 2),
        out_specs=vmem,
        scratch_shapes=scratch,
        compiler_params=pltpu.CompilerParams(vmem_limit_bytes=40 * 2**20),
        cost_estimate=pl.CostEstimate(
            flops=6 * work * chans * w_in.shape[1],
            bytes_accessed=work * chans * 10,
            transcendentals=2 * work * w_in.shape[1],
        ),
        name=f"layer_{layer}",
    )(*args)


def by_circles(dec_cot, saved_conv, dec_weight, w_in, w_out, conv_taps, dilation):
    layers = w_in.shape[0]
    cells, rows, chans = saved_conv.shape[2:]
    lat_size = rows * lax.axis_size("lat")
    segment, lon, lat = (lax.axis_index(a) for a in AXES)

    def home(c):
        return c + 1

    def gather(value):
        found = [value]
        for k in range(1, 4):
            found.append(
                routed(value, lambda c, z, j: (c, home(c), j) if z == (home(c) + k) % 4 else None)
            )
        return found

    cot = partner(dec_cot[0], "segment").transpose(1, 0, 2)
    conv = saved_conv[0].transpose(0, 2, 1, 3)
    tops, bottoms = [], []
    for layer in range(layers):
        tops.append(conv[layer, : layer + 1])
        bottoms.append(conv[layer, rows - layer - 1 :])
    cot_top = cot[:layers]
    cot_bottom = cot[rows - layers :]
    v = cot.shape[2]
    tops.append(jnp.concatenate([cot_top[0::2], cot_top[1::2]], axis=2))
    bottoms.append(jnp.concatenate([cot_bottom[0::2], cot_bottom[1::2]], axis=2))
    below = routed(jnp.concatenate(tops, axis=0), lambda c, z, j: (c, z, j - 1))
    above = routed(jnp.concatenate(bottoms, axis=0), lambda c, z, j: (c, z, j + 1))

    def wide(layer):
        start = layer * (layer + 1) // 2
        return jnp.concatenate(
            [above[start : start + layer + 1], conv[layer], below[start : start + layer + 1]], axis=0
        )

    def cot_rows(edge):
        pair = edge[layers * (layers + 1) // 2 :]
        return jnp.stack([pair[..., :v], pair[..., v:]], axis=1).reshape(layers, cells, v)

    wide_cot = jnp.concatenate([cot_rows(above), cot, cot_rows(below)], axis=0)
    both = gather(jnp.concatenate([wide(layers - 1), wide_cot], axis=2))
    pieces = {layers - 1: [b[..., :chans] for b in both]}
    cots = [b[..., chans:] for b in both]
    for layer in reversed(range(layers - 1)):
        pieces[layer] = gather(wide(layer))

    gradient = None
    row = (lat * rows).astype(jnp.int32).reshape(1)
    for layer in reversed(range(layers)):
        gradient = run_layer(
            layer, layers, lat_size, dilation[layer].reshape(1), row, pieces[layer], cots,
            dec_weight, gradient, w_in[layer], w_out[layer], conv_taps[layer],
        )

    result = jnp.where(lon == home(segment), gradient[:, :cells], 0)
    for k in range(1, 4):
        quarter = gradient[:, k * cells : (k + 1) * cells]
        result = result + routed(
            quarter, lambda c, z, j: (c, (z + k) % 4, j) if z == home(c) else None
        )
    return result.transpose(1, 0, 2)[None]


def solution(mesh):
    in_specs = (
        P("segment", "lon", "lat", None),
        P("segment", None, "lon", "lat", None),
        P(),
        P(),
        P(),
        P(),
        P(),
    )
    out_specs = P("segment", "lon", "lat", None)
    gathers = mesh.shape["lon"] == 4 and mesh.shape["segment"] == 2
    return jax.shard_map(
        by_circles if gathers else by_exchange,
        mesh=mesh,
        in_specs=in_specs,
        out_specs=out_specs,
        check_vma=False,
    )
```

```python
import functools

import jax
import jax.numpy as jnp
from jax import lax
from jax.experimental import pallas as pl
from jax.experimental.pallas import tpu as pltpu
from jax.sharding import PartitionSpec as P

AXES = ("segment", "lon", "lat")


def with_halo(cells, sides, width):
    for axis, dim in sides:
        count = lax.axis_size(axis)
        ends = count - 1
        head = lax.slice_in_dim(cells, 0, width, axis=dim)
        tail = lax.slice_in_dim(cells, cells.shape[dim] - width, cells.shape[dim], axis=dim)
        cells = jnp.concatenate(
            [
                lax.ppermute(tail, axis, [(i, (i + 1) % count) for i in range(ends)]),
                cells,
                lax.ppermute(head, axis, [((i + 1) % count, i) for i in range(ends)]),
            ],
            axis=dim,
        )
    return cells


def from_behind(value, axis, steps):
    count = lax.axis_size(axis)
    pairs = [(source, (source + steps) % count) for source in range(count)]
    return lax.ppermute(value, axis, pairs)


def partner(block, axis):
    count = lax.axis_size(axis)
    return lax.ppermute(block, axis, [(i, i ^ 1) for i in range(count) if i ^ 1 < count])


def gelu_slope(hidden):
    normal_cdf = 0.5 * (1.0 + lax.erf(hidden * 0.7071067811865476))
    density = jnp.exp(-0.5 * hidden * hidden) * 0.3989422804014327
    return normal_cdf + hidden * density


def tap_adjoint(conv_grad, taps_now, offset):
    lon_cells = conv_grad.shape[0]
    lat_padded = with_halo(conv_grad, (("lat", 1),), 1)
    meridional = taps_now[3] * lat_padded[:, 2:] + taps_now[4] * lat_padded[:, :-2]
    centre = taps_now[1] * conv_grad
    rim_width = 3 * lon_cells
    pieces = []
    for distance in (3, 2, 1, 0, -1, -2, -3):
        pieces.append(conv_grad if distance == 0 else from_behind(conv_grad, "lon", distance))
    padded = jnp.concatenate(pieces, axis=0)
    ahead_cells = lax.dynamic_slice_in_dim(padded, rim_width + offset, lon_cells, 0)
    behind = lax.dynamic_slice_in_dim(padded, rim_width - offset, lon_cells, 0)
    zonal_sum = taps_now[0] * ahead_cells + taps_now[2] * behind
    zonal_sum = lax.optimization_barrier(zonal_sum.astype(jnp.bfloat16)).astype(jnp.float32)
    return zonal_sum + centre + meridional


def by_exchange(dec_cot, saved_conv, dec_weight, w_in, w_out, conv_taps, dilation):
    lon_cells, lat_rows, chans = saved_conv.shape[2:]
    own_cot = dec_cot[0].reshape(-1, dec_cot.shape[3])
    projected = jnp.einsum(
        "nv,cv->nc", own_cot, dec_weight, preferred_element_type=jnp.float32
    ).astype(jnp.bfloat16)
    gradient = lax.optimization_barrier(partner(projected, "segment")).astype(jnp.float32)
    for layer in reversed(range(w_in.shape[0])):
        conv_out = saved_conv[0, layer].reshape(-1, chans)
        hidden = jnp.dot(conv_out, w_in[layer], preferred_element_type=jnp.float32)
        act_grad = jnp.einsum(
            "nc,hc->nh",
            gradient.astype(jnp.bfloat16),
            w_out[layer],
            preferred_element_type=jnp.float32,
        )
        pre_grad = (act_grad * gelu_slope(hidden)).astype(jnp.bfloat16)
        conv_grad = jnp.einsum(
            "nh,ch->nc", pre_grad, w_in[layer], preferred_element_type=jnp.float32
        ).astype(jnp.bfloat16)
        tapped = tap_adjoint(
            conv_grad.reshape(lon_cells, lat_rows, chans), conv_taps[layer], dilation[layer]
        )
        gradient = gradient + tapped.reshape(-1, chans)
    return gradient.reshape(1, lon_cells, lat_rows, chans).astype(jnp.bfloat16)


def routed(value, hop):
    cores, cols, rows = (lax.axis_size(a) for a in AXES)
    pairs = []
    for c in range(cores):
        for z in range(cols):
            for j in range(rows):
                to = hop(c, z, j)
                if to is not None and 0 <= to[2] < rows:
                    pairs.append(((c * cols + z) * rows + j, (to[0] * cols + to[1]) * rows + to[2]))
    return lax.ppermute(value, AXES, pairs)


def row_chunks(low, high):
    count = max(1, (high - low) // 4)
    edges = [low + (high - low) * i // count for i in range(count + 1)]
    return list(zip(edges[:-1], edges[1:]))


def on_home():
    return lax.axis_index("lon") == lax.axis_index("segment") + 1


def edge_start(layer):
    return layer * (layer + 1) // 2


def edges_kernel(layers, conv, cot, first_ref, top_ref, bottom_ref):
    rows, chans, v = cot.shape[0], conv.shape[3], cot.shape[2]
    first_ref[:, :, :chans] = conv[layers - 1]
    first_ref[:, :, chans:] = cot[...]
    for layer in range(layers):
        here = slice(edge_start(layer), edge_start(layer + 1))
        top_ref[here] = conv[layer, : layer + 1]
        bottom_ref[here] = conv[layer, rows - layer - 1 :]
    for k in range(layers):
        at, lanes = edge_start(layers) + k // 2, slice(k % 2 * v, (k % 2 + 1) * v)
        top_ref[at, :, lanes] = cot[k]
        bottom_ref[at, :, lanes] = cot[rows - layers + k]


def cut_edges(conv, cot):
    layers, rows, cells, chans = conv.shape
    edge = jax.ShapeDtypeStruct((edge_start(layers) + layers // 2, cells, chans), conv.dtype)
    first = jax.ShapeDtypeStruct((rows, cells, chans + cot.shape[2]), conv.dtype)
    vmem = pl.BlockSpec(memory_space=pltpu.VMEM)
    return pl.pallas_call(
        functools.partial(edges_kernel, layers),
        out_shape=(first, edge, edge),
        in_specs=[vmem, vmem],
        out_specs=(vmem, vmem, vmem),
        compiler_params=pltpu.CompilerParams(vmem_limit_bytes=16 * 2**20),
        name="edges",
    )(conv, cot)


def layer_kernel(layer, layers, slot, *refs):
    pl.when(on_home())(functools.partial(layer_body, layer, layers, slot, *refs))


def layer_body(layer, layers, slot, *refs):
    first, last = layer == layers - 1, layer == 0
    offset_ref, refs = refs[0], refs[1:]
    mains, halos, refs = refs[:4], refs[4:8], refs[8:]
    carried, w_in, w_out, taps, refs = refs[0], refs[1], refs[2], refs[3], refs[4:]
    outs, refs = (refs[:4], refs[4:]) if last else (refs[:1], refs[1:])
    cg = refs[0]
    rows, cells = mains[0].shape[-3:-1]
    chans = halos[0].shape[2]
    v = mains[0].shape[-1] - chans
    lon, wide = 4 * cells, layer + 1
    window = rows + 2 * wide
    halves = [(h, slice(h * 128, (h + 1) * 128)) for h in range(chans // 128)]
    half_halo = halos[0].shape[0] // 2
    offset = offset_ref[layer]
    lat = lax.axis_index("lat")
    has_above = jnp.where(lat > 0, 1.0, 0.0).astype(jnp.float32)
    has_below = jnp.where(lat < lax.axis_size("lat") - 1, 1.0, 0.0).astype(jnp.float32)

    def main_row(p, r):
        return mains[p][r] if slot is None else mains[p][slot, r]

    def conv_row(r):
        if r < wide:
            return [h[edge_start(layer) + r] for h in halos]
        if r < wide + rows:
            return [main_row(p, r - wide)[:, :chans] for p in range(4)]
        return [h[half_halo + edge_start(layer) + r - wide - rows] for h in halos]

    def cot_row(r):
        if wide <= r < wide + rows:
            return [main_row(p, r - wide)[:, chans:] for p in range(4)]
        k = r if r < wide else r - wide - rows
        at = edge_start(layers) + k // 2 + (0 if r < wide else half_halo)
        return [h[at, :, k % 2 * v : (k % 2 + 1) * v] for h in halos]

    def nt(a, b):
        return lax.dot_general(a, b, (((1,), (1,)), ((), ())), preferred_element_type=jnp.float32)

    def taps_of(r):
        for h, lanes in halves:
            t = [taps[layer, k : k + 1, lanes] for k in range(5)]
            total = t[0] * cg[r, h, pl.ds(offset, lon)] + t[2] * cg[r, h, pl.ds(lon - offset, lon)]
            total += t[1] * cg[r, h, 0:lon] + t[3] * cg[r + 1, h, 0:lon] + t[4] * cg[r - 1, h, 0:lon]
            if first:
                total += refs[1][r, :, lanes].astype(jnp.float32)
            else:
                total += carried[r, :, lanes]
            if last:
                low = total.astype(jnp.bfloat16)
                for p in range(4):
                    outs[p][r - 1, :, lanes] = low[p * cells : (p + 1) * cells]
            else:
                outs[0][r - 1, :, lanes] = total

    done = 1
    for r0, r1 in row_chunks(0, window):
        count = (r1 - r0) * lon
        conv_out = jnp.concatenate(sum([conv_row(r) for r in range(r0, r1)], []), axis=0)
        hidden = jnp.dot(conv_out, w_in[layer], preferred_element_type=jnp.float32)
        if first:
            cot = jnp.concatenate(sum([cot_row(r) for r in range(r0, r1)], []), axis=0)
            low = nt(cot, carried[...]).astype(jnp.bfloat16)
        else:
            low = carried[r0:r1].reshape(count, chans).astype(jnp.bfloat16)
        pre = (nt(low, w_out[layer]) * gelu_slope(hidden)).astype(jnp.bfloat16)
        conv_grad = nt(pre, w_in[layer]).reshape(r1 - r0, lon, chans)
        while done < r0 - 1:
            taps_of(done)
            done += 1
        if first:
            refs[1][r0:r1] = low.reshape(r1 - r0, lon, chans)
        for r in range(r0, r1):
            rows_here = conv_grad[r - r0]
            if r < wide:
                rows_here = rows_here * has_above
            if r >= wide + rows:
                rows_here = rows_here * has_below
            for h, lanes in halves:
                cg[r, h, 0:lon] = rows_here[:, lanes]
                cg[r, h, lon : 2 * lon] = rows_here[:, lanes]
    while done < window - 1:
        taps_of(done)
        done += 1


def run_layer(layer, layers, slot, offsets, mains, halos, carried, w_in, w_out, taps):
    first, last = layer == layers - 1, layer == 0
    rows, cells = mains[0].shape[-3:-1]
    chans = halos[0].shape[2]
    lon = 4 * cells
    window = rows + 2 * (layer + 1)
    smem = pl.BlockSpec(memory_space=pltpu.SMEM)
    vmem = pl.BlockSpec(memory_space=pltpu.VMEM)
    args = [offsets, *mains, *halos, carried, w_in, w_out, taps]
    if last:
        out = [jax.ShapeDtypeStruct((rows, cells, chans), jnp.bfloat16)] * 4
    else:
        out = [jax.ShapeDtypeStruct((window - 2, lon, chans), jnp.float32)]
    scratch = [pltpu.VMEM((window, chans // 128, 2 * lon, 128), jnp.float32)]
    if first:
        scratch.append(pltpu.VMEM((window, lon, chans), jnp.bfloat16))
    work = window * lon
    return pl.pallas_call(
        functools.partial(layer_kernel, layer, layers, slot),
        out_shape=out,
        in_specs=[smem] + [vmem] * (len(args) - 1),
        out_specs=[vmem] * len(out),
        scratch_shapes=scratch,
        compiler_params=pltpu.CompilerParams(vmem_limit_bytes=32 * 2**20),
        cost_estimate=pl.CostEstimate(
            flops=6 * work * chans * w_in.shape[2],
            bytes_accessed=work * chans * 10,
            transcendentals=2 * work * w_in.shape[2],
        ),
        name=f"layer_{layer}",
    )(*args)


def by_circles(dec_cot, saved_conv, dec_weight, w_in, w_out, conv_taps, dilation):
    layers = w_in.shape[0]

    def home(c):
        return c + 1

    def gather(value):
        found = [value]
        for k in range(1, 4):
            found.append(
                routed(value, lambda c, z, j: (c, home(c), j) if z == (home(c) + k) % 4 else None)
            )
        return found

    cot = partner(dec_cot[0], "segment").transpose(1, 0, 2)
    conv = saved_conv[0].transpose(0, 2, 1, 3)
    message, top, bottom = cut_edges(conv, cot)
    below = routed(top, lambda c, z, j: (c, z, j - 1))
    above = routed(bottom, lambda c, z, j: (c, z, j + 1))
    mains = {layers - 1: (None, gather(message))}
    halos = gather(jnp.concatenate([above, below], axis=0))
    mains[layers - 2] = (None, gather(conv[layers - 2]))
    rest = gather(conv[: layers - 2])
    for layer in range(layers - 2):
        mains[layer] = (layer, rest)

    carried = dec_weight
    for layer in reversed(range(layers)):
        slot, pieces = mains[layer]
        found = run_layer(
            layer, layers, slot, dilation, pieces, halos, carried, w_in, w_out, conv_taps
        )
        carried = found[0]

    result = jnp.where(on_home(), found[0], 0)
    for k in range(1, 4):
        result = result + routed(
            found[k], lambda c, z, j: (c, (z + k) % 4, j) if z == home(c) else None
        )
    return result.transpose(1, 0, 2)[None]


def solution(mesh):
    in_specs = (
        P("segment", "lon", "lat", None),
        P("segment", None, "lon", "lat", None),
        P(),
        P(),
        P(),
        P(),
        P(),
    )
    out_specs = P("segment", "lon", "lat", None)
    gathers = mesh.shape["lon"] == 4 and mesh.shape["segment"] == 2
    return jax.shard_map(
        by_circles if gathers else by_exchange,
        mesh=mesh,
        in_specs=in_specs,
        out_specs=out_specs,
        check_vma=False,
    )
```

```python
import functools

import jax
import jax.numpy as jnp
from jax import lax
from jax.experimental import pallas as pl
from jax.experimental.pallas import tpu as pltpu
from jax.sharding import PartitionSpec as P

AXES = ("segment", "lon", "lat")


def with_halo(cells, sides, width):
    for axis, dim in sides:
        count = lax.axis_size(axis)
        ends = count - 1
        head = lax.slice_in_dim(cells, 0, width, axis=dim)
        tail = lax.slice_in_dim(cells, cells.shape[dim] - width, cells.shape[dim], axis=dim)
        cells = jnp.concatenate(
            [
                lax.ppermute(tail, axis, [(i, (i + 1) % count) for i in range(ends)]),
                cells,
                lax.ppermute(head, axis, [((i + 1) % count, i) for i in range(ends)]),
            ],
            axis=dim,
        )
    return cells


def from_behind(value, axis, steps):
    count = lax.axis_size(axis)
    pairs = [(source, (source + steps) % count) for source in range(count)]
    return lax.ppermute(value, axis, pairs)


def partner(block, axis):
    count = lax.axis_size(axis)
    return lax.ppermute(block, axis, [(i, i ^ 1) for i in range(count) if i ^ 1 < count])


def gelu_slope(hidden):
    normal_cdf = 0.5 * (1.0 + lax.erf(hidden * 0.7071067811865476))
    density = jnp.exp(-0.5 * hidden * hidden) * 0.3989422804014327
    return normal_cdf + hidden * density


def tap_adjoint(conv_grad, taps_now, offset):
    lon_cells = conv_grad.shape[0]
    lat_padded = with_halo(conv_grad, (("lat", 1),), 1)
    meridional = taps_now[3] * lat_padded[:, 2:] + taps_now[4] * lat_padded[:, :-2]
    centre = taps_now[1] * conv_grad
    rim_width = 3 * lon_cells
    pieces = []
    for distance in (3, 2, 1, 0, -1, -2, -3):
        pieces.append(conv_grad if distance == 0 else from_behind(conv_grad, "lon", distance))
    padded = jnp.concatenate(pieces, axis=0)
    ahead_cells = lax.dynamic_slice_in_dim(padded, rim_width + offset, lon_cells, 0)
    behind = lax.dynamic_slice_in_dim(padded, rim_width - offset, lon_cells, 0)
    zonal_sum = taps_now[0] * ahead_cells + taps_now[2] * behind
    zonal_sum = lax.optimization_barrier(zonal_sum.astype(jnp.bfloat16)).astype(jnp.float32)
    return zonal_sum + centre + meridional


def by_exchange(dec_cot, saved_conv, dec_weight, w_in, w_out, conv_taps, dilation):
    lon_cells, lat_rows, chans = saved_conv.shape[2:]
    own_cot = dec_cot[0].reshape(-1, dec_cot.shape[3])
    projected = jnp.einsum(
        "nv,cv->nc", own_cot, dec_weight, preferred_element_type=jnp.float32
    ).astype(jnp.bfloat16)
    gradient = lax.optimization_barrier(partner(projected, "segment")).astype(jnp.float32)
    for layer in reversed(range(w_in.shape[0])):
        conv_out = saved_conv[0, layer].reshape(-1, chans)
        hidden = jnp.dot(conv_out, w_in[layer], preferred_element_type=jnp.float32)
        act_grad = jnp.einsum(
            "nc,hc->nh",
            gradient.astype(jnp.bfloat16),
            w_out[layer],
            preferred_element_type=jnp.float32,
        )
        pre_grad = (act_grad * gelu_slope(hidden)).astype(jnp.bfloat16)
        conv_grad = jnp.einsum(
            "nh,ch->nc", pre_grad, w_in[layer], preferred_element_type=jnp.float32
        ).astype(jnp.bfloat16)
        tapped = tap_adjoint(
            conv_grad.reshape(lon_cells, lat_rows, chans), conv_taps[layer], dilation[layer]
        )
        gradient = gradient + tapped.reshape(-1, chans)
    return gradient.reshape(1, lon_cells, lat_rows, chans).astype(jnp.bfloat16)


def routed(value, hop):
    cores, cols, rows = (lax.axis_size(a) for a in AXES)
    pairs = []
    for c in range(cores):
        for z in range(cols):
            for j in range(rows):
                to = hop(c, z, j)
                if to is not None and 0 <= to[2] < rows:
                    pairs.append(((c * cols + z) * rows + j, (to[0] * cols + to[1]) * rows + to[2]))
    return lax.ppermute(value, AXES, pairs)


def row_chunks(low, high):
    count = max(1, round((high - low) / 7))
    edges = [low + (high - low) * i // count for i in range(count + 1)]
    return list(zip(edges[:-1], edges[1:]))


def home(s):
    return s + 1


def on_low():
    return lax.axis_index("lon") == home(lax.axis_index("segment"))


def on_high():
    return lax.axis_index("lon") == home(1 - lax.axis_index("segment"))


def to_pair(step):
    def hop(c, z, j):
        if z == (home(c) + step - 1) % 4:
            return c, home(c), j
        if z == (home(c) + step + 1) % 4:
            return 1 - c, home(c), j

    return hop


def to_other(c, z, j):
    return (1 - c, z, j) if z in (home(0), home(1)) else None


def edge_to(step):
    def hop(c, z, j):
        if z == (home(c) + step) % 4:
            return c, home(c), j + 1
        if z == (home(c) + step + 2) % 4:
            return 1 - c, home(c), j - 1

    return hop


def back_from(piece):
    def hop(c, z, j):
        if z == home(c):
            return c, (home(c) - 1 + piece) % 4, j
        if z == home(1 - c):
            return 1 - c, (home(1 - c) + 1 + piece) % 4, j

    return hop


def edge_start(layer):
    return layer * (layer + 1) // 2


def edges_kernel(layers, conv, cot, *outs):
    early_ref, late_ref = outs[layers:]
    rows, chans, v = cot.shape[0], conv.shape[3], cot.shape[2]
    for layer in range(layers - 1):
        outs[layer][...] = conv[layer]
    outs[layers - 1][:, :, :chans] = conv[layers - 1]
    outs[layers - 1][:, :, chans:] = cot[...]

    def edges(top_ref, bottom_ref):
        for layer in range(layers):
            here = slice(edge_start(layer), edge_start(layer + 1))
            top_ref[here] = conv[layer, : layer + 1]
            bottom_ref[here] = conv[layer, rows - layer - 1 :]
        for k in range(layers):
            at, lanes = edge_start(layers) + k // 2, slice(k % 2 * v, (k % 2 + 1) * v)
            top_ref[at, :, lanes] = cot[k]
            bottom_ref[at, :, lanes] = cot[rows - layers + k]

    bottom_first = (lax.axis_index("lon") - home(lax.axis_index("segment")) + 4) % 4 < 2
    pl.when(bottom_first)(lambda: edges(late_ref, early_ref))
    pl.when(jnp.logical_not(bottom_first))(lambda: edges(early_ref, late_ref))


def cut_edges(conv, cot):
    layers, rows, cells, chans = conv.shape
    edge = jax.ShapeDtypeStruct((edge_start(layers) + layers // 2, cells, chans), conv.dtype)
    plain = jax.ShapeDtypeStruct((rows, cells, chans), conv.dtype)
    first = jax.ShapeDtypeStruct((rows, cells, chans + cot.shape[2]), conv.dtype)
    vmem = pl.BlockSpec(memory_space=pltpu.VMEM)
    return pl.pallas_call(
        functools.partial(edges_kernel, layers),
        out_shape=[plain] * (layers - 1) + [first, edge, edge],
        in_specs=[vmem, vmem],
        out_specs=[vmem] * (layers + 2),
        compiler_params=pltpu.CompilerParams(vmem_limit_bytes=16 * 2**20),
        name="edges",
    )(conv, cot)


def layer_kernel(layer, layers, *refs):
    pl.when(on_low() | on_high())(functools.partial(layer_body, layer, layers, *refs))


def layer_body(layer, layers, *refs):
    first, last = layer == layers - 1, layer == 0
    offset_ref, refs = refs[0], refs[1:]
    mains, halos, refs = refs[:4], refs[4:8], refs[8:]
    carried, w_in, w_out, taps, refs = refs[0], refs[1], refs[2], refs[3], refs[4:]
    outs, refs = (refs[:4], refs[4:]) if last else (refs[:1], refs[1:])
    cg = refs[0]
    rows, cells = mains[0].shape[:2]
    chans = halos[0].shape[2]
    v = mains[0].shape[2] - chans
    lon, wide, own = 4 * cells, layer + 1, rows // 2
    window = own + 2 * wide
    halves = [(h, slice(h * 128, (h + 1) * 128)) for h in range(chans // 128)]
    offset = offset_ref[layer]
    low = on_low()
    lat = lax.axis_index("lat")
    has_edge = jnp.where(low, lat > 0, lat < lax.axis_size("lat") - 1)
    has_edge = jnp.where(has_edge, 1.0, 0.0).astype(jnp.float32)

    def main_at(r):
        return jnp.where(low, r - wide, rows - 1 - (r - wide))

    def conv_row(r):
        if r < wide:
            at = edge_start(layer) + jnp.where(low, r, wide - 1 - r)
            return [h[at] for h in halos]
        return [m[main_at(r), :, :chans] for m in mains]

    def cot_row(r):
        if r < wide:
            base = edge_start(layers)
            pair = jnp.where(low, r // 2, (wide - 1 - r) // 2)
            here = [h[base + pair] for h in halos]
            left = jnp.where(low, r % 2, (wide - 1 - r) % 2) == 0
            return [jnp.where(left, h[:, :v], h[:, v:]) for h in here]
        return [m[main_at(r), :, chans:] for m in mains]

    def nt(a, b):
        return lax.dot_general(a, b, (((1,), (1,)), ((), ())), preferred_element_type=jnp.float32)

    tap = [[taps[layer, k : k + 1, lanes] for k in range(5)] for _, lanes in halves]
    for t in tap:
        t[3], t[4] = jnp.where(low, t[3], t[4]), jnp.where(low, t[4], t[3])

    def taps_of(r):
        for h, lanes in halves:
            t = tap[h]
            total = t[0] * cg[r, h, pl.ds(offset, lon)] + t[2] * cg[r, h, pl.ds(lon - offset, lon)]
            total += t[1] * cg[r, h, 0:lon] + t[3] * cg[r + 1, h, 0:lon] + t[4] * cg[r - 1, h, 0:lon]
            if first:
                total += refs[1][r, :, lanes].astype(jnp.float32)
            else:
                total += carried[r, :, lanes]
            if last:
                low_bits = total.astype(jnp.bfloat16)
                at = jnp.where(low, r - 1, own - r)
                for p in range(4):
                    outs[p][at, :, lanes] = low_bits[p * cells : (p + 1) * cells]
            else:
                outs[0][r - 1, :, lanes] = total

    done = 1
    for r0, r1 in row_chunks(0, window):
        count = (r1 - r0) * lon
        conv_out = jnp.concatenate(sum([conv_row(r) for r in range(r0, r1)], []), axis=0)
        hidden = jnp.dot(conv_out, w_in[layer], preferred_element_type=jnp.float32)
        if first:
            cot = jnp.concatenate(sum([cot_row(r) for r in range(r0, r1)], []), axis=0)
            cot_low = nt(cot, carried[...]).astype(jnp.bfloat16)
        else:
            cot_low = carried[r0:r1].reshape(count, chans).astype(jnp.bfloat16)
        pre = (nt(cot_low, w_out[layer]) * gelu_slope(hidden)).astype(jnp.bfloat16)
        conv_grad = nt(pre, w_in[layer]).reshape(r1 - r0, lon, chans)
        while done < r0 - 1:
            taps_of(done)
            done += 1
        if first:
            refs[1][r0:r1] = cot_low.reshape(r1 - r0, lon, chans)
        for r in range(r0, r1):
            rows_here = conv_grad[r - r0]
            if r < wide:
                rows_here = rows_here * has_edge
            for h, lanes in halves:
                cg[r, h, 0:lon] = rows_here[:, lanes]
                cg[r, h, lon : 2 * lon] = rows_here[:, lanes]
    while done < window - 1:
        taps_of(done)
        done += 1


def run_layer(layer, layers, offsets, mains, halos, carried, w_in, w_out, taps):
    first, last = layer == layers - 1, layer == 0
    rows, cells = mains[0].shape[:2]
    chans = halos[0].shape[2]
    lon = 4 * cells
    window = rows // 2 + 2 * (layer + 1)
    smem = pl.BlockSpec(memory_space=pltpu.SMEM)
    vmem = pl.BlockSpec(memory_space=pltpu.VMEM)
    args = [offsets, *mains, *halos, carried, w_in, w_out, taps]
    if last:
        out = [jax.ShapeDtypeStruct((rows // 2, cells, chans), jnp.bfloat16)] * 4
    else:
        out = [jax.ShapeDtypeStruct((window - 2, lon, chans), jnp.float32)]
    scratch = [pltpu.VMEM((window, chans // 128, 2 * lon, 128), jnp.float32)]
    if first:
        scratch.append(pltpu.VMEM((window, lon, chans), jnp.bfloat16))
    work = window * lon
    return pl.pallas_call(
        functools.partial(layer_kernel, layer, layers),
        out_shape=out,
        in_specs=[smem] + [vmem] * (len(args) - 1),
        out_specs=[vmem] * len(out),
        scratch_shapes=scratch,
        compiler_params=pltpu.CompilerParams(vmem_limit_bytes=24 * 2**20),
        cost_estimate=pl.CostEstimate(
            flops=6 * work * chans * w_in.shape[2],
            bytes_accessed=work * chans * 10,
            transcendentals=2 * work * w_in.shape[2],
        ),
        name=f"layer_{layer}",
    )(*args)


def by_circles(dec_cot, saved_conv, dec_weight, w_in, w_out, conv_taps, dilation):
    layers = w_in.shape[0]
    cot = partner(dec_cot[0], "segment").transpose(1, 0, 2)
    conv = saved_conv[0].transpose(0, 2, 1, 3)
    *messages, early, late = cut_edges(conv, cot)
    mains = {}
    for layer in reversed(range(layers)):
        own = [routed(messages[layer], to_pair(step)) for step in range(2)]
        mains[layer] = own + [routed(half, to_other) for half in own]
        if layer == layers - 1:
            edges = [routed(early if step < 2 else late, edge_to(step)) for step in range(4)]
            halos = [edges[3], *edges[:3]]

    carried = dec_weight
    for layer in reversed(range(layers)):
        found = run_layer(
            layer, layers, dilation, mains[layer], halos, carried, w_in, w_out, conv_taps
        )
        carried = found[0]

    parts = [routed(found[p], back_from(p)) for p in range(4)]
    before = (lax.axis_index("lon") - home(lax.axis_index("segment")) + 5) % 4 < 2
    one, two = parts[0] + parts[1], parts[2] + parts[3]
    result = jnp.concatenate([jnp.where(before, one, two), jnp.where(before, two, one)], axis=0)
    return result.transpose(1, 0, 2)[None]


def solution(mesh):
    in_specs = (
        P("segment", "lon", "lat", None),
        P("segment", None, "lon", "lat", None),
        P(),
        P(),
        P(),
        P(),
        P(),
    )
    out_specs = P("segment", "lon", "lat", None)
    gathers = mesh.shape["lon"] == 4 and mesh.shape["segment"] == 2
    return jax.shard_map(
        by_circles if gathers else by_exchange,
        mesh=mesh,
        in_specs=in_specs,
        out_specs=out_specs,
        check_vma=False,
    )
```

```python
import functools

import jax
import jax.numpy as jnp
from jax import lax
from jax.experimental import pallas as pl
from jax.experimental.pallas import tpu as pltpu
from jax.sharding import PartitionSpec as P

AXES = ("segment", "lon", "lat")


def with_halo(cells, sides, width):
    for axis, dim in sides:
        count = lax.axis_size(axis)
        ends = count - 1
        head = lax.slice_in_dim(cells, 0, width, axis=dim)
        tail = lax.slice_in_dim(cells, cells.shape[dim] - width, cells.shape[dim], axis=dim)
        cells = jnp.concatenate(
            [
                lax.ppermute(tail, axis, [(i, (i + 1) % count) for i in range(ends)]),
                cells,
                lax.ppermute(head, axis, [((i + 1) % count, i) for i in range(ends)]),
            ],
            axis=dim,
        )
    return cells


def from_behind(value, axis, steps):
    count = lax.axis_size(axis)
    pairs = [(source, (source + steps) % count) for source in range(count)]
    return lax.ppermute(value, axis, pairs)


def partner(block, axis):
    count = lax.axis_size(axis)
    return lax.ppermute(block, axis, [(i, i ^ 1) for i in range(count) if i ^ 1 < count])


def gelu_slope(hidden):
    normal_cdf = 0.5 * (1.0 + lax.erf(hidden * 0.7071067811865476))
    density = jnp.exp(-0.5 * hidden * hidden) * 0.3989422804014327
    return normal_cdf + hidden * density


def tap_adjoint(conv_grad, taps_now, offset):
    lon_cells = conv_grad.shape[0]
    lat_padded = with_halo(conv_grad, (("lat", 1),), 1)
    meridional = taps_now[3] * lat_padded[:, 2:] + taps_now[4] * lat_padded[:, :-2]
    centre = taps_now[1] * conv_grad
    rim_width = 3 * lon_cells
    pieces = []
    for distance in (3, 2, 1, 0, -1, -2, -3):
        pieces.append(conv_grad if distance == 0 else from_behind(conv_grad, "lon", distance))
    padded = jnp.concatenate(pieces, axis=0)
    ahead_cells = lax.dynamic_slice_in_dim(padded, rim_width + offset, lon_cells, 0)
    behind = lax.dynamic_slice_in_dim(padded, rim_width - offset, lon_cells, 0)
    zonal_sum = taps_now[0] * ahead_cells + taps_now[2] * behind
    zonal_sum = lax.optimization_barrier(zonal_sum.astype(jnp.bfloat16)).astype(jnp.float32)
    return zonal_sum + centre + meridional


def by_exchange(dec_cot, saved_conv, dec_weight, w_in, w_out, conv_taps, dilation):
    lon_cells, lat_rows, chans = saved_conv.shape[2:]
    own_cot = dec_cot[0].reshape(-1, dec_cot.shape[3])
    projected = jnp.einsum(
        "nv,cv->nc", own_cot, dec_weight, preferred_element_type=jnp.float32
    ).astype(jnp.bfloat16)
    gradient = lax.optimization_barrier(partner(projected, "segment")).astype(jnp.float32)
    for layer in reversed(range(w_in.shape[0])):
        conv_out = saved_conv[0, layer].reshape(-1, chans)
        hidden = jnp.dot(conv_out, w_in[layer], preferred_element_type=jnp.float32)
        act_grad = jnp.einsum(
            "nc,hc->nh",
            gradient.astype(jnp.bfloat16),
            w_out[layer],
            preferred_element_type=jnp.float32,
        )
        pre_grad = (act_grad * gelu_slope(hidden)).astype(jnp.bfloat16)
        conv_grad = jnp.einsum(
            "nh,ch->nc", pre_grad, w_in[layer], preferred_element_type=jnp.float32
        ).astype(jnp.bfloat16)
        tapped = tap_adjoint(
            conv_grad.reshape(lon_cells, lat_rows, chans), conv_taps[layer], dilation[layer]
        )
        gradient = gradient + tapped.reshape(-1, chans)
    return gradient.reshape(1, lon_cells, lat_rows, chans).astype(jnp.bfloat16)


def routed(value, hop):
    cores, cols, rows = (lax.axis_size(a) for a in AXES)
    pairs = []
    for c in range(cores):
        for z in range(cols):
            for j in range(rows):
                to = hop(c, z, j)
                if to is not None and 0 <= to[2] < rows:
                    pairs.append(((c * cols + z) * rows + j, (to[0] * cols + to[1]) * rows + to[2]))
    return lax.ppermute(value, AXES, pairs)


def row_chunks(low, high):
    count = max(1, round((high - low) / 7))
    edges = [low + (high - low) * i // count for i in range(count + 1)]
    return list(zip(edges[:-1], edges[1:]))


def on_home():
    return lax.axis_index("lon") == lax.axis_index("segment") + 1


def edge_start(layer):
    return layer * (layer + 1) // 2


def edges_kernel(layers, groups, conv, cot, *outs):
    *messages, top_ref, bottom_ref = outs
    rows, chans, v = cot.shape[0], conv.shape[3], cot.shape[2]
    for message, group in zip(messages, groups):
        for k, layer in enumerate(group):
            message[:, :, k * chans : (k + 1) * chans] = conv[layer]
    messages[0][:, :, len(groups[0]) * chans :] = cot[...]
    for layer in range(layers):
        here = slice(edge_start(layer), edge_start(layer + 1))
        top_ref[here] = conv[layer, : layer + 1]
        bottom_ref[here] = conv[layer, rows - layer - 1 :]
    for k in range(layers):
        at, lanes = edge_start(layers) + k // 2, slice(k % 2 * v, (k % 2 + 1) * v)
        top_ref[at, :, lanes] = cot[k]
        bottom_ref[at, :, lanes] = cot[rows - layers + k]


def cut_edges(groups, conv, cot):
    layers, rows, cells, chans = conv.shape
    edge = jax.ShapeDtypeStruct((edge_start(layers) + layers // 2, cells, chans), conv.dtype)
    widths = [len(group) * chans for group in groups]
    widths[0] += cot.shape[2]
    messages = [jax.ShapeDtypeStruct((rows, cells, width), conv.dtype) for width in widths]
    vmem = pl.BlockSpec(memory_space=pltpu.VMEM)
    return pl.pallas_call(
        functools.partial(edges_kernel, layers, groups),
        out_shape=messages + [edge, edge],
        in_specs=[vmem, vmem],
        out_specs=[vmem] * (len(groups) + 2),
        compiler_params=pltpu.CompilerParams(vmem_limit_bytes=16 * 2**20),
        name="edges",
    )(conv, cot)


def layer_kernel(layer, layers, place, *refs):
    pl.when(on_home())(functools.partial(layer_body, layer, layers, place, *refs))


def layer_body(layer, layers, place, *refs):
    first, last = layer == layers - 1, layer == 0
    offset_ref, refs = refs[0], refs[1:]
    mains, halos, refs = refs[:4], refs[4:8], refs[8:]
    carried, w_in, w_out, taps, refs = refs[0], refs[1], refs[2], refs[3], refs[4:]
    outs, refs = (refs[:4], refs[4:]) if last else (refs[:1], refs[1:])
    cg = refs[0]
    rows, cells = mains[0].shape[:2]
    chans = halos[0].shape[2]
    convs, cots = slice(place * chans, (place + 1) * chans), slice(2 * chans, mains[0].shape[2])
    v = cots.stop - cots.start
    lon, wide = 4 * cells, layer + 1
    window = rows + 2 * wide
    halves = [(h, slice(h * 128, (h + 1) * 128)) for h in range(chans // 128)]
    half_halo = halos[0].shape[0] // 2
    offset = offset_ref[layer]
    lat = lax.axis_index("lat")
    has_above = jnp.where(lat > 0, 1.0, 0.0).astype(jnp.float32)
    has_below = jnp.where(lat < lax.axis_size("lat") - 1, 1.0, 0.0).astype(jnp.float32)

    def conv_row(r):
        if r < wide:
            return [h[edge_start(layer) + r] for h in halos]
        if r < wide + rows:
            return [m[r - wide, :, convs] for m in mains]
        return [h[half_halo + edge_start(layer) + r - wide - rows] for h in halos]

    def cot_row(r):
        if wide <= r < wide + rows:
            return [m[r - wide, :, cots] for m in mains]
        k = r if r < wide else r - wide - rows
        at = edge_start(layers) + k // 2 + (0 if r < wide else half_halo)
        return [h[at, :, k % 2 * v : (k % 2 + 1) * v] for h in halos]

    def nt(a, b):
        return lax.dot_general(a, b, (((1,), (1,)), ((), ())), preferred_element_type=jnp.float32)

    def taps_of(r):
        for h, lanes in halves:
            t = [taps[layer, k : k + 1, lanes] for k in range(5)]
            total = t[0] * cg[r, h, pl.ds(offset, lon)] + t[2] * cg[r, h, pl.ds(lon - offset, lon)]
            total += t[1] * cg[r, h, 0:lon] + t[3] * cg[r + 1, h, 0:lon] + t[4] * cg[r - 1, h, 0:lon]
            if first:
                total += refs[1][r, :, lanes].astype(jnp.float32)
            else:
                total += carried[r, :, lanes]
            if last:
                low = total.astype(jnp.bfloat16)
                for p in range(4):
                    outs[p][r - 1, :, lanes] = low[p * cells : (p + 1) * cells]
            else:
                outs[0][r - 1, :, lanes] = total

    done = 1
    for r0, r1 in row_chunks(0, window):
        count = (r1 - r0) * lon
        conv_out = jnp.concatenate(sum([conv_row(r) for r in range(r0, r1)], []), axis=0)
        hidden = jnp.dot(conv_out, w_in[layer], preferred_element_type=jnp.float32)
        if first:
            cot = jnp.concatenate(sum([cot_row(r) for r in range(r0, r1)], []), axis=0)
            low = nt(cot, carried[...]).astype(jnp.bfloat16)
        else:
            low = carried[r0:r1].reshape(count, chans).astype(jnp.bfloat16)
        pre = (nt(low, w_out[layer]) * gelu_slope(hidden)).astype(jnp.bfloat16)
        conv_grad = nt(pre, w_in[layer]).reshape(r1 - r0, lon, chans)
        while done < r0 - 1:
            taps_of(done)
            done += 1
        if first:
            refs[1][r0:r1] = low.reshape(r1 - r0, lon, chans)
        for r in range(r0, r1):
            rows_here = conv_grad[r - r0]
            if r < wide:
                rows_here = rows_here * has_above
            if r >= wide + rows:
                rows_here = rows_here * has_below
            for h, lanes in halves:
                cg[r, h, 0:lon] = rows_here[:, lanes]
                cg[r, h, lon : 2 * lon] = rows_here[:, lanes]
    while done < window - 1:
        taps_of(done)
        done += 1


def run_layer(layer, layers, place, offsets, mains, halos, carried, w_in, w_out, taps):
    first, last = layer == layers - 1, layer == 0
    rows, cells = mains[0].shape[:2]
    chans = halos[0].shape[2]
    lon = 4 * cells
    window = rows + 2 * (layer + 1)
    smem = pl.BlockSpec(memory_space=pltpu.SMEM)
    vmem = pl.BlockSpec(memory_space=pltpu.VMEM)
    args = [offsets, *mains, *halos, carried, w_in, w_out, taps]
    if last:
        out = [jax.ShapeDtypeStruct((rows, cells, chans), jnp.bfloat16)] * 4
    else:
        out = [jax.ShapeDtypeStruct((window - 2, lon, chans), jnp.float32)]
    scratch = [pltpu.VMEM((window, chans // 128, 2 * lon, 128), jnp.float32)]
    if first:
        scratch.append(pltpu.VMEM((window, lon, chans), jnp.bfloat16))
    work = window * lon
    return pl.pallas_call(
        functools.partial(layer_kernel, layer, layers, place),
        out_shape=out,
        in_specs=[smem] + [vmem] * (len(args) - 1),
        out_specs=[vmem] * len(out),
        scratch_shapes=scratch,
        compiler_params=pltpu.CompilerParams(vmem_limit_bytes=32 * 2**20),
        cost_estimate=pl.CostEstimate(
            flops=6 * work * chans * w_in.shape[2],
            bytes_accessed=work * chans * 10,
            transcendentals=2 * work * w_in.shape[2],
        ),
        name=f"layer_{layer}",
    )(*args)


def by_circles(dec_cot, saved_conv, dec_weight, w_in, w_out, conv_taps, dilation):
    layers = w_in.shape[0]

    def home(c):
        return c + 1

    def gather(value):
        found = [value]
        for k in range(1, 4):
            found.append(
                routed(value, lambda c, z, j: (c, home(c), j) if z == (home(c) + k) % 4 else None)
            )
        return found

    cot = partner(dec_cot[0], "segment").transpose(1, 0, 2)
    conv = saved_conv[0].transpose(0, 2, 1, 3)
    groups = ((3, 2), (1, 0))
    early, late, top, bottom = cut_edges(groups, conv, cot)
    below = routed(top, lambda c, z, j: (c, z, j - 1))
    above = routed(bottom, lambda c, z, j: (c, z, j + 1))
    early = gather(early)
    halos = gather(jnp.concatenate([above, below], axis=0))
    late, *early = lax.optimization_barrier((late, *early))
    late = gather(late)
    mains = {3: (0, early), 2: (1, early), 1: (0, late), 0: (1, late)}

    carried = dec_weight
    for layer in reversed(range(layers)):
        place, pieces = mains[layer]
        found = run_layer(
            layer, layers, place, dilation, pieces, halos, carried, w_in, w_out, conv_taps
        )
        carried = found[0]

    result = jnp.where(on_home(), found[0], 0)
    for k in range(1, 4):
        result = result + routed(
            found[k], lambda c, z, j: (c, (z + k) % 4, j) if z == home(c) else None
        )
    return result.transpose(1, 0, 2)[None]


def solution(mesh):
    in_specs = (
        P("segment", "lon", "lat", None),
        P("segment", None, "lon", "lat", None),
        P(),
        P(),
        P(),
        P(),
        P(),
    )
    out_specs = P("segment", "lon", "lat", None)
    gathers = mesh.shape["lon"] == 4 and mesh.shape["segment"] == 2
    return jax.shard_map(
        by_circles if gathers else by_exchange,
        mesh=mesh,
        in_specs=in_specs,
        out_specs=out_specs,
        check_vma=False,
    )
```

```python
import functools

import jax
import jax.numpy as jnp
from jax import lax
from jax.experimental import pallas as pl
from jax.experimental.pallas import tpu as pltpu
from jax.sharding import PartitionSpec as P

AXES = ("segment", "lon", "lat")


def with_halo(cells, sides, width):
    for axis, dim in sides:
        count = lax.axis_size(axis)
        ends = count - 1
        head = lax.slice_in_dim(cells, 0, width, axis=dim)
        tail = lax.slice_in_dim(cells, cells.shape[dim] - width, cells.shape[dim], axis=dim)
        cells = jnp.concatenate(
            [
                lax.ppermute(tail, axis, [(i, (i + 1) % count) for i in range(ends)]),
                cells,
                lax.ppermute(head, axis, [((i + 1) % count, i) for i in range(ends)]),
            ],
            axis=dim,
        )
    return cells


def from_behind(value, axis, steps):
    count = lax.axis_size(axis)
    pairs = [(source, (source + steps) % count) for source in range(count)]
    return lax.ppermute(value, axis, pairs)


def partner(block, axis):
    count = lax.axis_size(axis)
    return lax.ppermute(block, axis, [(i, i ^ 1) for i in range(count) if i ^ 1 < count])


def gelu_slope(hidden):
    normal_cdf = 0.5 * (1.0 + lax.erf(hidden * 0.7071067811865476))
    density = jnp.exp(-0.5 * hidden * hidden) * 0.3989422804014327
    return normal_cdf + hidden * density


def tap_adjoint(conv_grad, taps_now, offset):
    lon_cells = conv_grad.shape[0]
    lat_padded = with_halo(conv_grad, (("lat", 1),), 1)
    meridional = taps_now[3] * lat_padded[:, 2:] + taps_now[4] * lat_padded[:, :-2]
    centre = taps_now[1] * conv_grad
    rim_width = 3 * lon_cells
    pieces = []
    for distance in (3, 2, 1, 0, -1, -2, -3):
        pieces.append(conv_grad if distance == 0 else from_behind(conv_grad, "lon", distance))
    padded = jnp.concatenate(pieces, axis=0)
    ahead_cells = lax.dynamic_slice_in_dim(padded, rim_width + offset, lon_cells, 0)
    behind = lax.dynamic_slice_in_dim(padded, rim_width - offset, lon_cells, 0)
    zonal_sum = taps_now[0] * ahead_cells + taps_now[2] * behind
    zonal_sum = lax.optimization_barrier(zonal_sum.astype(jnp.bfloat16)).astype(jnp.float32)
    return zonal_sum + centre + meridional


def by_exchange(dec_cot, saved_conv, dec_weight, w_in, w_out, conv_taps, dilation):
    lon_cells, lat_rows, chans = saved_conv.shape[2:]
    own_cot = dec_cot[0].reshape(-1, dec_cot.shape[3])
    projected = jnp.einsum(
        "nv,cv->nc", own_cot, dec_weight, preferred_element_type=jnp.float32
    ).astype(jnp.bfloat16)
    gradient = lax.optimization_barrier(partner(projected, "segment")).astype(jnp.float32)
    for layer in reversed(range(w_in.shape[0])):
        conv_out = saved_conv[0, layer].reshape(-1, chans)
        hidden = jnp.dot(conv_out, w_in[layer], preferred_element_type=jnp.float32)
        act_grad = jnp.einsum(
            "nc,hc->nh",
            gradient.astype(jnp.bfloat16),
            w_out[layer],
            preferred_element_type=jnp.float32,
        )
        pre_grad = (act_grad * gelu_slope(hidden)).astype(jnp.bfloat16)
        conv_grad = jnp.einsum(
            "nh,ch->nc", pre_grad, w_in[layer], preferred_element_type=jnp.float32
        ).astype(jnp.bfloat16)
        tapped = tap_adjoint(
            conv_grad.reshape(lon_cells, lat_rows, chans), conv_taps[layer], dilation[layer]
        )
        gradient = gradient + tapped.reshape(-1, chans)
    return gradient.reshape(1, lon_cells, lat_rows, chans).astype(jnp.bfloat16)


def routed(value, hop):
    cores, cols, rows = (lax.axis_size(a) for a in AXES)
    pairs = []
    for c in range(cores):
        for z in range(cols):
            for j in range(rows):
                to = hop(c, z, j)
                if to is not None and 0 <= to[2] < rows:
                    pairs.append(((c * cols + z) * rows + j, (to[0] * cols + to[1]) * rows + to[2]))
    return lax.ppermute(value, AXES, pairs)


def row_chunks(low, high):
    count = max(1, round((high - low) / 7))
    edges = [low + (high - low) * i // count for i in range(count + 1)]
    return list(zip(edges[:-1], edges[1:]))


def on_home():
    return lax.axis_index("lon") == lax.axis_index("segment") + 1


def edge_start(layer):
    return layer * (layer + 1) // 2


def edges_kernel(layers, groups, conv, cot, *outs):
    *messages, top_ref, bottom_ref = outs
    rows, chans, v = cot.shape[0], conv.shape[3], cot.shape[2]
    for message, group in zip(messages, groups):
        for k, layer in enumerate(group):
            message[:, :, k * chans : (k + 1) * chans] = conv[layer]
    messages[0][:, :, len(groups[0]) * chans :] = cot[...]
    for layer in range(layers):
        here = slice(edge_start(layer), edge_start(layer + 1))
        top_ref[here] = conv[layer, : layer + 1]
        bottom_ref[here] = conv[layer, rows - layer - 1 :]
    for k in range(layers):
        at, lanes = edge_start(layers) + k // 2, slice(k % 2 * v, (k % 2 + 1) * v)
        top_ref[at, :, lanes] = cot[k]
        bottom_ref[at, :, lanes] = cot[rows - layers + k]


def cut_edges(groups, conv, cot):
    layers, rows, cells, chans = conv.shape
    edge = jax.ShapeDtypeStruct((edge_start(layers) + layers // 2, cells, chans), conv.dtype)
    widths = [len(group) * chans for group in groups]
    widths[0] += cot.shape[2]
    messages = [jax.ShapeDtypeStruct((rows, cells, width), conv.dtype) for width in widths]
    vmem = pl.BlockSpec(memory_space=pltpu.VMEM)
    return pl.pallas_call(
        functools.partial(edges_kernel, layers, groups),
        out_shape=messages + [edge, edge],
        in_specs=[vmem, vmem],
        out_specs=[vmem] * (len(groups) + 2),
        compiler_params=pltpu.CompilerParams(vmem_limit_bytes=16 * 2**20),
        name="edges",
    )(conv, cot)


def nt(a, b):
    return lax.dot_general(a, b, (((1,), (1,)), ((), ())), preferred_element_type=jnp.float32)


def halves_of(chans):
    return [(h, slice(h * 128, (h + 1) * 128)) for h in range(chans // 128)]


def in_order(pieces):
    upward = lax.axis_index("segment") == 0
    own, one, two, three = pieces
    return [own, jnp.where(upward, one, three), two, jnp.where(upward, three, one)]


def conv_gradient(conv_out, cot_low, w_in, w_out):
    hidden = jnp.dot(conv_out, w_in, preferred_element_type=jnp.float32)
    pre = (nt(cot_low, w_out) * gelu_slope(hidden)).astype(jnp.bfloat16)
    return nt(pre, w_in)


def keep_row(cg, at, row):
    lon = row.shape[0]
    for h, lanes in halves_of(row.shape[1]):
        cg[at, h, 0:lon] = row[:, lanes]
        cg[at, h, lon : 2 * lon] = row[:, lanes]


def tapped(cg, at, h, taps, offset):
    lon = cg.shape[2] // 2
    total = taps[0] * cg[at, h, pl.ds(offset, lon)] + taps[2] * cg[at, h, pl.ds(lon - offset, lon)]
    total += taps[1] * cg[at, h, 0:lon]
    return total + taps[3] * cg[at + 1, h, 0:lon] + taps[4] * cg[at - 1, h, 0:lon]


def inner_kernel(layer, layers, place, *refs):
    pl.when(on_home())(functools.partial(inner_body, layer, layers, place, *refs))


def inner_body(layer, layers, place, *refs):
    first, last = layer == layers - 1, layer == 0
    offset_ref, mains, refs = refs[0], refs[1:5], refs[5:]
    carried, w_in, w_out, taps, refs = refs[0], refs[1], refs[2], refs[3], refs[4:]
    outs, refs = (refs[:4], refs[4:]) if last else (refs[:1], refs[1:])
    cg_edges, refs = refs[0], refs[1:]
    if first:
        handed_edges, cg, handed = refs
    else:
        (cg,) = refs
    lon, chans = cg_edges.shape[1:]
    cells, rows = lon // 4, cg.shape[0]
    skipped = layers - 1 - layer
    convs, cots = slice(place * chans, (place + 1) * chans), slice(2 * chans, mains[0].shape[2])
    offset = offset_ref[layer]

    def rows_of(r0, r1, lanes):
        found = [in_order([m[skipped + r, :, lanes] for m in mains]) for r in range(r0, r1)]
        return jnp.concatenate(sum(found, []), axis=0)

    def taps_of(r):
        for h, lanes in halves_of(chans):
            total = tapped(cg, r, h, [taps[layer, k : k + 1, lanes] for k in range(5)], offset)
            total += (handed[r, :, lanes].astype(jnp.float32) if first else carried[r, :, lanes])
            if last:
                low = total.astype(jnp.bfloat16)
                quarters = in_order([low[p * cells : (p + 1) * cells] for p in range(4)])
                for p in range(4):
                    outs[p][r - 1, :, lanes] = quarters[p]
            else:
                outs[0][r - 1, :, lanes] = total

    edge_rows = (0, 1, rows - 2, rows - 1)
    done = 1
    for r0, r1 in row_chunks(0, rows):
        if first:
            cot_low = nt(rows_of(r0, r1, cots), carried[...]).astype(jnp.bfloat16)
        else:
            cot_low = carried[r0:r1].reshape((r1 - r0) * lon, chans).astype(jnp.bfloat16)
        conv_grad = conv_gradient(rows_of(r0, r1, convs), cot_low, w_in[layer], w_out[layer])
        conv_grad = conv_grad.reshape(r1 - r0, lon, chans)
        while done < r0 - 1:
            taps_of(done)
            done += 1
        if first:
            handed[r0:r1] = cot_low.reshape(r1 - r0, lon, chans)
        for r in range(r0, r1):
            keep_row(cg, r, conv_grad[r - r0])
            if r in edge_rows:
                cg_edges[edge_rows.index(r)] = conv_grad[r - r0]
    while done < rows - 1:
        taps_of(done)
        done += 1
    if first:
        handed_edges[0] = handed[0].astype(jnp.float32)
        handed_edges[1] = handed[rows - 1].astype(jnp.float32)


def run_inner(layer, layers, place, offsets, mains, carried, w_in, w_out, taps):
    first, last = layer == layers - 1, layer == 0
    rows, cells = mains[0].shape[:2]
    chans = w_in.shape[1]
    lon = 4 * cells
    rows -= 2 * (layers - 1 - layer)
    smem = pl.BlockSpec(memory_space=pltpu.SMEM)
    vmem = pl.BlockSpec(memory_space=pltpu.VMEM)
    args = [offsets, *mains, carried, w_in, w_out, taps]
    if last:
        out = [jax.ShapeDtypeStruct((rows - 2, cells, chans), jnp.bfloat16)] * 4
    else:
        out = [jax.ShapeDtypeStruct((rows - 2, lon, chans), jnp.float32)]
    out.append(jax.ShapeDtypeStruct((4, lon, chans), jnp.float32))
    scratch = [pltpu.VMEM((rows, chans // 128, 2 * lon, 128), jnp.float32)]
    if first:
        out.append(jax.ShapeDtypeStruct((2, lon, chans), jnp.float32))
        scratch.append(pltpu.VMEM((rows, lon, chans), jnp.bfloat16))
    work = rows * lon
    return pl.pallas_call(
        functools.partial(inner_kernel, layer, layers, place),
        out_shape=out,
        in_specs=[smem] + [vmem] * (len(args) - 1),
        out_specs=[vmem] * len(out),
        scratch_shapes=scratch,
        compiler_params=pltpu.CompilerParams(vmem_limit_bytes=24 * 2**20),
        cost_estimate=pl.CostEstimate(
            flops=6 * work * chans * w_in.shape[2],
            bytes_accessed=work * chans * 10,
            transcendentals=2 * work * w_in.shape[2],
        ),
        name=f"inner_{layer}",
    )(*args)


def outer_kernel(layers, *refs):
    pl.when(on_home())(functools.partial(outer_body, layers, *refs))


def outer_body(layers, *refs):
    offset_ref, refs = refs[0], refs[1:]
    halos, mains, refs = refs[:4], (refs[4:8], refs[8:12]), refs[12:]
    inner, refs = refs[:4], refs[4:]
    handed_edges, gradients, refs = refs[0], refs[1:layers], refs[layers:]
    cg_edges, refs = refs[:layers], refs[layers:]
    dec_weight, w_in, w_out, taps, refs = refs[0], refs[1], refs[2], refs[3], refs[4:]
    outs, (cg, grad) = refs[:4], refs[4:]
    rows, cells = mains[0][0].shape[:2]
    lon, chans = cg_edges[0].shape[1:]
    v = dec_weight.shape[1]
    half_halo = halos[0].shape[0] // 2
    lat = lax.axis_index("lat")
    has_above = jnp.where(lat > 0, 1.0, 0.0).astype(jnp.float32)
    has_below = jnp.where(lat < lax.axis_size("lat") - 1, 1.0, 0.0).astype(jnp.float32)

    def conv_row(layer, r):
        if 0 <= r < rows:
            place = (layers - 1 - layer) % 2
            group = mains[(layers - 1 - layer) // 2]
            return in_order([m[r, :, place * chans : (place + 1) * chans] for m in group])
        at = edge_start(layer) + (r + layer + 1 if r < 0 else half_halo + r - rows)
        return in_order([h[at] for h in halos])

    def cot_row(r):
        k = r + layers if r < 0 else r - rows
        at = edge_start(layers) + k // 2 + (0 if r < 0 else half_halo)
        return in_order([h[at, :, k % 2 * v : (k % 2 + 1) * v] for h in halos])

    for p in range(4):
        outs[p][layers : rows - layers] = inner[p][...]
    for layer in reversed(range(layers)):
        shift = layers - 1 - layer
        here = [*range(-layers + shift, shift), *range(rows - shift, rows - shift + layers)]
        if layer == layers - 1:
            cot = jnp.concatenate(sum([cot_row(r) for r in here], []), axis=0)
            cot_low = nt(cot, dec_weight[...]).astype(jnp.bfloat16)
            grad[...] = cot_low.astype(jnp.float32).reshape(grad.shape)
            near = [handed_edges[0], handed_edges[1]]
        else:
            cot_low = grad[...].reshape(len(here) * lon, chans).astype(jnp.bfloat16)
            before = gradients[layers - 2 - layer]
            near = [before[0], before[before.shape[0] - 1]]
        conv_out = jnp.concatenate(sum([conv_row(layer, r) for r in here], []), axis=0)
        conv_grad = conv_gradient(conv_out, cot_low, w_in[layer], w_out[layer])
        conv_grad = conv_grad.reshape(len(here), lon, chans)
        edge = cg_edges[layers - 1 - layer]
        for k, r in enumerate(here):
            row = conv_grad[k]
            if r < 0:
                row = row * has_above
            if r >= rows:
                row = row * has_below
            keep_row(cg, k if k < layers else k + 4, row)
        for k in range(4):
            keep_row(cg, layers + k, edge[k])
        old = [grad[k] for k in range(2 * layers)]
        old = [*old[1:layers], near[0], near[1], *old[layers:-1]]
        places = [*range(1, layers + 1), *range(layers + 3, 2 * layers + 3)]
        for k, at in enumerate(places):
            for h, lanes in halves_of(chans):
                tap = [taps[layer, n : n + 1, lanes] for n in range(5)]
                total = old[k][:, lanes] + tapped(cg, at, h, tap, offset_ref[layer])
                if layer:
                    grad[k, :, lanes] = total
                else:
                    low = total.astype(jnp.bfloat16)
                    quarters = in_order([low[p * cells : (p + 1) * cells] for p in range(4)])
                    r = k if k < layers else rows - 2 * layers + k
                    for p in range(4):
                        outs[p][r, :, lanes] = quarters[p]


def run_outer(layers, offsets, halos, mains, inner, handed_edges, gradients, cg_edges, weights):
    rows, cells = mains[0][0].shape[:2]
    lon, chans = cg_edges[0].shape[1:]
    smem = pl.BlockSpec(memory_space=pltpu.SMEM)
    vmem = pl.BlockSpec(memory_space=pltpu.VMEM)
    args = [offsets, *halos, *mains[0], *mains[1], *inner, handed_edges, *gradients, *cg_edges]
    args += weights
    work = 2 * layers * layers * lon
    return pl.pallas_call(
        functools.partial(outer_kernel, layers),
        out_shape=[jax.ShapeDtypeStruct((rows, cells, chans), jnp.bfloat16)] * 4,
        in_specs=[smem] + [vmem] * (len(args) - 1),
        out_specs=[vmem] * 4,
        scratch_shapes=[
            pltpu.VMEM((2 * layers + 4, chans // 128, 2 * lon, 128), jnp.float32),
            pltpu.VMEM((2 * layers, lon, chans), jnp.float32),
        ],
        compiler_params=pltpu.CompilerParams(vmem_limit_bytes=24 * 2**20),
        cost_estimate=pl.CostEstimate(
            flops=6 * work * chans * weights[1].shape[2],
            bytes_accessed=work * chans * 10,
            transcendentals=2 * work * weights[1].shape[2],
        ),
        name="outer",
    )(*args)


def by_circles(dec_cot, saved_conv, dec_weight, w_in, w_out, conv_taps, dilation):
    layers = w_in.shape[0]

    def home(c):
        return c + 1

    def away(c, k):
        return (home(c) + (k if c == 0 else -k)) % 4

    order = (2, 1, 3)

    def gather(value):
        found = {0: value}
        for k in order:
            found[k] = routed(
                value, lambda c, z, j: (c, home(c), j) if z == away(c, k) else None
            )
        return [found[k] for k in range(4)]

    def neighbours(c, z, j):
        if z == away(c, 1):
            return c, home(c), j
        if z == away(c, 2):
            return 1 - c, home(c), j

    def across(c, z, j):
        return (1 - c, z, j) if z == home(1 - c) else None

    cot = partner(dec_cot[0], "segment").transpose(1, 0, 2)
    conv = saved_conv[0].transpose(0, 2, 1, 3)
    groups = ((3, 2), (1, 0))
    early, late, top, bottom = cut_edges(groups, conv, cot)
    first = gather(early)
    second = gather(late)
    below = routed(top, lambda c, z, j: (c, z, j - 1))
    above = routed(bottom, lambda c, z, j: (c, z, j + 1))

    carried, gradients, cg_edges = dec_weight, [], []
    for layer in reversed(range(layers)):
        mains = first if layer > 1 else second
        found = run_inner(
            layer, layers, (layers - 1 - layer) % 2, dilation, mains, carried, w_in, w_out, conv_taps
        )
        if layer == layers - 1:
            carried, cg_edge, handed_edges = found
        elif layer:
            carried, cg_edge = found
        else:
            *inner, cg_edge = found
        cg_edges.append(cg_edge)
        if layer:
            gradients.append(carried)
        if layer == layers - 1:
            edges = jnp.concatenate([above, below], axis=0)
            edges, carried = lax.optimization_barrier((edges, carried))
            one = routed(edges, neighbours)
            three = routed(edges, lambda c, z, j: (c, home(c), j) if z == away(c, 3) else None)
        if layer == 1:
            one, carried = lax.optimization_barrier((one, carried))
            halos = [edges, one, routed(one, across), three]
    weights = [dec_weight, w_in, w_out, conv_taps]
    found = run_outer(
        layers, dilation, halos, (first, second), inner, handed_edges, gradients, cg_edges, weights
    )

    result = jnp.where(on_home(), found[0], 0)
    for k in order:
        result = result + routed(
            found[k], lambda c, z, j: (c, away(c, k), j) if z == home(c) else None
        )
    return result.transpose(1, 0, 2)[None]


def solution(mesh):
    in_specs = (
        P("segment", "lon", "lat", None),
        P("segment", None, "lon", "lat", None),
        P(),
        P(),
        P(),
        P(),
        P(),
    )
    out_specs = P("segment", "lon", "lat", None)
    gathers = mesh.shape["lon"] == 4 and mesh.shape["segment"] == 2
    return jax.shard_map(
        by_circles if gathers else by_exchange,
        mesh=mesh,
        in_specs=in_specs,
        out_specs=out_specs,
        check_vma=False,
    )
```

```python
import functools

import jax
import jax.numpy as jnp
from jax import lax
from jax.experimental import pallas as pl
from jax.experimental.pallas import tpu as pltpu
from jax.sharding import PartitionSpec as P

AXES = ("segment", "lon", "lat")


def with_halo(cells, sides, width):
    for axis, dim in sides:
        count = lax.axis_size(axis)
        ends = count - 1
        head = lax.slice_in_dim(cells, 0, width, axis=dim)
        tail = lax.slice_in_dim(cells, cells.shape[dim] - width, cells.shape[dim], axis=dim)
        cells = jnp.concatenate(
            [
                lax.ppermute(tail, axis, [(i, (i + 1) % count) for i in range(ends)]),
                cells,
                lax.ppermute(head, axis, [((i + 1) % count, i) for i in range(ends)]),
            ],
            axis=dim,
        )
    return cells


def from_behind(value, axis, steps):
    count = lax.axis_size(axis)
    pairs = [(source, (source + steps) % count) for source in range(count)]
    return lax.ppermute(value, axis, pairs)


def partner(block, axis):
    count = lax.axis_size(axis)
    return lax.ppermute(block, axis, [(i, i ^ 1) for i in range(count) if i ^ 1 < count])


def gelu_slope(hidden):
    normal_cdf = 0.5 * (1.0 + lax.erf(hidden * 0.7071067811865476))
    density = jnp.exp(-0.5 * hidden * hidden) * 0.3989422804014327
    return normal_cdf + hidden * density


def tap_adjoint(conv_grad, taps_now, offset):
    lon_cells = conv_grad.shape[0]
    lat_padded = with_halo(conv_grad, (("lat", 1),), 1)
    meridional = taps_now[3] * lat_padded[:, 2:] + taps_now[4] * lat_padded[:, :-2]
    centre = taps_now[1] * conv_grad
    rim_width = 3 * lon_cells
    pieces = []
    for distance in (3, 2, 1, 0, -1, -2, -3):
        pieces.append(conv_grad if distance == 0 else from_behind(conv_grad, "lon", distance))
    padded = jnp.concatenate(pieces, axis=0)
    ahead_cells = lax.dynamic_slice_in_dim(padded, rim_width + offset, lon_cells, 0)
    behind = lax.dynamic_slice_in_dim(padded, rim_width - offset, lon_cells, 0)
    zonal_sum = taps_now[0] * ahead_cells + taps_now[2] * behind
    zonal_sum = lax.optimization_barrier(zonal_sum.astype(jnp.bfloat16)).astype(jnp.float32)
    return zonal_sum + centre + meridional


def by_exchange(dec_cot, saved_conv, dec_weight, w_in, w_out, conv_taps, dilation):
    lon_cells, lat_rows, chans = saved_conv.shape[2:]
    own_cot = dec_cot[0].reshape(-1, dec_cot.shape[3])
    projected = jnp.einsum(
        "nv,cv->nc", own_cot, dec_weight, preferred_element_type=jnp.float32
    ).astype(jnp.bfloat16)
    gradient = lax.optimization_barrier(partner(projected, "segment")).astype(jnp.float32)
    for layer in reversed(range(w_in.shape[0])):
        conv_out = saved_conv[0, layer].reshape(-1, chans)
        hidden = jnp.dot(conv_out, w_in[layer], preferred_element_type=jnp.float32)
        act_grad = jnp.einsum(
            "nc,hc->nh",
            gradient.astype(jnp.bfloat16),
            w_out[layer],
            preferred_element_type=jnp.float32,
        )
        pre_grad = (act_grad * gelu_slope(hidden)).astype(jnp.bfloat16)
        conv_grad = jnp.einsum(
            "nh,ch->nc", pre_grad, w_in[layer], preferred_element_type=jnp.float32
        ).astype(jnp.bfloat16)
        tapped = tap_adjoint(
            conv_grad.reshape(lon_cells, lat_rows, chans), conv_taps[layer], dilation[layer]
        )
        gradient = gradient + tapped.reshape(-1, chans)
    return gradient.reshape(1, lon_cells, lat_rows, chans).astype(jnp.bfloat16)


def routed(value, hop):
    cores, cols, rows = (lax.axis_size(a) for a in AXES)
    pairs = []
    for c in range(cores):
        for z in range(cols):
            for j in range(rows):
                to = hop(c, z, j)
                if to is not None and 0 <= to[2] < rows:
                    pairs.append(((c * cols + z) * rows + j, (to[0] * cols + to[1]) * rows + to[2]))
    return lax.ppermute(value, AXES, pairs)


def row_chunks(low, high):
    count = max(1, round((high - low) / 7))
    edges = [low + (high - low) * i // count for i in range(count + 1)]
    return list(zip(edges[:-1], edges[1:]))


def on_home():
    return lax.axis_index("lon") == lax.axis_index("segment") + 1


GROUPS = ((3, 2), (1, 0))
MESSAGE = {layer: (g, k) for g, group in enumerate(GROUPS) for k, layer in enumerate(group)}


def edge_start(layer):
    return layer * (layer + 1) // 2


def edges_kernel(layers, groups, conv, cot, *outs):
    *messages, top_ref, bottom_ref = outs
    cot = jnp.swapaxes(cot[...].astype(jnp.float32), 0, 1).astype(conv.dtype)
    rows, chans, v = cot.shape[0], conv.shape[3], cot.shape[2]
    for message, group in zip(messages, groups):
        for k, layer in enumerate(group):
            message[:, :, k * chans : (k + 1) * chans] = conv[layer]
    messages[0][:, :, len(groups[0]) * chans :] = cot
    for layer in range(layers):
        here = slice(edge_start(layer), edge_start(layer + 1))
        top_ref[here] = conv[layer, : layer + 1]
        bottom_ref[here] = conv[layer, rows - layer - 1 :]
    for k in range(layers):
        at, lanes = edge_start(layers) + k // 2, slice(k % 2 * v, (k % 2 + 1) * v)
        top_ref[at, :, lanes] = cot[k]
        bottom_ref[at, :, lanes] = cot[rows - layers + k]


def cut_edges(groups, conv, cot):
    layers, rows, cells, chans = conv.shape
    edge = jax.ShapeDtypeStruct((edge_start(layers) + layers // 2, cells, chans), conv.dtype)
    widths = [len(group) * chans for group in groups]
    widths[0] += cot.shape[2]
    messages = [jax.ShapeDtypeStruct((rows, cells, width), conv.dtype) for width in widths]
    vmem = pl.BlockSpec(memory_space=pltpu.VMEM)
    return pl.pallas_call(
        functools.partial(edges_kernel, layers, groups),
        out_shape=messages + [edge, edge],
        in_specs=[vmem, vmem],
        out_specs=[vmem] * (len(groups) + 2),
        compiler_params=pltpu.CompilerParams(vmem_limit_bytes=16 * 2**20),
        name="edges",
    )(conv, cot)


def nt(a, b):
    return lax.dot_general(a, b, (((1,), (1,)), ((), ())), preferred_element_type=jnp.float32)


def halves_of(chans):
    return [(h, slice(h * 128, (h + 1) * 128)) for h in range(chans // 128)]


def in_order(pieces):
    upward = lax.axis_index("segment") == 0
    own, one, two, three = pieces
    return [own, jnp.where(upward, one, three), two, jnp.where(upward, three, one)]


def conv_gradient(conv_out, cot_low, w_in, w_out):
    hidden = jnp.dot(conv_out, w_in, preferred_element_type=jnp.float32)
    pre = (nt(cot_low, w_out) * gelu_slope(hidden)).astype(jnp.bfloat16)
    return nt(pre, w_in)


def keep_row(cg, at, row):
    lon = row.shape[0]
    for h, lanes in halves_of(row.shape[1]):
        cg[at, h, 0:lon] = row[:, lanes]
        cg[at, h, lon : 2 * lon] = row[:, lanes]


def tapped(cg, at, h, taps, offset):
    lon = cg.shape[2] // 2
    total = taps[0] * cg[at, h, pl.ds(offset, lon)] + taps[2] * cg[at, h, pl.ds(lon - offset, lon)]
    total += taps[1] * cg[at, h, 0:lon]
    return total + taps[3] * cg[at + 1, h, 0:lon] + taps[4] * cg[at - 1, h, 0:lon]


def inner_kernel(layer, layers, place, *refs):
    pl.when(on_home())(functools.partial(inner_body, layer, layers, place, *refs))


def inner_body(layer, layers, place, *refs):
    first, last = layer == layers - 1, layer == 0
    offset_ref, mains, refs = refs[0], refs[1:5], refs[5:]
    carried, w_in, w_out, taps, refs = refs[0], refs[1], refs[2], refs[3], refs[4:]
    outs, refs = (refs[:4], refs[4:]) if last else (refs[:1], refs[1:])
    cg_edges, refs = refs[0], refs[1:]
    if first:
        handed_edges, cg, handed = refs
    else:
        (cg,) = refs
    lon, chans = cg_edges.shape[1:]
    cells, rows = lon // 4, cg.shape[0]
    skipped = layers - 1 - layer
    convs, cots = slice(place * chans, (place + 1) * chans), slice(len(GROUPS[0]) * chans, mains[0].shape[2])
    offset = offset_ref[layer]

    def rows_of(r0, r1, lanes):
        found = [in_order([m[skipped + r, :, lanes] for m in mains]) for r in range(r0, r1)]
        return jnp.concatenate(sum(found, []), axis=0)

    def taps_of(r):
        for h, lanes in halves_of(chans):
            total = tapped(cg, r, h, [taps[layer, k : k + 1, lanes] for k in range(5)], offset)
            total += (handed[r, :, lanes].astype(jnp.float32) if first else carried[r, :, lanes])
            if last:
                low = total.astype(jnp.bfloat16)
                quarters = in_order([low[p * cells : (p + 1) * cells] for p in range(4)])
                for p in range(4):
                    outs[p][r - 1, :, lanes] = quarters[p]
            else:
                outs[0][r - 1, :, lanes] = total

    edge_rows = (0, 1, rows - 2, rows - 1)
    for r0, r1 in row_chunks(0, rows):
        if first:
            cot_low = nt(rows_of(r0, r1, cots), carried[...]).astype(jnp.bfloat16)
        else:
            cot_low = carried[r0:r1].reshape((r1 - r0) * lon, chans).astype(jnp.bfloat16)
        conv_grad = conv_gradient(rows_of(r0, r1, convs), cot_low, w_in[layer], w_out[layer])
        conv_grad = conv_grad.reshape(r1 - r0, lon, chans)
        if first:
            handed[r0:r1] = cot_low.reshape(r1 - r0, lon, chans)
        for r in range(r0, r1):
            keep_row(cg, r, conv_grad[r - r0])
            if r in edge_rows:
                cg_edges[edge_rows.index(r)] = conv_grad[r - r0]
    half = (rows - 2) // 2

    def taps_of_half(k, carry):
        for r in range(half):
            taps_of(1 + k * half + r)
        return carry

    lax.fori_loop(0, 2, taps_of_half, 0)
    if first:
        handed_edges[0] = handed[0].astype(jnp.float32)
        handed_edges[1] = handed[rows - 1].astype(jnp.float32)


def run_inner(layer, layers, place, offsets, mains, carried, w_in, w_out, taps):
    first, last = layer == layers - 1, layer == 0
    rows, cells = mains[0].shape[:2]
    chans = w_in.shape[1]
    lon = 4 * cells
    rows -= 2 * (layers - 1 - layer)
    smem = pl.BlockSpec(memory_space=pltpu.SMEM)
    vmem = pl.BlockSpec(memory_space=pltpu.VMEM)
    args = [offsets, *mains, carried, w_in, w_out, taps]
    if last:
        out = [jax.ShapeDtypeStruct((rows - 2, cells, chans), jnp.bfloat16)] * 4
    else:
        out = [jax.ShapeDtypeStruct((rows - 2, lon, chans), jnp.float32)]
    out.append(jax.ShapeDtypeStruct((4, lon, chans), jnp.float32))
    scratch = [pltpu.VMEM((rows, chans // 128, 2 * lon, 128), jnp.float32)]
    if first:
        out.append(jax.ShapeDtypeStruct((2, lon, chans), jnp.float32))
        scratch.append(pltpu.VMEM((rows, lon, chans), jnp.bfloat16))
    work = rows * lon
    return pl.pallas_call(
        functools.partial(inner_kernel, layer, layers, place),
        out_shape=out,
        in_specs=[smem] + [vmem] * (len(args) - 1),
        out_specs=[vmem] * len(out),
        scratch_shapes=scratch,
        compiler_params=pltpu.CompilerParams(vmem_limit_bytes=24 * 2**20),
        cost_estimate=pl.CostEstimate(
            flops=6 * work * chans * w_in.shape[2],
            bytes_accessed=work * chans * 10,
            transcendentals=2 * work * w_in.shape[2],
        ),
        name=f"inner_{layer}",
    )(*args)


def outer_kernel(layers, *refs):
    pl.when(on_home())(functools.partial(outer_body, layers, *refs))


def outer_body(layers, *refs):
    offset_ref, refs = refs[0], refs[1:]
    halos, mains, refs = refs[:4], (refs[4:8], refs[8:12]), refs[12:]
    inner, refs = refs[:4], refs[4:]
    handed_edges, gradients, refs = refs[0], refs[1:layers], refs[layers:]
    cg_edges, refs = refs[:layers], refs[layers:]
    dec_weight, w_in, w_out, taps, refs = refs[0], refs[1], refs[2], refs[3], refs[4:]
    outs, (cg, grad) = refs[:4], refs[4:]
    rows, cells = mains[0][0].shape[:2]
    lon, chans = cg_edges[0].shape[1:]
    v = dec_weight.shape[1]
    half_halo = halos[0].shape[0] // 2
    lat = lax.axis_index("lat")
    has_above = jnp.where(lat > 0, 1.0, 0.0).astype(jnp.float32)
    has_below = jnp.where(lat < lax.axis_size("lat") - 1, 1.0, 0.0).astype(jnp.float32)

    def conv_row(layer, r):
        if 0 <= r < rows:
            group, place = MESSAGE[layer]
            return in_order([m[r, :, place * chans : (place + 1) * chans] for m in mains[group]])
        at = edge_start(layer) + (r + layer + 1 if r < 0 else half_halo + r - rows)
        return in_order([h[at] for h in halos])

    def cot_row(r):
        k = r + layers if r < 0 else r - rows
        at = edge_start(layers) + k // 2 + (0 if r < 0 else half_halo)
        return in_order([h[at, :, k % 2 * v : (k % 2 + 1) * v] for h in halos])

    for p in range(4):
        outs[p][layers : rows - layers] = inner[p][...]
    for layer in reversed(range(layers)):
        shift = layers - 1 - layer
        here = [*range(-layers + shift, shift), *range(rows - shift, rows - shift + layers)]
        if layer == layers - 1:
            cot = jnp.concatenate(sum([cot_row(r) for r in here], []), axis=0)
            cot_low = nt(cot, dec_weight[...]).astype(jnp.bfloat16)
            grad[...] = cot_low.astype(jnp.float32).reshape(grad.shape)
            near = [handed_edges[0], handed_edges[1]]
        else:
            cot_low = grad[...].reshape(len(here) * lon, chans).astype(jnp.bfloat16)
            before = gradients[layers - 2 - layer]
            near = [before[0], before[before.shape[0] - 1]]
        conv_out = jnp.concatenate(sum([conv_row(layer, r) for r in here], []), axis=0)
        conv_grad = conv_gradient(conv_out, cot_low, w_in[layer], w_out[layer])
        conv_grad = conv_grad.reshape(len(here), lon, chans)
        edge = cg_edges[layers - 1 - layer]
        for k, r in enumerate(here):
            row = conv_grad[k]
            if r < 0:
                row = row * has_above
            if r >= rows:
                row = row * has_below
            keep_row(cg, k if k < layers else k + 4, row)
        for k in range(4):
            keep_row(cg, layers + k, edge[k])
        old = [grad[k] for k in range(2 * layers)]
        old = [*old[1:layers], near[0], near[1], *old[layers:-1]]
        places = [*range(1, layers + 1), *range(layers + 3, 2 * layers + 3)]
        for k, at in enumerate(places):
            for h, lanes in halves_of(chans):
                tap = [taps[layer, n : n + 1, lanes] for n in range(5)]
                total = old[k][:, lanes] + tapped(cg, at, h, tap, offset_ref[layer])
                if layer:
                    grad[k, :, lanes] = total
                else:
                    low = total.astype(jnp.bfloat16)
                    quarters = in_order([low[p * cells : (p + 1) * cells] for p in range(4)])
                    r = k if k < layers else rows - 2 * layers + k
                    for p in range(4):
                        outs[p][r, :, lanes] = quarters[p]


def run_outer(layers, offsets, halos, mains, inner, handed_edges, gradients, cg_edges, weights):
    rows, cells = mains[0][0].shape[:2]
    lon, chans = cg_edges[0].shape[1:]
    smem = pl.BlockSpec(memory_space=pltpu.SMEM)
    vmem = pl.BlockSpec(memory_space=pltpu.VMEM)
    args = [offsets, *halos, *mains[0], *mains[1], *inner, handed_edges, *gradients, *cg_edges]
    args += weights
    work = 2 * layers * layers * lon
    return pl.pallas_call(
        functools.partial(outer_kernel, layers),
        out_shape=[jax.ShapeDtypeStruct((rows, cells, chans), jnp.bfloat16)] * 4,
        in_specs=[smem] + [vmem] * (len(args) - 1),
        out_specs=[vmem] * 4,
        scratch_shapes=[
            pltpu.VMEM((2 * layers + 4, chans // 128, 2 * lon, 128), jnp.float32),
            pltpu.VMEM((2 * layers, lon, chans), jnp.float32),
        ],
        compiler_params=pltpu.CompilerParams(vmem_limit_bytes=24 * 2**20),
        cost_estimate=pl.CostEstimate(
            flops=6 * work * chans * weights[1].shape[2],
            bytes_accessed=work * chans * 10,
            transcendentals=2 * work * weights[1].shape[2],
        ),
        name="outer",
    )(*args)


def by_circles(dec_cot, saved_conv, dec_weight, w_in, w_out, conv_taps, dilation):
    layers = w_in.shape[0]

    def home(c):
        return c + 1

    def away(c, k):
        return (home(c) + (k if c == 0 else -k)) % 4

    order = (3, 1, 2)

    def gather(value):
        found = {0: value}
        for k in order:
            found[k] = routed(
                value, lambda c, z, j: (c, home(c), j) if z == away(c, k) else None
            )
        return [found[k] for k in range(4)]

    def neighbours(c, z, j):
        if z == away(c, 1):
            return c, home(c), j
        if z == away(c, 2):
            return 1 - c, home(c), j

    def across(c, z, j):
        return (1 - c, z, j) if z == home(1 - c) else None

    cot = partner(dec_cot[0], "segment")
    conv = saved_conv[0].transpose(0, 2, 1, 3)
    early, late, top, bottom = cut_edges(GROUPS, conv, cot)
    first = gather(early)
    below = routed(top, lambda c, z, j: (c, z, j - 1))
    above = routed(bottom, lambda c, z, j: (c, z, j + 1))

    two = routed(late, lambda c, z, j: (c, home(c), j) if z == away(c, 2) else None)
    sides, above, below = lax.optimization_barrier((late, above, below))
    one = routed(sides, lambda c, z, j: (c, home(c), j) if z == away(c, 1) else None)
    three = routed(sides, lambda c, z, j: (c, home(c), j) if z == away(c, 3) else None)
    second = [late, one, two, three]

    carried, gradients, cg_edges = dec_weight, [], []
    for layer in reversed(range(layers)):
        group, place = MESSAGE[layer]
        mains = (first, second)[group]
        found = run_inner(
            layer, layers, place, dilation, mains, carried, w_in, w_out, conv_taps
        )
        if layer == layers - 1:
            carried, cg_edge, handed_edges = found
        elif layer:
            carried, cg_edge = found
        else:
            *inner, cg_edge = found
        cg_edges.append(cg_edge)
        if layer:
            gradients.append(carried)
        if layer == layers - 1:
            edges = jnp.concatenate([above, below], axis=0)
            edges, carried = lax.optimization_barrier((edges, carried))
            one = routed(edges, neighbours)
            three = routed(edges, lambda c, z, j: (c, home(c), j) if z == away(c, 3) else None)
        if layer == 1:
            one, carried = lax.optimization_barrier((one, carried))
            halos = [edges, one, routed(one, across), three]
    weights = [dec_weight, w_in, w_out, conv_taps]
    found = run_outer(
        layers, dilation, halos, (first, second), inner, handed_edges, gradients, cg_edges, weights
    )

    result = jnp.where(on_home(), found[0], 0)
    for k in order:
        result = result + routed(
            found[k], lambda c, z, j: (c, away(c, k), j) if z == home(c) else None
        )
    return result.transpose(1, 0, 2)[None]


def solution(mesh):
    in_specs = (
        P("segment", "lon", "lat", None),
        P("segment", None, "lon", "lat", None),
        P(),
        P(),
        P(),
        P(),
        P(),
    )
    out_specs = P("segment", "lon", "lat", None)
    gathers = mesh.shape["lon"] == 4 and mesh.shape["segment"] == 2
    return jax.shard_map(
        by_circles if gathers else by_exchange,
        mesh=mesh,
        in_specs=in_specs,
        out_specs=out_specs,
        check_vma=False,
    )
```

```python
import functools

import jax
import jax.numpy as jnp
from jax import lax
from jax.experimental import pallas as pl
from jax.experimental.pallas import tpu as pltpu
from jax.sharding import PartitionSpec as P

AXES = ("segment", "lon", "lat")


def with_halo(cells, sides, width):
    for axis, dim in sides:
        count = lax.axis_size(axis)
        ends = count - 1
        head = lax.slice_in_dim(cells, 0, width, axis=dim)
        tail = lax.slice_in_dim(cells, cells.shape[dim] - width, cells.shape[dim], axis=dim)
        cells = jnp.concatenate(
            [
                lax.ppermute(tail, axis, [(i, (i + 1) % count) for i in range(ends)]),
                cells,
                lax.ppermute(head, axis, [((i + 1) % count, i) for i in range(ends)]),
            ],
            axis=dim,
        )
    return cells


def from_behind(value, axis, steps):
    count = lax.axis_size(axis)
    pairs = [(source, (source + steps) % count) for source in range(count)]
    return lax.ppermute(value, axis, pairs)


def partner(block, axis):
    count = lax.axis_size(axis)
    return lax.ppermute(block, axis, [(i, i ^ 1) for i in range(count) if i ^ 1 < count])


def gelu_slope(hidden):
    normal_cdf = 0.5 * (1.0 + lax.erf(hidden * 0.7071067811865476))
    density = jnp.exp(-0.5 * hidden * hidden) * 0.3989422804014327
    return normal_cdf + hidden * density


def tap_adjoint(conv_grad, taps_now, offset):
    lon_cells = conv_grad.shape[0]
    lat_padded = with_halo(conv_grad, (("lat", 1),), 1)
    meridional = taps_now[3] * lat_padded[:, 2:] + taps_now[4] * lat_padded[:, :-2]
    centre = taps_now[1] * conv_grad
    rim_width = 3 * lon_cells
    pieces = []
    for distance in (3, 2, 1, 0, -1, -2, -3):
        pieces.append(conv_grad if distance == 0 else from_behind(conv_grad, "lon", distance))
    padded = jnp.concatenate(pieces, axis=0)
    ahead_cells = lax.dynamic_slice_in_dim(padded, rim_width + offset, lon_cells, 0)
    behind = lax.dynamic_slice_in_dim(padded, rim_width - offset, lon_cells, 0)
    zonal_sum = taps_now[0] * ahead_cells + taps_now[2] * behind
    zonal_sum = lax.optimization_barrier(zonal_sum.astype(jnp.bfloat16)).astype(jnp.float32)
    return zonal_sum + centre + meridional


def by_exchange(dec_cot, saved_conv, dec_weight, w_in, w_out, conv_taps, dilation):
    lon_cells, lat_rows, chans = saved_conv.shape[2:]
    own_cot = dec_cot[0].reshape(-1, dec_cot.shape[3])
    projected = jnp.einsum(
        "nv,cv->nc", own_cot, dec_weight, preferred_element_type=jnp.float32
    ).astype(jnp.bfloat16)
    gradient = lax.optimization_barrier(partner(projected, "segment")).astype(jnp.float32)
    for layer in reversed(range(w_in.shape[0])):
        conv_out = saved_conv[0, layer].reshape(-1, chans)
        hidden = jnp.dot(conv_out, w_in[layer], preferred_element_type=jnp.float32)
        act_grad = jnp.einsum(
            "nc,hc->nh",
            gradient.astype(jnp.bfloat16),
            w_out[layer],
            preferred_element_type=jnp.float32,
        )
        pre_grad = (act_grad * gelu_slope(hidden)).astype(jnp.bfloat16)
        conv_grad = jnp.einsum(
            "nh,ch->nc", pre_grad, w_in[layer], preferred_element_type=jnp.float32
        ).astype(jnp.bfloat16)
        tapped = tap_adjoint(
            conv_grad.reshape(lon_cells, lat_rows, chans), conv_taps[layer], dilation[layer]
        )
        gradient = gradient + tapped.reshape(-1, chans)
    return gradient.reshape(1, lon_cells, lat_rows, chans).astype(jnp.bfloat16)


def routed(value, hop):
    cores, cols, rows = (lax.axis_size(a) for a in AXES)
    pairs = []
    for c in range(cores):
        for z in range(cols):
            for j in range(rows):
                to = hop(c, z, j)
                if to is not None and 0 <= to[2] < rows:
                    pairs.append(((c * cols + z) * rows + j, (to[0] * cols + to[1]) * rows + to[2]))
    return lax.ppermute(value, AXES, pairs)


def row_chunks(low, high):
    count = max(1, round((high - low) / 7))
    edges = [low + (high - low) * i // count for i in range(count + 1)]
    return list(zip(edges[:-1], edges[1:]))


def on_home():
    return lax.axis_index("lon") == lax.axis_index("segment") + 1


GROUPS = ((3, 2), (1, 0))
MESSAGE = {layer: (g, k) for g, group in enumerate(GROUPS) for k, layer in enumerate(group)}


def edge_start(layer):
    return layer * (layer + 1) // 2


def edges_kernel(layers, groups, conv, cot, *outs):
    *messages, top_ref, bottom_ref = outs
    cot = jnp.swapaxes(cot[...].astype(jnp.float32), 0, 1).astype(conv.dtype)
    rows, chans, v = cot.shape[0], conv.shape[3], cot.shape[2]
    for message, group in zip(messages, groups):
        for k, layer in enumerate(group):
            message[:, :, k * chans : (k + 1) * chans] = conv[layer]
    messages[0][:, :, len(groups[0]) * chans :] = cot
    for layer in range(layers):
        here = slice(edge_start(layer), edge_start(layer + 1))
        top_ref[here] = conv[layer, : layer + 1]
        bottom_ref[here] = conv[layer, rows - layer - 1 :]
    for k in range(layers):
        at, lanes = edge_start(layers) + k // 2, slice(k % 2 * v, (k % 2 + 1) * v)
        top_ref[at, :, lanes] = cot[k]
        bottom_ref[at, :, lanes] = cot[rows - layers + k]


def cut_edges(groups, conv, cot):
    layers, rows, cells, chans = conv.shape
    edge = jax.ShapeDtypeStruct((edge_start(layers) + layers // 2, cells, chans), conv.dtype)
    widths = [len(group) * chans for group in groups]
    widths[0] += cot.shape[2]
    messages = [jax.ShapeDtypeStruct((rows, cells, width), conv.dtype) for width in widths]
    vmem = pl.BlockSpec(memory_space=pltpu.VMEM)
    return pl.pallas_call(
        functools.partial(edges_kernel, layers, groups),
        out_shape=messages + [edge, edge],
        in_specs=[vmem, vmem],
        out_specs=[vmem] * (len(groups) + 2),
        compiler_params=pltpu.CompilerParams(vmem_limit_bytes=16 * 2**20),
        name="edges",
    )(conv, cot)


def nt(a, b):
    return lax.dot_general(a, b, (((1,), (1,)), ((), ())), preferred_element_type=jnp.float32)


def halves_of(chans):
    return [(h, slice(h * 128, (h + 1) * 128)) for h in range(chans // 128)]


def in_order(pieces):
    upward = lax.axis_index("segment") == 0
    own, one, two, three = pieces
    return [own, jnp.where(upward, one, three), two, jnp.where(upward, three, one)]


def conv_gradient(conv_out, cot_low, w_in, w_out):
    hidden = jnp.dot(conv_out, w_in, preferred_element_type=jnp.float32)
    pre = (nt(cot_low, w_out) * gelu_slope(hidden)).astype(jnp.bfloat16)
    return nt(pre, w_in)


def keep_row(cg, at, row):
    lon = row.shape[0]
    for h, lanes in halves_of(row.shape[1]):
        cg[at, h, 0:lon] = row[:, lanes]
        cg[at, h, lon : 2 * lon] = row[:, lanes]


def tapped(cg, at, h, taps, offset):
    lon = cg.shape[2] // 2
    total = taps[0] * cg[at, h, pl.ds(offset, lon)] + taps[2] * cg[at, h, pl.ds(lon - offset, lon)]
    total += taps[1] * cg[at, h, 0:lon]
    return total + taps[3] * cg[at + 1, h, 0:lon] + taps[4] * cg[at - 1, h, 0:lon]


def inner_kernel(layer, layers, place, *refs):
    pl.when(on_home())(functools.partial(inner_body, layer, layers, place, *refs))


def inner_body(layer, layers, place, *refs):
    first, last = layer == layers - 1, layer == 0
    offset_ref, mains, refs = refs[0], refs[1:5], refs[5:]
    carried, w_in, w_out, taps, refs = refs[0], refs[1], refs[2], refs[3], refs[4:]
    outs, refs = (refs[:4], refs[4:]) if last else (refs[:1], refs[1:])
    cg_edges, refs = refs[0], refs[1:]
    if first:
        handed_edges, cg, handed = refs
    else:
        (cg,) = refs
    lon, chans = cg_edges.shape[1:]
    cells, rows = lon // 4, cg.shape[0]
    skipped = layers - 1 - layer
    convs, cots = slice(place * chans, (place + 1) * chans), slice(len(GROUPS[0]) * chans, mains[0].shape[2])
    offset = offset_ref[layer]

    def rows_of(r0, r1, lanes):
        found = [in_order([m[skipped + r, :, lanes] for m in mains]) for r in range(r0, r1)]
        return jnp.concatenate(sum(found, []), axis=0)

    def taps_of(r):
        for h, lanes in halves_of(chans):
            total = tapped(cg, r, h, [taps[layer, k : k + 1, lanes] for k in range(5)], offset)
            total += (handed[r, :, lanes].astype(jnp.float32) if first else carried[r, :, lanes])
            if last:
                low = total.astype(jnp.bfloat16)
                quarters = in_order([low[p * cells : (p + 1) * cells] for p in range(4)])
                for p in range(4):
                    outs[p][r - 1, :, lanes] = quarters[p]
            else:
                outs[0][r - 1, :, lanes] = total

    edge_rows = (0, 1, rows - 2, rows - 1)
    for r0, r1 in row_chunks(0, rows):
        if first:
            cot_low = nt(rows_of(r0, r1, cots), carried[...]).astype(jnp.bfloat16)
        else:
            cot_low = carried[r0:r1].reshape((r1 - r0) * lon, chans).astype(jnp.bfloat16)
        conv_grad = conv_gradient(rows_of(r0, r1, convs), cot_low, w_in[layer], w_out[layer])
        conv_grad = conv_grad.reshape(r1 - r0, lon, chans)
        if first:
            handed[r0:r1] = cot_low.reshape(r1 - r0, lon, chans)
        for r in range(r0, r1):
            keep_row(cg, r, conv_grad[r - r0])
            if r in edge_rows:
                cg_edges[edge_rows.index(r)] = conv_grad[r - r0]
    half = (rows - 2) // 2

    def taps_of_half(k, carry):
        for r in range(half):
            taps_of(1 + k * half + r)
        return carry

    lax.fori_loop(0, 2, taps_of_half, 0)
    if first:
        handed_edges[0] = handed[0].astype(jnp.float32)
        handed_edges[1] = handed[rows - 1].astype(jnp.float32)


def run_inner(layer, layers, place, offsets, mains, carried, w_in, w_out, taps):
    first, last = layer == layers - 1, layer == 0
    rows, cells = mains[0].shape[:2]
    chans = w_in.shape[1]
    lon = 4 * cells
    rows -= 2 * (layers - 1 - layer)
    smem = pl.BlockSpec(memory_space=pltpu.SMEM)
    vmem = pl.BlockSpec(memory_space=pltpu.VMEM)
    args = [offsets, *mains, carried, w_in, w_out, taps]
    if last:
        out = [jax.ShapeDtypeStruct((rows - 2, cells, chans), jnp.bfloat16)] * 4
    else:
        out = [jax.ShapeDtypeStruct((rows - 2, lon, chans), jnp.float32)]
    out.append(jax.ShapeDtypeStruct((4, lon, chans), jnp.float32))
    scratch = [pltpu.VMEM((rows, chans // 128, 2 * lon, 128), jnp.float32)]
    if first:
        out.append(jax.ShapeDtypeStruct((2, lon, chans), jnp.float32))
        scratch.append(pltpu.VMEM((rows, lon, chans), jnp.bfloat16))
    work = rows * lon
    return pl.pallas_call(
        functools.partial(inner_kernel, layer, layers, place),
        out_shape=out,
        in_specs=[smem] + [vmem] * (len(args) - 1),
        out_specs=[vmem] * len(out),
        scratch_shapes=scratch,
        compiler_params=pltpu.CompilerParams(vmem_limit_bytes=24 * 2**20),
        cost_estimate=pl.CostEstimate(
            flops=6 * work * chans * w_in.shape[2],
            bytes_accessed=work * chans * 10,
            transcendentals=2 * work * w_in.shape[2],
        ),
        name=f"inner_{layer}",
    )(*args)


def outer_kernel(layers, *refs):
    pl.when(on_home())(functools.partial(outer_body, layers, *refs))


def outer_body(layers, *refs):
    offset_ref, refs = refs[0], refs[1:]
    halos, mains, refs = refs[:4], (refs[4:8], refs[8:12]), refs[12:]
    inner, refs = refs[:4], refs[4:]
    handed_edges, gradients, refs = refs[0], refs[1:layers], refs[layers:]
    cg_edges, refs = refs[:layers], refs[layers:]
    dec_weight, w_in, w_out, taps, refs = refs[0], refs[1], refs[2], refs[3], refs[4:]
    outs, cg, grad = refs[:4], refs[4:6], refs[6:8]
    rows, cells = mains[0][0].shape[:2]
    lon, chans = cg_edges[0].shape[1:]
    v = dec_weight.shape[1]
    half_halo = halos[0].shape[0] // 2
    lat = lax.axis_index("lat")
    has_above = jnp.where(lat > 0, 1.0, 0.0).astype(jnp.float32)
    has_below = jnp.where(lat < lax.axis_size("lat") - 1, 1.0, 0.0).astype(jnp.float32)

    def conv_row(layer, r):
        if 0 <= r < rows:
            group, place = MESSAGE[layer]
            return in_order([m[r, :, place * chans : (place + 1) * chans] for m in mains[group]])
        at = edge_start(layer) + (r + layer + 1 if r < 0 else half_halo + r - rows)
        return in_order([h[at] for h in halos])

    def cot_row(r):
        k = r + layers if r < 0 else r - rows
        at = edge_start(layers) + k // 2 + (0 if r < 0 else half_halo)
        return in_order([h[at, :, k % 2 * v : (k % 2 + 1) * v] for h in halos])

    def gradient_rows(layer, side):
        shift = layers - 1 - layer
        here = range(-layers + shift, shift) if side == 0 else range(rows - shift, rows - shift + layers)
        if layer == layers - 1:
            cot = jnp.concatenate(sum([cot_row(r) for r in here], []), axis=0)
            cot_low = nt(cot, dec_weight[...]).astype(jnp.bfloat16)
            grad[side][...] = cot_low.astype(jnp.float32).reshape(grad[side].shape)
        else:
            cot_low = grad[side][...].reshape(layers * lon, chans).astype(jnp.bfloat16)
        conv_out = jnp.concatenate(sum([conv_row(layer, r) for r in here], []), axis=0)
        found = conv_gradient(conv_out, cot_low, w_in[layer], w_out[layer])
        found = found.reshape(layers, lon, chans)
        edge = cg_edges[layers - 1 - layer]
        for k, r in enumerate(here):
            row = found[k]
            if r < 0:
                row = row * has_above
            if r >= rows:
                row = row * has_below
            keep_row(cg[side], k if side == 0 else k + 2, row)
        for k in range(2):
            keep_row(cg[side], layers + k if side == 0 else k, edge[k + 2 * side])

    def gradient_taps(layer, side):
        if layer == layers - 1:
            near = handed_edges[side]
        else:
            before = gradients[layers - 2 - layer]
            near = before[0 if side == 0 else before.shape[0] - 1]
        old = [grad[side][k] for k in range(layers)]
        old = [*old[1:], near] if side == 0 else [near, *old[:-1]]
        for k in range(layers):
            for h, lanes in halves_of(chans):
                tap = [taps[layer, n : n + 1, lanes] for n in range(5)]
                total = old[k][:, lanes] + tapped(cg[side], k + 1, h, tap, offset_ref[layer])
                if layer:
                    grad[side][k, :, lanes] = total
                else:
                    quarters = quarters_of(total.astype(jnp.bfloat16))
                    r = k if side == 0 else rows - layers + k
                    for p in range(4):
                        outs[p][r, :, lanes] = quarters[p]

    def quarters_of(row):
        return in_order([row[p * cells : (p + 1) * cells] for p in range(4)])

    for p in range(4):
        outs[p][layers : rows - layers] = inner[p][...]
    gradient_rows(layers - 1, 0)
    for layer in reversed(range(layers)):
        gradient_rows(layer, 1)
        gradient_taps(layer, 0)
        if layer:
            gradient_rows(layer - 1, 0)
        gradient_taps(layer, 1)


def run_outer(layers, offsets, halos, mains, inner, handed_edges, gradients, cg_edges, weights):
    rows, cells = mains[0][0].shape[:2]
    lon, chans = cg_edges[0].shape[1:]
    smem = pl.BlockSpec(memory_space=pltpu.SMEM)
    vmem = pl.BlockSpec(memory_space=pltpu.VMEM)
    args = [offsets, *halos, *mains[0], *mains[1], *inner, handed_edges, *gradients, *cg_edges]
    args += weights
    work = 2 * layers * layers * lon
    return pl.pallas_call(
        functools.partial(outer_kernel, layers),
        out_shape=[jax.ShapeDtypeStruct((rows, cells, chans), jnp.bfloat16)] * 4,
        in_specs=[smem] + [vmem] * (len(args) - 1),
        out_specs=[vmem] * 4,
        scratch_shapes=[
            *[pltpu.VMEM((layers + 2, chans // 128, 2 * lon, 128), jnp.float32)] * 2,
            *[pltpu.VMEM((layers, lon, chans), jnp.float32)] * 2,
        ],
        compiler_params=pltpu.CompilerParams(vmem_limit_bytes=24 * 2**20),
        cost_estimate=pl.CostEstimate(
            flops=6 * work * chans * weights[1].shape[2],
            bytes_accessed=work * chans * 10,
            transcendentals=2 * work * weights[1].shape[2],
        ),
        name="outer",
    )(*args)


def by_circles(dec_cot, saved_conv, dec_weight, w_in, w_out, conv_taps, dilation):
    layers = w_in.shape[0]

    def home(c):
        return c + 1

    def away(c, k):
        return (home(c) + (k if c == 0 else -k)) % 4

    order = (3, 1, 2)

    def gather(value):
        found = {0: value}
        for k in order:
            found[k] = routed(
                value, lambda c, z, j: (c, home(c), j) if z == away(c, k) else None
            )
        return [found[k] for k in range(4)]

    def neighbours(c, z, j):
        if z == away(c, 1):
            return c, home(c), j
        if z == away(c, 2):
            return 1 - c, home(c), j

    def across(c, z, j):
        return (1 - c, z, j) if z == home(1 - c) else None

    cot = partner(dec_cot[0], "segment")
    conv = saved_conv[0].transpose(0, 2, 1, 3)
    early, late, top, bottom = cut_edges(GROUPS, conv, cot)
    first = gather(early)
    below = routed(top, lambda c, z, j: (c, z, j - 1))
    above = routed(bottom, lambda c, z, j: (c, z, j + 1))

    two = routed(late, lambda c, z, j: (c, home(c), j) if z == away(c, 2) else None)
    sides, above, below = lax.optimization_barrier((late, above, below))
    one = routed(sides, lambda c, z, j: (c, home(c), j) if z == away(c, 1) else None)
    three = routed(sides, lambda c, z, j: (c, home(c), j) if z == away(c, 3) else None)
    second = [late, one, two, three]

    carried, gradients, cg_edges = dec_weight, [], []
    for layer in reversed(range(layers)):
        group, place = MESSAGE[layer]
        mains = (first, second)[group]
        found = run_inner(
            layer, layers, place, dilation, mains, carried, w_in, w_out, conv_taps
        )
        if layer == layers - 1:
            carried, cg_edge, handed_edges = found
        elif layer:
            carried, cg_edge = found
        else:
            *inner, cg_edge = found
        cg_edges.append(cg_edge)
        if layer:
            gradients.append(carried)
        if layer == layers - 1:
            edges = jnp.concatenate([above, below], axis=0)
            edges, carried = lax.optimization_barrier((edges, carried))
            one = routed(edges, neighbours)
            three = routed(edges, lambda c, z, j: (c, home(c), j) if z == away(c, 3) else None)
        if layer == 1:
            one, carried = lax.optimization_barrier((one, carried))
            halos = [edges, one, routed(one, across), three]
    weights = [dec_weight, w_in, w_out, conv_taps]
    found = run_outer(
        layers, dilation, halos, (first, second), inner, handed_edges, gradients, cg_edges, weights
    )

    result = jnp.where(on_home(), found[0], 0)
    for k in (2, 3, 1):
        result = result + routed(
            found[k], lambda c, z, j: (c, away(c, k), j) if z == home(c) else None
        )
    return result.transpose(1, 0, 2)[None]


def solution(mesh):
    in_specs = (
        P("segment", "lon", "lat", None),
        P("segment", None, "lon", "lat", None),
        P(),
        P(),
        P(),
        P(),
        P(),
    )
    out_specs = P("segment", "lon", "lat", None)
    gathers = mesh.shape["lon"] == 4 and mesh.shape["segment"] == 2
    return jax.shard_map(
        by_circles if gathers else by_exchange,
        mesh=mesh,
        in_specs=in_specs,
        out_specs=out_specs,
        check_vma=False,
    )
```

```python
import functools

import jax
import jax.numpy as jnp
from jax import lax
from jax.experimental import pallas as pl
from jax.experimental.pallas import tpu as pltpu
from jax.sharding import PartitionSpec as P

AXES = ("segment", "lon", "lat")


def with_halo(cells, sides, width):
    for axis, dim in sides:
        count = lax.axis_size(axis)
        ends = count - 1
        head = lax.slice_in_dim(cells, 0, width, axis=dim)
        tail = lax.slice_in_dim(cells, cells.shape[dim] - width, cells.shape[dim], axis=dim)
        cells = jnp.concatenate(
            [
                lax.ppermute(tail, axis, [(i, (i + 1) % count) for i in range(ends)]),
                cells,
                lax.ppermute(head, axis, [((i + 1) % count, i) for i in range(ends)]),
            ],
            axis=dim,
        )
    return cells


def from_behind(value, axis, steps):
    count = lax.axis_size(axis)
    pairs = [(source, (source + steps) % count) for source in range(count)]
    return lax.ppermute(value, axis, pairs)


def partner(block, axis):
    count = lax.axis_size(axis)
    return lax.ppermute(block, axis, [(i, i ^ 1) for i in range(count) if i ^ 1 < count])


def gelu_slope(hidden):
    normal_cdf = 0.5 * (1.0 + lax.erf(hidden * 0.7071067811865476))
    density = jnp.exp(-0.5 * hidden * hidden) * 0.3989422804014327
    return normal_cdf + hidden * density


def tap_adjoint(conv_grad, taps_now, offset):
    lon_cells = conv_grad.shape[0]
    lat_padded = with_halo(conv_grad, (("lat", 1),), 1)
    meridional = taps_now[3] * lat_padded[:, 2:] + taps_now[4] * lat_padded[:, :-2]
    centre = taps_now[1] * conv_grad
    rim_width = 3 * lon_cells
    pieces = []
    for distance in (3, 2, 1, 0, -1, -2, -3):
        pieces.append(conv_grad if distance == 0 else from_behind(conv_grad, "lon", distance))
    padded = jnp.concatenate(pieces, axis=0)
    ahead_cells = lax.dynamic_slice_in_dim(padded, rim_width + offset, lon_cells, 0)
    behind = lax.dynamic_slice_in_dim(padded, rim_width - offset, lon_cells, 0)
    zonal_sum = taps_now[0] * ahead_cells + taps_now[2] * behind
    zonal_sum = lax.optimization_barrier(zonal_sum.astype(jnp.bfloat16)).astype(jnp.float32)
    return zonal_sum + centre + meridional


def by_exchange(dec_cot, saved_conv, dec_weight, w_in, w_out, conv_taps, dilation):
    lon_cells, lat_rows, chans = saved_conv.shape[2:]
    own_cot = dec_cot[0].reshape(-1, dec_cot.shape[3])
    projected = jnp.einsum(
        "nv,cv->nc", own_cot, dec_weight, preferred_element_type=jnp.float32
    ).astype(jnp.bfloat16)
    gradient = lax.optimization_barrier(partner(projected, "segment")).astype(jnp.float32)
    for layer in reversed(range(w_in.shape[0])):
        conv_out = saved_conv[0, layer].reshape(-1, chans)
        hidden = jnp.dot(conv_out, w_in[layer], preferred_element_type=jnp.float32)
        act_grad = jnp.einsum(
            "nc,hc->nh",
            gradient.astype(jnp.bfloat16),
            w_out[layer],
            preferred_element_type=jnp.float32,
        )
        pre_grad = (act_grad * gelu_slope(hidden)).astype(jnp.bfloat16)
        conv_grad = jnp.einsum(
            "nh,ch->nc", pre_grad, w_in[layer], preferred_element_type=jnp.float32
        ).astype(jnp.bfloat16)
        tapped = tap_adjoint(
            conv_grad.reshape(lon_cells, lat_rows, chans), conv_taps[layer], dilation[layer]
        )
        gradient = gradient + tapped.reshape(-1, chans)
    return gradient.reshape(1, lon_cells, lat_rows, chans).astype(jnp.bfloat16)


def routed(value, hop):
    cores, cols, rows = (lax.axis_size(a) for a in AXES)
    pairs = []
    for c in range(cores):
        for z in range(cols):
            for j in range(rows):
                to = hop(c, z, j)
                if to is not None and 0 <= to[2] < rows:
                    pairs.append(((c * cols + z) * rows + j, (to[0] * cols + to[1]) * rows + to[2]))
    return lax.ppermute(value, AXES, pairs)


def row_chunks(low, high):
    count = max(1, round((high - low) / 7))
    edges = [low + (high - low) * i // count for i in range(count + 1)]
    return list(zip(edges[:-1], edges[1:]))


def on_home():
    return lax.axis_index("lon") == lax.axis_index("segment") + 1


GROUPS = ((3, 2), (1, 0))
MESSAGE = {layer: (g, k) for g, group in enumerate(GROUPS) for k, layer in enumerate(group)}


def edge_start(layer):
    return layer * (layer + 1) // 2


def edges_kernel(layers, groups, conv, cot, *outs):
    *messages, top_ref, bottom_ref = outs
    cot = jnp.swapaxes(cot[...].astype(jnp.float32), 0, 1).astype(conv.dtype)
    rows, chans, v = cot.shape[0], conv.shape[3], cot.shape[2]
    for message, group in zip(messages, groups):
        for k, layer in enumerate(group):
            message[:, :, k * chans : (k + 1) * chans] = conv[layer]
    messages[0][:, :, len(groups[0]) * chans :] = cot
    for layer in range(layers):
        here = slice(edge_start(layer), edge_start(layer + 1))
        top_ref[here] = conv[layer, : layer + 1]
        bottom_ref[here] = conv[layer, rows - layer - 1 :]
    for k in range(layers):
        at, lanes = edge_start(layers) + k // 2, slice(k % 2 * v, (k % 2 + 1) * v)
        top_ref[at, :, lanes] = cot[k]
        bottom_ref[at, :, lanes] = cot[rows - layers + k]


def cut_edges(groups, conv, cot):
    layers, rows, cells, chans = conv.shape
    edge = jax.ShapeDtypeStruct((edge_start(layers) + layers // 2, cells, chans), conv.dtype)
    widths = [len(group) * chans for group in groups]
    widths[0] += cot.shape[2]
    messages = [jax.ShapeDtypeStruct((rows, cells, width), conv.dtype) for width in widths]
    vmem = pl.BlockSpec(memory_space=pltpu.VMEM)
    return pl.pallas_call(
        functools.partial(edges_kernel, layers, groups),
        out_shape=messages + [edge, edge],
        in_specs=[vmem, vmem],
        out_specs=[vmem] * (len(groups) + 2),
        compiler_params=pltpu.CompilerParams(vmem_limit_bytes=16 * 2**20),
        name="edges",
    )(conv, cot)


def nt(a, b):
    return lax.dot_general(a, b, (((1,), (1,)), ((), ())), preferred_element_type=jnp.float32)


def halves_of(chans):
    return [(h, slice(h * 128, (h + 1) * 128)) for h in range(chans // 128)]


def in_order(pieces):
    upward = lax.axis_index("segment") == 0
    own, one, two, three = pieces
    return [own, jnp.where(upward, one, three), two, jnp.where(upward, three, one)]


def conv_gradient(conv_out, cot_low, w_in, w_out):
    hidden = jnp.dot(conv_out, w_in, preferred_element_type=jnp.float32)
    pre = (nt(cot_low, w_out) * gelu_slope(hidden)).astype(jnp.bfloat16)
    return nt(pre, w_in)


def keep_row(cg, at, row):
    lon = row.shape[0]
    for h, lanes in halves_of(row.shape[1]):
        cg[at, h, 0:lon] = row[:, lanes]
        cg[at, h, lon : 2 * lon] = row[:, lanes]


def tapped(cg, at, h, taps, offset):
    lon = cg.shape[2] // 2
    total = taps[0] * cg[at, h, pl.ds(offset, lon)] + taps[2] * cg[at, h, pl.ds(lon - offset, lon)]
    total += taps[1] * cg[at, h, 0:lon]
    return total + taps[3] * cg[at + 1, h, 0:lon] + taps[4] * cg[at - 1, h, 0:lon]


def inner_kernel(layer, layers, place, *refs):
    pl.when(on_home())(functools.partial(inner_body, layer, layers, place, *refs))


def inner_body(layer, layers, place, *refs):
    first, last = layer == layers - 1, layer == 0
    offset_ref, mains, refs = refs[0], [refs[1 + k] for k in (3, 1, 0, 2)], refs[5:]
    carried, w_in, w_out, taps, refs = refs[0], refs[1], refs[2], refs[3], refs[4:]
    outs, refs = (refs[:4], refs[4:]) if last else (refs[:1], refs[1:])
    cg_edges, refs = refs[0], refs[1:]
    if first:
        handed_edges, cg, handed = refs
    else:
        (cg,) = refs
    lon, chans = cg_edges.shape[1:]
    cells, rows = lon // 4, cg.shape[0]
    skipped = layers - 1 - layer
    convs, cots = slice(place * chans, (place + 1) * chans), slice(len(GROUPS[0]) * chans, mains[0].shape[2])
    offset = offset_ref[layer]

    def rows_of(r0, r1, lanes):
        found = [in_order([m[skipped + r, :, lanes] for m in mains]) for r in range(r0, r1)]
        return jnp.concatenate(sum(found, []), axis=0)

    def taps_of(r):
        for h, lanes in halves_of(chans):
            total = tapped(cg, r, h, [taps[layer, k : k + 1, lanes] for k in range(5)], offset)
            total += (handed[r, :, lanes].astype(jnp.float32) if first else carried[r, :, lanes])
            if last:
                low = total.astype(jnp.bfloat16)
                quarters = in_order([low[p * cells : (p + 1) * cells] for p in range(4)])
                for p in range(4):
                    outs[p][r - 1, :, lanes] = quarters[p]
            else:
                outs[0][r - 1, :, lanes] = total

    edge_rows = (0, 1, rows - 2, rows - 1)
    for r0, r1 in row_chunks(0, rows):
        if first:
            cot_low = nt(rows_of(r0, r1, cots), carried[...]).astype(jnp.bfloat16)
        else:
            cot_low = carried[r0:r1].reshape((r1 - r0) * lon, chans).astype(jnp.bfloat16)
        conv_grad = conv_gradient(rows_of(r0, r1, convs), cot_low, w_in[layer], w_out[layer])
        conv_grad = conv_grad.reshape(r1 - r0, lon, chans)
        if first:
            handed[r0:r1] = cot_low.reshape(r1 - r0, lon, chans)
        for r in range(r0, r1):
            keep_row(cg, r, conv_grad[r - r0])
            if r in edge_rows:
                cg_edges[edge_rows.index(r)] = conv_grad[r - r0]
    half = (rows - 2) // 2

    def taps_of_half(k, carry):
        for r in range(half):
            taps_of(1 + k * half + r)
        return carry

    lax.fori_loop(0, 2, taps_of_half, 0)
    if first:
        handed_edges[0] = handed[0].astype(jnp.float32)
        handed_edges[1] = handed[rows - 1].astype(jnp.float32)


def run_inner(layer, layers, place, offsets, mains, carried, w_in, w_out, taps):
    first, last = layer == layers - 1, layer == 0
    rows, cells = mains[0].shape[:2]
    chans = w_in.shape[1]
    lon = 4 * cells
    rows -= 2 * (layers - 1 - layer)
    smem = pl.BlockSpec(memory_space=pltpu.SMEM)
    vmem = pl.BlockSpec(memory_space=pltpu.VMEM)
    args = [offsets, *(mains[k] for k in (2, 1, 3, 0)), carried, w_in, w_out, taps]
    if last:
        out = [jax.ShapeDtypeStruct((rows - 2, cells, chans), jnp.bfloat16)] * 4
    else:
        out = [jax.ShapeDtypeStruct((rows - 2, lon, chans), jnp.float32)]
    out.append(jax.ShapeDtypeStruct((4, lon, chans), jnp.float32))
    scratch = [pltpu.VMEM((rows, chans // 128, 2 * lon, 128), jnp.float32)]
    if first:
        out.append(jax.ShapeDtypeStruct((2, lon, chans), jnp.float32))
        scratch.append(pltpu.VMEM((rows, lon, chans), jnp.bfloat16))
    work = rows * lon
    return pl.pallas_call(
        functools.partial(inner_kernel, layer, layers, place),
        out_shape=out,
        in_specs=[smem] + [vmem] * (len(args) - 1),
        out_specs=[vmem] * len(out),
        scratch_shapes=scratch,
        compiler_params=pltpu.CompilerParams(vmem_limit_bytes=24 * 2**20),
        cost_estimate=pl.CostEstimate(
            flops=6 * work * chans * w_in.shape[2],
            bytes_accessed=work * chans * 10,
            transcendentals=2 * work * w_in.shape[2],
        ),
        name=f"inner_{layer}",
    )(*args)


def outer_kernel(layers, *refs):
    pl.when(on_home())(functools.partial(outer_body, layers, *refs))


def outer_body(layers, *refs):
    offset_ref, refs = refs[0], refs[1:]
    halos, mains, refs = refs[:4], (refs[4:8], refs[8:12]), refs[12:]
    inner, refs = refs[:4], refs[4:]
    handed_edges, gradients, refs = refs[0], refs[1:layers], refs[layers:]
    cg_edges, refs = refs[:layers], refs[layers:]
    dec_weight, w_in, w_out, taps, refs = refs[0], refs[1], refs[2], refs[3], refs[4:]
    outs, cg, grad = refs[:4], refs[4:6], refs[6:8]
    rows, cells = mains[0][0].shape[:2]
    lon, chans = cg_edges[0].shape[1:]
    v = dec_weight.shape[1]
    half_halo = halos[0].shape[0] // 2
    lat = lax.axis_index("lat")
    has_above = jnp.where(lat > 0, 1.0, 0.0).astype(jnp.float32)
    has_below = jnp.where(lat < lax.axis_size("lat") - 1, 1.0, 0.0).astype(jnp.float32)

    def conv_row(layer, r):
        if 0 <= r < rows:
            group, place = MESSAGE[layer]
            return in_order([m[r, :, place * chans : (place + 1) * chans] for m in mains[group]])
        at = edge_start(layer) + (r + layer + 1 if r < 0 else half_halo + r - rows)
        return in_order([h[at] for h in halos])

    def cot_row(r):
        k = r + layers if r < 0 else r - rows
        at = edge_start(layers) + k // 2 + (0 if r < 0 else half_halo)
        return in_order([h[at, :, k % 2 * v : (k % 2 + 1) * v] for h in halos])

    def gradient_rows(layer, side):
        shift = layers - 1 - layer
        here = range(-layers + shift, shift) if side == 0 else range(rows - shift, rows - shift + layers)
        if layer == layers - 1:
            cot = jnp.concatenate(sum([cot_row(r) for r in here], []), axis=0)
            cot_low = nt(cot, dec_weight[...]).astype(jnp.bfloat16)
            grad[side][...] = cot_low.astype(jnp.float32).reshape(grad[side].shape)
        else:
            cot_low = grad[side][...].reshape(layers * lon, chans).astype(jnp.bfloat16)
        conv_out = jnp.concatenate(sum([conv_row(layer, r) for r in here], []), axis=0)
        found = conv_gradient(conv_out, cot_low, w_in[layer], w_out[layer])
        found = found.reshape(layers, lon, chans)
        edge = cg_edges[layers - 1 - layer]
        for k, r in enumerate(here):
            row = found[k]
            if r < 0:
                row = row * has_above
            if r >= rows:
                row = row * has_below
            keep_row(cg[side], k if side == 0 else k + 2, row)
        for k in range(2):
            keep_row(cg[side], layers + k if side == 0 else k, edge[k + 2 * side])

    def gradient_taps(layer, side):
        if layer == layers - 1:
            near = handed_edges[side]
        else:
            before = gradients[layers - 2 - layer]
            near = before[0 if side == 0 else before.shape[0] - 1]
        old = [grad[side][k] for k in range(layers)]
        old = [*old[1:], near] if side == 0 else [near, *old[:-1]]
        for k in range(layers):
            for h, lanes in halves_of(chans):
                tap = [taps[layer, n : n + 1, lanes] for n in range(5)]
                total = old[k][:, lanes] + tapped(cg[side], k + 1, h, tap, offset_ref[layer])
                if layer:
                    grad[side][k, :, lanes] = total
                else:
                    quarters = quarters_of(total.astype(jnp.bfloat16))
                    r = k if side == 0 else rows - layers + k
                    for p in range(4):
                        outs[p][r, :, lanes] = quarters[p]

    def quarters_of(row):
        return in_order([row[p * cells : (p + 1) * cells] for p in range(4)])

    for p in range(4):
        outs[p][layers : rows - layers] = inner[p][...]
    gradient_rows(layers - 1, 0)
    for layer in reversed(range(layers)):
        gradient_rows(layer, 1)
        gradient_taps(layer, 0)
        if layer:
            gradient_rows(layer - 1, 0)
        gradient_taps(layer, 1)


def run_outer(layers, offsets, halos, mains, inner, handed_edges, gradients, cg_edges, weights):
    rows, cells = mains[0][0].shape[:2]
    lon, chans = cg_edges[0].shape[1:]
    smem = pl.BlockSpec(memory_space=pltpu.SMEM)
    vmem = pl.BlockSpec(memory_space=pltpu.VMEM)
    args = [offsets, *halos, *mains[0], *mains[1], *inner, handed_edges, *gradients, *cg_edges]
    args += weights
    work = 2 * layers * layers * lon
    return pl.pallas_call(
        functools.partial(outer_kernel, layers),
        out_shape=[jax.ShapeDtypeStruct((rows, cells, chans), jnp.bfloat16)] * 4,
        in_specs=[smem] + [vmem] * (len(args) - 1),
        out_specs=[vmem] * 4,
        scratch_shapes=[
            *[pltpu.VMEM((layers + 2, chans // 128, 2 * lon, 128), jnp.float32)] * 2,
            *[pltpu.VMEM((layers, lon, chans), jnp.float32)] * 2,
        ],
        compiler_params=pltpu.CompilerParams(vmem_limit_bytes=24 * 2**20),
        cost_estimate=pl.CostEstimate(
            flops=6 * work * chans * weights[1].shape[2],
            bytes_accessed=work * chans * 10,
            transcendentals=2 * work * weights[1].shape[2],
        ),
        name="outer",
    )(*args)


def by_circles(dec_cot, saved_conv, dec_weight, w_in, w_out, conv_taps, dilation):
    layers = w_in.shape[0]

    def home(c):
        return c + 1

    def away(c, k):
        return (home(c) + (k if c == 0 else -k)) % 4

    order = (3, 1, 2)

    def gather(value):
        found = {0: value}
        for k in order:
            found[k] = routed(
                value, lambda c, z, j: (c, home(c), j) if z == away(c, k) else None
            )
        return [found[k] for k in range(4)]

    def neighbours(c, z, j):
        if z == away(c, 1):
            return c, home(c), j
        if z == away(c, 2):
            return 1 - c, home(c), j

    def across(c, z, j):
        return (1 - c, z, j) if z == home(1 - c) else None

    cot = partner(dec_cot[0], "segment")
    conv = saved_conv[0].transpose(0, 2, 1, 3)
    early, late, top, bottom = cut_edges(GROUPS, conv, cot)
    first = gather(early)
    below = routed(top, lambda c, z, j: (c, z, j - 1))
    above = routed(bottom, lambda c, z, j: (c, z, j + 1))

    two = routed(late, lambda c, z, j: (c, home(c), j) if z == away(c, 2) else None)
    sides, above, below = lax.optimization_barrier((late, above, below))
    one = routed(sides, lambda c, z, j: (c, home(c), j) if z == away(c, 1) else None)
    three = routed(sides, lambda c, z, j: (c, home(c), j) if z == away(c, 3) else None)
    second = [late, one, two, three]

    carried, gradients, cg_edges = dec_weight, [], []
    for layer in reversed(range(layers)):
        group, place = MESSAGE[layer]
        mains = (first, second)[group]
        found = run_inner(
            layer, layers, place, dilation, mains, carried, w_in, w_out, conv_taps
        )
        if layer == layers - 1:
            carried, cg_edge, handed_edges = found
        elif layer:
            carried, cg_edge = found
        else:
            *inner, cg_edge = found
        cg_edges.append(cg_edge)
        if layer:
            gradients.append(carried)
        if layer == layers - 1:
            edges = jnp.concatenate([above, below], axis=0)
            edges, carried = lax.optimization_barrier((edges, carried))
            one = routed(edges, neighbours)
            three = routed(edges, lambda c, z, j: (c, home(c), j) if z == away(c, 3) else None)
        if layer == 1:
            one, carried = lax.optimization_barrier((one, carried))
            halos = [edges, one, routed(one, across), three]
    weights = [dec_weight, w_in, w_out, conv_taps]
    found = run_outer(
        layers, dilation, halos, (first, second), inner, handed_edges, gradients, cg_edges, weights
    )

    result = jnp.where(on_home(), found[0], 0)
    for k in (2, 3, 1):
        result = result + routed(
            found[k], lambda c, z, j: (c, away(c, k), j) if z == home(c) else None
        )
    return result.transpose(1, 0, 2)[None]


def solution(mesh):
    in_specs = (
        P("segment", "lon", "lat", None),
        P("segment", None, "lon", "lat", None),
        P(),
        P(),
        P(),
        P(),
        P(),
    )
    out_specs = P("segment", "lon", "lat", None)
    gathers = mesh.shape["lon"] == 4 and mesh.shape["segment"] == 2
    return jax.shard_map(
        by_circles if gathers else by_exchange,
        mesh=mesh,
        in_specs=in_specs,
        out_specs=out_specs,
        check_vma=False,
    )
```

```python
import functools

import jax
import jax.numpy as jnp
from jax import lax
from jax.experimental import pallas as pl
from jax.experimental.pallas import tpu as pltpu
from jax.sharding import PartitionSpec as P

AXES = ("segment", "lon", "lat")


def with_halo(cells, sides, width):
    for axis, dim in sides:
        count = lax.axis_size(axis)
        ends = count - 1
        head = lax.slice_in_dim(cells, 0, width, axis=dim)
        tail = lax.slice_in_dim(cells, cells.shape[dim] - width, cells.shape[dim], axis=dim)
        cells = jnp.concatenate(
            [
                lax.ppermute(tail, axis, [(i, (i + 1) % count) for i in range(ends)]),
                cells,
                lax.ppermute(head, axis, [((i + 1) % count, i) for i in range(ends)]),
            ],
            axis=dim,
        )
    return cells


def from_behind(value, axis, steps):
    count = lax.axis_size(axis)
    pairs = [(source, (source + steps) % count) for source in range(count)]
    return lax.ppermute(value, axis, pairs)


def partner(block, axis):
    count = lax.axis_size(axis)
    return lax.ppermute(block, axis, [(i, i ^ 1) for i in range(count) if i ^ 1 < count])


def gelu_slope(hidden):
    normal_cdf = 0.5 * (1.0 + lax.erf(hidden * 0.7071067811865476))
    density = jnp.exp(-0.5 * hidden * hidden) * 0.3989422804014327
    return normal_cdf + hidden * density


def tap_adjoint(conv_grad, taps_now, offset):
    lon_cells = conv_grad.shape[0]
    lat_padded = with_halo(conv_grad, (("lat", 1),), 1)
    meridional = taps_now[3] * lat_padded[:, 2:] + taps_now[4] * lat_padded[:, :-2]
    centre = taps_now[1] * conv_grad
    rim_width = 3 * lon_cells
    pieces = []
    for distance in (3, 2, 1, 0, -1, -2, -3):
        pieces.append(conv_grad if distance == 0 else from_behind(conv_grad, "lon", distance))
    padded = jnp.concatenate(pieces, axis=0)
    ahead_cells = lax.dynamic_slice_in_dim(padded, rim_width + offset, lon_cells, 0)
    behind = lax.dynamic_slice_in_dim(padded, rim_width - offset, lon_cells, 0)
    zonal_sum = taps_now[0] * ahead_cells + taps_now[2] * behind
    zonal_sum = lax.optimization_barrier(zonal_sum.astype(jnp.bfloat16)).astype(jnp.float32)
    return zonal_sum + centre + meridional


def by_exchange(dec_cot, saved_conv, dec_weight, w_in, w_out, conv_taps, dilation):
    lon_cells, lat_rows, chans = saved_conv.shape[2:]
    own_cot = dec_cot[0].reshape(-1, dec_cot.shape[3])
    projected = jnp.einsum(
        "nv,cv->nc", own_cot, dec_weight, preferred_element_type=jnp.float32
    ).astype(jnp.bfloat16)
    gradient = lax.optimization_barrier(partner(projected, "segment")).astype(jnp.float32)
    for layer in reversed(range(w_in.shape[0])):
        conv_out = saved_conv[0, layer].reshape(-1, chans)
        hidden = jnp.dot(conv_out, w_in[layer], preferred_element_type=jnp.float32)
        act_grad = jnp.einsum(
            "nc,hc->nh",
            gradient.astype(jnp.bfloat16),
            w_out[layer],
            preferred_element_type=jnp.float32,
        )
        pre_grad = (act_grad * gelu_slope(hidden)).astype(jnp.bfloat16)
        conv_grad = jnp.einsum(
            "nh,ch->nc", pre_grad, w_in[layer], preferred_element_type=jnp.float32
        ).astype(jnp.bfloat16)
        tapped = tap_adjoint(
            conv_grad.reshape(lon_cells, lat_rows, chans), conv_taps[layer], dilation[layer]
        )
        gradient = gradient + tapped.reshape(-1, chans)
    return gradient.reshape(1, lon_cells, lat_rows, chans).astype(jnp.bfloat16)


def routed(value, hop):
    cores, cols, rows = (lax.axis_size(a) for a in AXES)
    pairs = []
    for c in range(cores):
        for z in range(cols):
            for j in range(rows):
                to = hop(c, z, j)
                if to is not None and 0 <= to[2] < rows:
                    pairs.append(((c * cols + z) * rows + j, (to[0] * cols + to[1]) * rows + to[2]))
    return lax.ppermute(value, AXES, pairs)


def row_chunks(low, high):
    count = max(1, round((high - low) / 11))
    edges = [low + (high - low) * i // count for i in range(count + 1)]
    return list(zip(edges[:-1], edges[1:]))


def on_home():
    return lax.axis_index("lon") == lax.axis_index("segment") + 1


GROUPS = ((3, 2), (1, 0))
MESSAGE = {layer: (g, k) for g, group in enumerate(GROUPS) for k, layer in enumerate(group)}


def edge_start(layer):
    return layer * (layer + 1) // 2


def edges_kernel(layers, groups, conv, cot, *outs):
    *messages, top_ref, bottom_ref = outs
    cot = jnp.swapaxes(cot[...].astype(jnp.float32), 0, 1).astype(conv.dtype)
    rows, chans, v = cot.shape[0], conv.shape[3], cot.shape[2]
    for message, group in zip(messages, groups):
        for k, layer in enumerate(group):
            message[:, :, k * chans : (k + 1) * chans] = conv[layer]
    messages[0][:, :, len(groups[0]) * chans :] = cot
    for layer in range(layers):
        here = slice(edge_start(layer), edge_start(layer + 1))
        top_ref[here] = conv[layer, : layer + 1]
        bottom_ref[here] = conv[layer, rows - layer - 1 :]
    for k in range(layers):
        at, lanes = edge_start(layers) + k // 2, slice(k % 2 * v, (k % 2 + 1) * v)
        top_ref[at, :, lanes] = cot[k]
        bottom_ref[at, :, lanes] = cot[rows - layers + k]


def cut_edges(groups, conv, cot):
    layers, rows, cells, chans = conv.shape
    edge = jax.ShapeDtypeStruct((edge_start(layers) + layers // 2, cells, chans), conv.dtype)
    widths = [len(group) * chans for group in groups]
    widths[0] += cot.shape[2]
    messages = [jax.ShapeDtypeStruct((rows, cells, width), conv.dtype) for width in widths]
    vmem = pl.BlockSpec(memory_space=pltpu.VMEM)
    return pl.pallas_call(
        functools.partial(edges_kernel, layers, groups),
        out_shape=messages + [edge, edge],
        in_specs=[vmem, vmem],
        out_specs=[vmem] * (len(groups) + 2),
        compiler_params=pltpu.CompilerParams(vmem_limit_bytes=16 * 2**20),
        name="edges",
    )(conv, cot)


def nt(a, b):
    return lax.dot_general(a, b, (((1,), (1,)), ((), ())), preferred_element_type=jnp.float32)


def halves_of(chans):
    return [(h, slice(h * 128, (h + 1) * 128)) for h in range(chans // 128)]


def in_order(pieces):
    upward = lax.axis_index("segment") == 0
    own, one, two, three = pieces
    return [own, jnp.where(upward, one, three), two, jnp.where(upward, three, one)]


def conv_gradient(conv_out, cot_low, w_in, w_out):
    hidden = jnp.dot(conv_out, w_in, preferred_element_type=jnp.float32)
    pre = (nt(cot_low, w_out) * gelu_slope(hidden)).astype(jnp.bfloat16)
    return nt(pre, w_in)


def keep_row(cg, at, row):
    lon = row.shape[0]
    for h, lanes in halves_of(row.shape[1]):
        cg[at, h, 0:lon] = row[:, lanes]
        cg[at, h, lon : 2 * lon] = row[:, lanes]


def tapped(cg, at, h, taps, offset):
    lon = cg.shape[2] // 2
    total = taps[0] * cg[at, h, pl.ds(offset, lon)] + taps[2] * cg[at, h, pl.ds(lon - offset, lon)]
    total += taps[1] * cg[at, h, 0:lon]
    return total + taps[3] * cg[at + 1, h, 0:lon] + taps[4] * cg[at - 1, h, 0:lon]


def inner_kernel(layer, layers, place, *refs):
    pl.when(on_home())(functools.partial(inner_body, layer, layers, place, *refs))


def inner_body(layer, layers, place, *refs):
    first, last = layer == layers - 1, layer == 0
    offset_ref, mains, refs = refs[0], [refs[1 + k] for k in (3, 1, 0, 2)], refs[5:]
    carried, w_in, w_out, taps, refs = refs[0], refs[1], refs[2], refs[3], refs[4:]
    outs, refs = (refs[:4], refs[4:]) if last else (refs[:1], refs[1:])
    cg_edges, refs = refs[0], refs[1:]
    if first:
        handed_edges, cg, handed = refs
    else:
        (cg,) = refs
    lon, chans = cg_edges.shape[1:]
    cells, rows = lon // 4, cg.shape[0]
    skipped = layers - 1 - layer
    convs, cots = slice(place * chans, (place + 1) * chans), slice(len(GROUPS[0]) * chans, mains[0].shape[2])
    offset = offset_ref[layer]

    def rows_of(r0, r1, lanes):
        found = [in_order([m[skipped + r, :, lanes] for m in mains]) for r in range(r0, r1)]
        return jnp.concatenate(sum(found, []), axis=0)

    def taps_of(r):
        for h, lanes in halves_of(chans):
            total = tapped(cg, r, h, [taps[layer, k : k + 1, lanes] for k in range(5)], offset)
            total += (handed[r, :, lanes].astype(jnp.float32) if first else carried[r, :, lanes])
            if last:
                low = total.astype(jnp.bfloat16)
                quarters = in_order([low[p * cells : (p + 1) * cells] for p in range(4)])
                for p in range(4):
                    outs[p][r - 1, :, lanes] = quarters[p]
            else:
                outs[0][r - 1, :, lanes] = total

    edge_rows = (0, 1, rows - 2, rows - 1)
    for r0, r1 in row_chunks(0, rows):
        if first:
            cot_low = nt(rows_of(r0, r1, cots), carried[...]).astype(jnp.bfloat16)
        else:
            cot_low = carried[r0:r1].reshape((r1 - r0) * lon, chans).astype(jnp.bfloat16)
        conv_grad = conv_gradient(rows_of(r0, r1, convs), cot_low, w_in[layer], w_out[layer])
        conv_grad = conv_grad.reshape(r1 - r0, lon, chans)
        if first:
            handed[r0:r1] = cot_low.reshape(r1 - r0, lon, chans)
        for r in range(r0, r1):
            keep_row(cg, r, conv_grad[r - r0])
            if r in edge_rows:
                cg_edges[edge_rows.index(r)] = conv_grad[r - r0]
    half = (rows - 2) // 2

    def taps_of_half(k, carry):
        for r in range(half):
            taps_of(1 + k * half + r)
        return carry

    lax.fori_loop(0, 2, taps_of_half, 0)
    if first:
        handed_edges[0] = handed[0].astype(jnp.float32)
        handed_edges[1] = handed[rows - 1].astype(jnp.float32)


def run_inner(layer, layers, place, offsets, mains, carried, w_in, w_out, taps):
    first, last = layer == layers - 1, layer == 0
    rows, cells = mains[0].shape[:2]
    chans = w_in.shape[1]
    lon = 4 * cells
    rows -= 2 * (layers - 1 - layer)
    smem = pl.BlockSpec(memory_space=pltpu.SMEM)
    vmem = pl.BlockSpec(memory_space=pltpu.VMEM)
    args = [offsets, *(mains[k] for k in (2, 1, 3, 0)), carried, w_in, w_out, taps]
    if last:
        out = [jax.ShapeDtypeStruct((rows - 2, cells, chans), jnp.bfloat16)] * 4
    else:
        out = [jax.ShapeDtypeStruct((rows - 2, lon, chans), jnp.float32)]
    out.append(jax.ShapeDtypeStruct((4, lon, chans), jnp.float32))
    scratch = [pltpu.VMEM((rows, chans // 128, 2 * lon, 128), jnp.float32)]
    if first:
        out.append(jax.ShapeDtypeStruct((2, lon, chans), jnp.float32))
        scratch.append(pltpu.VMEM((rows, lon, chans), jnp.bfloat16))
    work = rows * lon
    return pl.pallas_call(
        functools.partial(inner_kernel, layer, layers, place),
        out_shape=out,
        in_specs=[smem] + [vmem] * (len(args) - 1),
        out_specs=[vmem] * len(out),
        scratch_shapes=scratch,
        compiler_params=pltpu.CompilerParams(vmem_limit_bytes=24 * 2**20),
        cost_estimate=pl.CostEstimate(
            flops=6 * work * chans * w_in.shape[2],
            bytes_accessed=work * chans * 10,
            transcendentals=2 * work * w_in.shape[2],
        ),
        name=f"inner_{layer}",
    )(*args)


def outer_kernel(layers, *refs):
    pl.when(on_home())(functools.partial(outer_body, layers, *refs))


def outer_body(layers, *refs):
    offset_ref, refs = refs[0], refs[1:]
    halos, mains, refs = refs[:4], (refs[4:8], refs[8:12]), refs[12:]
    inner, refs = refs[:4], refs[4:]
    handed_edges, gradients, refs = refs[0], refs[1:layers], refs[layers:]
    cg_edges, refs = refs[:layers], refs[layers:]
    dec_weight, w_in, w_out, taps, refs = refs[0], refs[1], refs[2], refs[3], refs[4:]
    outs, cg, grad = refs[:4], refs[4:6], refs[6:8]
    rows, cells = mains[0][0].shape[:2]
    lon, chans = cg_edges[0].shape[1:]
    v = dec_weight.shape[1]
    half_halo = halos[0].shape[0] // 2
    lat = lax.axis_index("lat")
    has_above = jnp.where(lat > 0, 1.0, 0.0).astype(jnp.float32)
    has_below = jnp.where(lat < lax.axis_size("lat") - 1, 1.0, 0.0).astype(jnp.float32)

    def conv_row(layer, r):
        if 0 <= r < rows:
            group, place = MESSAGE[layer]
            return in_order([m[r, :, place * chans : (place + 1) * chans] for m in mains[group]])
        at = edge_start(layer) + (r + layer + 1 if r < 0 else half_halo + r - rows)
        return in_order([h[at] for h in halos])

    def cot_row(r):
        k = r + layers if r < 0 else r - rows
        at = edge_start(layers) + k // 2 + (0 if r < 0 else half_halo)
        return in_order([h[at, :, k % 2 * v : (k % 2 + 1) * v] for h in halos])

    def gradient_rows(layer, side):
        shift = layers - 1 - layer
        here = range(-layers + shift, shift) if side == 0 else range(rows - shift, rows - shift + layers)
        if layer == layers - 1:
            cot = jnp.concatenate(sum([cot_row(r) for r in here], []), axis=0)
            cot_low = nt(cot, dec_weight[...]).astype(jnp.bfloat16)
            grad[side][...] = cot_low.astype(jnp.float32).reshape(grad[side].shape)
        else:
            cot_low = grad[side][...].reshape(layers * lon, chans).astype(jnp.bfloat16)
        conv_out = jnp.concatenate(sum([conv_row(layer, r) for r in here], []), axis=0)
        found = conv_gradient(conv_out, cot_low, w_in[layer], w_out[layer])
        found = found.reshape(layers, lon, chans)
        edge = cg_edges[layers - 1 - layer]
        for k, r in enumerate(here):
            row = found[k]
            if r < 0:
                row = row * has_above
            if r >= rows:
                row = row * has_below
            keep_row(cg[side], k if side == 0 else k + 2, row)
        for k in range(2):
            keep_row(cg[side], layers + k if side == 0 else k, edge[k + 2 * side])

    def gradient_taps(layer, side):
        if layer == layers - 1:
            near = handed_edges[side]
        else:
            before = gradients[layers - 2 - layer]
            near = before[0 if side == 0 else before.shape[0] - 1]
        old = [grad[side][k] for k in range(layers)]
        old = [*old[1:], near] if side == 0 else [near, *old[:-1]]
        for k in range(layers):
            for h, lanes in halves_of(chans):
                tap = [taps[layer, n : n + 1, lanes] for n in range(5)]
                total = old[k][:, lanes] + tapped(cg[side], k + 1, h, tap, offset_ref[layer])
                if layer:
                    grad[side][k, :, lanes] = total
                else:
                    quarters = quarters_of(total.astype(jnp.bfloat16))
                    r = k if side == 0 else rows - layers + k
                    for p in range(4):
                        outs[p][r, :, lanes] = quarters[p]

    def quarters_of(row):
        return in_order([row[p * cells : (p + 1) * cells] for p in range(4)])

    for p in range(4):
        outs[p][layers : rows - layers] = inner[p][...]
    gradient_rows(layers - 1, 0)
    for layer in reversed(range(layers)):
        gradient_rows(layer, 1)
        gradient_taps(layer, 0)
        if layer:
            gradient_rows(layer - 1, 0)
        gradient_taps(layer, 1)


def run_outer(layers, offsets, halos, mains, inner, handed_edges, gradients, cg_edges, weights):
    rows, cells = mains[0][0].shape[:2]
    lon, chans = cg_edges[0].shape[1:]
    smem = pl.BlockSpec(memory_space=pltpu.SMEM)
    vmem = pl.BlockSpec(memory_space=pltpu.VMEM)
    args = [offsets, *halos, *mains[0], *mains[1], *inner, handed_edges, *gradients, *cg_edges]
    args += weights
    work = 2 * layers * layers * lon
    return pl.pallas_call(
        functools.partial(outer_kernel, layers),
        out_shape=[jax.ShapeDtypeStruct((rows, cells, chans), jnp.bfloat16)] * 4,
        in_specs=[smem] + [vmem] * (len(args) - 1),
        out_specs=[vmem] * 4,
        scratch_shapes=[
            *[pltpu.VMEM((layers + 2, chans // 128, 2 * lon, 128), jnp.float32)] * 2,
            *[pltpu.VMEM((layers, lon, chans), jnp.float32)] * 2,
        ],
        compiler_params=pltpu.CompilerParams(vmem_limit_bytes=24 * 2**20),
        cost_estimate=pl.CostEstimate(
            flops=6 * work * chans * weights[1].shape[2],
            bytes_accessed=work * chans * 10,
            transcendentals=2 * work * weights[1].shape[2],
        ),
        name="outer",
    )(*args)


def by_circles(dec_cot, saved_conv, dec_weight, w_in, w_out, conv_taps, dilation):
    layers = w_in.shape[0]

    def home(c):
        return c + 1

    def away(c, k):
        return (home(c) + (k if c == 0 else -k)) % 4

    order = (3, 1, 2)

    def gather(value):
        found = {0: value}
        for k in order:
            found[k] = routed(
                value, lambda c, z, j: (c, home(c), j) if z == away(c, k) else None
            )
        return [found[k] for k in range(4)]

    def neighbours(c, z, j):
        if z == away(c, 1):
            return c, home(c), j
        if z == away(c, 2):
            return 1 - c, home(c), j

    def across(c, z, j):
        return (1 - c, z, j) if z == home(1 - c) else None

    cot = partner(dec_cot[0], "segment")
    conv = saved_conv[0].transpose(0, 2, 1, 3)
    early, late, top, bottom = cut_edges(GROUPS, conv, cot)
    first = gather(early)
    below = routed(top, lambda c, z, j: (c, z, j - 1))
    above = routed(bottom, lambda c, z, j: (c, z, j + 1))

    two = routed(late, lambda c, z, j: (c, home(c), j) if z == away(c, 2) else None)
    sides, above, below = lax.optimization_barrier((late, above, below))
    one = routed(sides, lambda c, z, j: (c, home(c), j) if z == away(c, 1) else None)
    three = routed(sides, lambda c, z, j: (c, home(c), j) if z == away(c, 3) else None)
    second = [late, one, two, three]

    carried, gradients, cg_edges = dec_weight, [], []
    for layer in reversed(range(layers)):
        group, place = MESSAGE[layer]
        mains = (first, second)[group]
        found = run_inner(
            layer, layers, place, dilation, mains, carried, w_in, w_out, conv_taps
        )
        if layer == layers - 1:
            carried, cg_edge, handed_edges = found
        elif layer:
            carried, cg_edge = found
        else:
            *inner, cg_edge = found
        cg_edges.append(cg_edge)
        if layer:
            gradients.append(carried)
        if layer == layers - 1:
            edges = jnp.concatenate([above, below], axis=0)
            edges, carried = lax.optimization_barrier((edges, carried))
            one = routed(edges, neighbours)
            three = routed(edges, lambda c, z, j: (c, home(c), j) if z == away(c, 3) else None)
        if layer == 1:
            one, carried = lax.optimization_barrier((one, carried))
            halos = [edges, one, routed(one, across), three]
    weights = [dec_weight, w_in, w_out, conv_taps]
    found = run_outer(
        layers, dilation, halos, (first, second), inner, handed_edges, gradients, cg_edges, weights
    )

    result = jnp.where(on_home(), found[0], 0)
    for k in (2, 3, 1):
        result = result + routed(
            found[k], lambda c, z, j: (c, away(c, k), j) if z == home(c) else None
        )
    return result.transpose(1, 0, 2)[None]


def solution(mesh):
    in_specs = (
        P("segment", "lon", "lat", None),
        P("segment", None, "lon", "lat", None),
        P(),
        P(),
        P(),
        P(),
        P(),
    )
    out_specs = P("segment", "lon", "lat", None)
    gathers = mesh.shape["lon"] == 4 and mesh.shape["segment"] == 2
    return jax.shard_map(
        by_circles if gathers else by_exchange,
        mesh=mesh,
        in_specs=in_specs,
        out_specs=out_specs,
        check_vma=False,
    )
```

```python
import functools

import jax
import jax.numpy as jnp
from jax import lax
from jax.experimental import pallas as pl
from jax.experimental.pallas import tpu as pltpu
from jax.sharding import PartitionSpec as P

AXES = ("segment", "lon", "lat")


def with_halo(cells, sides, width):
    for axis, dim in sides:
        count = lax.axis_size(axis)
        ends = count - 1
        head = lax.slice_in_dim(cells, 0, width, axis=dim)
        tail = lax.slice_in_dim(cells, cells.shape[dim] - width, cells.shape[dim], axis=dim)
        cells = jnp.concatenate(
            [
                lax.ppermute(tail, axis, [(i, (i + 1) % count) for i in range(ends)]),
                cells,
                lax.ppermute(head, axis, [((i + 1) % count, i) for i in range(ends)]),
            ],
            axis=dim,
        )
    return cells


def from_behind(value, axis, steps):
    count = lax.axis_size(axis)
    pairs = [(source, (source + steps) % count) for source in range(count)]
    return lax.ppermute(value, axis, pairs)


def partner(block, axis):
    count = lax.axis_size(axis)
    return lax.ppermute(block, axis, [(i, i ^ 1) for i in range(count) if i ^ 1 < count])


def gelu_slope(hidden):
    normal_cdf = 0.5 * (1.0 + lax.erf(hidden * 0.7071067811865476))
    density = jnp.exp(-0.5 * hidden * hidden) * 0.3989422804014327
    return normal_cdf + hidden * density


def tap_adjoint(conv_grad, taps_now, offset):
    lon_cells = conv_grad.shape[0]
    lat_padded = with_halo(conv_grad, (("lat", 1),), 1)
    meridional = taps_now[3] * lat_padded[:, 2:] + taps_now[4] * lat_padded[:, :-2]
    centre = taps_now[1] * conv_grad
    rim_width = 3 * lon_cells
    pieces = []
    for distance in (3, 2, 1, 0, -1, -2, -3):
        pieces.append(conv_grad if distance == 0 else from_behind(conv_grad, "lon", distance))
    padded = jnp.concatenate(pieces, axis=0)
    ahead_cells = lax.dynamic_slice_in_dim(padded, rim_width + offset, lon_cells, 0)
    behind = lax.dynamic_slice_in_dim(padded, rim_width - offset, lon_cells, 0)
    zonal_sum = taps_now[0] * ahead_cells + taps_now[2] * behind
    zonal_sum = lax.optimization_barrier(zonal_sum.astype(jnp.bfloat16)).astype(jnp.float32)
    return zonal_sum + centre + meridional


def by_exchange(dec_cot, saved_conv, dec_weight, w_in, w_out, conv_taps, dilation):
    lon_cells, lat_rows, chans = saved_conv.shape[2:]
    own_cot = dec_cot[0].reshape(-1, dec_cot.shape[3])
    projected = jnp.einsum(
        "nv,cv->nc", own_cot, dec_weight, preferred_element_type=jnp.float32
    ).astype(jnp.bfloat16)
    gradient = lax.optimization_barrier(partner(projected, "segment")).astype(jnp.float32)
    for layer in reversed(range(w_in.shape[0])):
        conv_out = saved_conv[0, layer].reshape(-1, chans)
        hidden = jnp.dot(conv_out, w_in[layer], preferred_element_type=jnp.float32)
        act_grad = jnp.einsum(
            "nc,hc->nh",
            gradient.astype(jnp.bfloat16),
            w_out[layer],
            preferred_element_type=jnp.float32,
        )
        pre_grad = (act_grad * gelu_slope(hidden)).astype(jnp.bfloat16)
        conv_grad = jnp.einsum(
            "nh,ch->nc", pre_grad, w_in[layer], preferred_element_type=jnp.float32
        ).astype(jnp.bfloat16)
        tapped = tap_adjoint(
            conv_grad.reshape(lon_cells, lat_rows, chans), conv_taps[layer], dilation[layer]
        )
        gradient = gradient + tapped.reshape(-1, chans)
    return gradient.reshape(1, lon_cells, lat_rows, chans).astype(jnp.bfloat16)


def routed(value, hop):
    cores, cols, rows = (lax.axis_size(a) for a in AXES)
    pairs = []
    for c in range(cores):
        for z in range(cols):
            for j in range(rows):
                to = hop(c, z, j)
                if to is not None and 0 <= to[2] < rows:
                    pairs.append(((c * cols + z) * rows + j, (to[0] * cols + to[1]) * rows + to[2]))
    return lax.ppermute(value, AXES, pairs)


def row_chunks(low, high):
    count = max(1, round((high - low) / 24))
    edges = [low + (high - low) * i // count for i in range(count + 1)]
    return list(zip(edges[:-1], edges[1:]))


def on_home():
    return lax.axis_index("lon") == lax.axis_index("segment") + 1


GROUPS = ((3, 2), (1, 0))
MESSAGE = {layer: (g, k) for g, group in enumerate(GROUPS) for k, layer in enumerate(group)}


def edge_start(layer):
    return layer * (layer + 1) // 2


def edges_kernel(layers, groups, conv, cot, *outs):
    *messages, top_ref, bottom_ref = outs
    cot = jnp.swapaxes(cot[...].astype(jnp.float32), 0, 1).astype(conv.dtype)
    rows, chans, v = cot.shape[0], conv.shape[3], cot.shape[2]
    for message, group in zip(messages, groups):
        for k, layer in enumerate(group):
            message[:, :, k * chans : (k + 1) * chans] = conv[layer]
    messages[0][:, :, len(groups[0]) * chans :] = cot
    for layer in range(layers):
        here = slice(edge_start(layer), edge_start(layer + 1))
        top_ref[here] = conv[layer, : layer + 1]
        bottom_ref[here] = conv[layer, rows - layer - 1 :]
    for k in range(layers):
        at, lanes = edge_start(layers) + k // 2, slice(k % 2 * v, (k % 2 + 1) * v)
        top_ref[at, :, lanes] = cot[k]
        bottom_ref[at, :, lanes] = cot[rows - layers + k]


def cut_edges(groups, conv, cot):
    layers, rows, cells, chans = conv.shape
    edge = jax.ShapeDtypeStruct((edge_start(layers) + layers // 2, cells, chans), conv.dtype)
    widths = [len(group) * chans for group in groups]
    widths[0] += cot.shape[2]
    messages = [jax.ShapeDtypeStruct((rows, cells, width), conv.dtype) for width in widths]
    vmem = pl.BlockSpec(memory_space=pltpu.VMEM)
    return pl.pallas_call(
        functools.partial(edges_kernel, layers, groups),
        out_shape=messages + [edge, edge],
        in_specs=[vmem, vmem],
        out_specs=[vmem] * (len(groups) + 2),
        compiler_params=pltpu.CompilerParams(vmem_limit_bytes=16 * 2**20),
        name="edges",
    )(conv, cot)


def nt(a, b):
    return lax.dot_general(a, b, (((1,), (1,)), ((), ())), preferred_element_type=jnp.float32)


def halves_of(chans):
    return [(h, slice(h * 128, (h + 1) * 128)) for h in range(chans // 128)]


def in_order(pieces):
    upward = lax.axis_index("segment") == 0
    own, one, two, three = pieces
    return [own, jnp.where(upward, one, three), two, jnp.where(upward, three, one)]


def conv_gradient(conv_out, cot_low, w_in, w_out):
    hidden = jnp.dot(conv_out, w_in, preferred_element_type=jnp.float32)
    pre = (nt(cot_low, w_out) * gelu_slope(hidden)).astype(jnp.bfloat16)
    return nt(pre, w_in)


def keep_row(cg, at, row):
    lon = row.shape[0]
    for h, lanes in halves_of(row.shape[1]):
        cg[at, h, 0:lon] = row[:, lanes]
        cg[at, h, lon : 2 * lon] = row[:, lanes]


def tapped(cg, at, h, taps, offset):
    lon = cg.shape[2] // 2
    total = taps[0] * cg[at, h, pl.ds(offset, lon)] + taps[2] * cg[at, h, pl.ds(lon - offset, lon)]
    total += taps[1] * cg[at, h, 0:lon]
    return total + taps[3] * cg[at + 1, h, 0:lon] + taps[4] * cg[at - 1, h, 0:lon]


def inner_kernel(layer, layers, place, *refs):
    pl.when(on_home())(functools.partial(inner_body, layer, layers, place, *refs))


def inner_body(layer, layers, place, *refs):
    first, last = layer == layers - 1, layer == 0
    offset_ref, mains, refs = refs[0], [refs[1 + k] for k in (3, 1, 0, 2)], refs[5:]
    carried, w_in, w_out, taps, refs = refs[0], refs[1], refs[2], refs[3], refs[4:]
    outs, refs = (refs[:4], refs[4:]) if last else (refs[:1], refs[1:])
    cg_edges, refs = refs[0], refs[1:]
    if first:
        handed_edges, cg, handed = refs
    else:
        (cg,) = refs
    lon, chans = cg_edges.shape[1:]
    cells, rows = lon // 4, cg.shape[0]
    skipped = layers - 1 - layer
    convs, cots = slice(place * chans, (place + 1) * chans), slice(len(GROUPS[0]) * chans, mains[0].shape[2])
    offset = offset_ref[layer]

    def rows_of(r0, r1, lanes):
        found = [in_order([m[skipped + r, :, lanes] for m in mains]) for r in range(r0, r1)]
        return jnp.concatenate(sum(found, []), axis=0)

    def taps_of(r):
        for h, lanes in halves_of(chans):
            total = tapped(cg, r, h, [taps[layer, k : k + 1, lanes] for k in range(5)], offset)
            total += (handed[r, :, lanes].astype(jnp.float32) if first else carried[r, :, lanes])
            if last:
                low = total.astype(jnp.bfloat16)
                quarters = in_order([low[p * cells : (p + 1) * cells] for p in range(4)])
                for p in range(4):
                    outs[p][r - 1, :, lanes] = quarters[p]
            else:
                outs[0][r - 1, :, lanes] = total

    edge_rows = (0, 1, rows - 2, rows - 1)
    for r0, r1 in row_chunks(0, rows):
        if first:
            cot_low = nt(rows_of(r0, r1, cots), carried[...]).astype(jnp.bfloat16)
        else:
            cot_low = carried[r0:r1].reshape((r1 - r0) * lon, chans).astype(jnp.bfloat16)
        conv_grad = conv_gradient(rows_of(r0, r1, convs), cot_low, w_in[layer], w_out[layer])
        conv_grad = conv_grad.reshape(r1 - r0, lon, chans)
        if first:
            handed[r0:r1] = cot_low.reshape(r1 - r0, lon, chans)
        for r in range(r0, r1):
            keep_row(cg, r, conv_grad[r - r0])
            if r in edge_rows:
                cg_edges[edge_rows.index(r)] = conv_grad[r - r0]
    half = (rows - 2) // 2

    def taps_of_half(k, carry):
        for r in range(half):
            taps_of(1 + k * half + r)
        return carry

    lax.fori_loop(0, 2, taps_of_half, 0)
    if first:
        handed_edges[0] = handed[0].astype(jnp.float32)
        handed_edges[1] = handed[rows - 1].astype(jnp.float32)


def run_inner(layer, layers, place, offsets, mains, carried, w_in, w_out, taps):
    first, last = layer == layers - 1, layer == 0
    rows, cells = mains[0].shape[:2]
    chans = w_in.shape[1]
    lon = 4 * cells
    rows -= 2 * (layers - 1 - layer)
    smem = pl.BlockSpec(memory_space=pltpu.SMEM)
    vmem = pl.BlockSpec(memory_space=pltpu.VMEM)
    args = [offsets, *(mains[k] for k in (2, 1, 3, 0)), carried, w_in, w_out, taps]
    if last:
        out = [jax.ShapeDtypeStruct((rows - 2, cells, chans), jnp.bfloat16)] * 4
    else:
        out = [jax.ShapeDtypeStruct((rows - 2, lon, chans), jnp.float32)]
    out.append(jax.ShapeDtypeStruct((4, lon, chans), jnp.float32))
    scratch = [pltpu.VMEM((rows, chans // 128, 2 * lon, 128), jnp.float32)]
    if first:
        out.append(jax.ShapeDtypeStruct((2, lon, chans), jnp.float32))
        scratch.append(pltpu.VMEM((rows, lon, chans), jnp.bfloat16))
    work = rows * lon
    return pl.pallas_call(
        functools.partial(inner_kernel, layer, layers, place),
        out_shape=out,
        in_specs=[smem] + [vmem] * (len(args) - 1),
        out_specs=[vmem] * len(out),
        scratch_shapes=scratch,
        compiler_params=pltpu.CompilerParams(vmem_limit_bytes=24 * 2**20),
        cost_estimate=pl.CostEstimate(
            flops=6 * work * chans * w_in.shape[2],
            bytes_accessed=work * chans * 10,
            transcendentals=2 * work * w_in.shape[2],
        ),
        name=f"inner_{layer}",
    )(*args)


def outer_kernel(layers, *refs):
    pl.when(on_home())(functools.partial(outer_body, layers, *refs))


def outer_body(layers, *refs):
    offset_ref, refs = refs[0], refs[1:]
    halos, mains, refs = refs[:4], (refs[4:8], refs[8:12]), refs[12:]
    inner, refs = refs[:4], refs[4:]
    handed_edges, gradients, refs = refs[0], refs[1:layers], refs[layers:]
    cg_edges, refs = refs[:layers], refs[layers:]
    dec_weight, w_in, w_out, taps, refs = refs[0], refs[1], refs[2], refs[3], refs[4:]
    outs, cg, grad = refs[:4], refs[4:6], refs[6:8]
    rows, cells = mains[0][0].shape[:2]
    lon, chans = cg_edges[0].shape[1:]
    v = dec_weight.shape[1]
    half_halo = halos[0].shape[0] // 2
    lat = lax.axis_index("lat")
    has_above = jnp.where(lat > 0, 1.0, 0.0).astype(jnp.float32)
    has_below = jnp.where(lat < lax.axis_size("lat") - 1, 1.0, 0.0).astype(jnp.float32)

    def conv_row(layer, r):
        if 0 <= r < rows:
            group, place = MESSAGE[layer]
            return in_order([m[r, :, place * chans : (place + 1) * chans] for m in mains[group]])
        at = edge_start(layer) + (r + layer + 1 if r < 0 else half_halo + r - rows)
        return in_order([h[at] for h in halos])

    def cot_row(r):
        k = r + layers if r < 0 else r - rows
        at = edge_start(layers) + k // 2 + (0 if r < 0 else half_halo)
        return in_order([h[at, :, k % 2 * v : (k % 2 + 1) * v] for h in halos])

    def gradient_rows(layer, side):
        shift = layers - 1 - layer
        here = range(-layers + shift, shift) if side == 0 else range(rows - shift, rows - shift + layers)
        if layer == layers - 1:
            cot = jnp.concatenate(sum([cot_row(r) for r in here], []), axis=0)
            cot_low = nt(cot, dec_weight[...]).astype(jnp.bfloat16)
            grad[side][...] = cot_low.astype(jnp.float32).reshape(grad[side].shape)
        else:
            cot_low = grad[side][...].reshape(layers * lon, chans).astype(jnp.bfloat16)
        conv_out = jnp.concatenate(sum([conv_row(layer, r) for r in here], []), axis=0)
        found = conv_gradient(conv_out, cot_low, w_in[layer], w_out[layer])
        found = found.reshape(layers, lon, chans)
        edge = cg_edges[layers - 1 - layer]
        for k, r in enumerate(here):
            row = found[k]
            if r < 0:
                row = row * has_above
            if r >= rows:
                row = row * has_below
            keep_row(cg[side], k if side == 0 else k + 2, row)
        for k in range(2):
            keep_row(cg[side], layers + k if side == 0 else k, edge[k + 2 * side])

    def gradient_taps(layer, side):
        if layer == layers - 1:
            near = handed_edges[side]
        else:
            before = gradients[layers - 2 - layer]
            near = before[0 if side == 0 else before.shape[0] - 1]
        old = [grad[side][k] for k in range(layers)]
        old = [*old[1:], near] if side == 0 else [near, *old[:-1]]
        for k in range(layers):
            for h, lanes in halves_of(chans):
                tap = [taps[layer, n : n + 1, lanes] for n in range(5)]
                total = old[k][:, lanes] + tapped(cg[side], k + 1, h, tap, offset_ref[layer])
                if layer:
                    grad[side][k, :, lanes] = total
                else:
                    quarters = quarters_of(total.astype(jnp.bfloat16))
                    r = k if side == 0 else rows - layers + k
                    for p in range(4):
                        outs[p][r, :, lanes] = quarters[p]

    def quarters_of(row):
        return in_order([row[p * cells : (p + 1) * cells] for p in range(4)])

    for p in range(4):
        outs[p][layers : rows - layers] = inner[p][...]
    gradient_rows(layers - 1, 0)
    for layer in reversed(range(layers)):
        gradient_rows(layer, 1)
        gradient_taps(layer, 0)
        if layer:
            gradient_rows(layer - 1, 0)
        gradient_taps(layer, 1)


def run_outer(layers, offsets, halos, mains, inner, handed_edges, gradients, cg_edges, weights):
    rows, cells = mains[0][0].shape[:2]
    lon, chans = cg_edges[0].shape[1:]
    smem = pl.BlockSpec(memory_space=pltpu.SMEM)
    vmem = pl.BlockSpec(memory_space=pltpu.VMEM)
    args = [offsets, *halos, *mains[0], *mains[1], *inner, handed_edges, *gradients, *cg_edges]
    args += weights
    work = 2 * layers * layers * lon
    return pl.pallas_call(
        functools.partial(outer_kernel, layers),
        out_shape=[jax.ShapeDtypeStruct((rows, cells, chans), jnp.bfloat16)] * 4,
        in_specs=[smem] + [vmem] * (len(args) - 1),
        out_specs=[vmem] * 4,
        scratch_shapes=[
            *[pltpu.VMEM((layers + 2, chans // 128, 2 * lon, 128), jnp.float32)] * 2,
            *[pltpu.VMEM((layers, lon, chans), jnp.float32)] * 2,
        ],
        compiler_params=pltpu.CompilerParams(vmem_limit_bytes=24 * 2**20),
        cost_estimate=pl.CostEstimate(
            flops=6 * work * chans * weights[1].shape[2],
            bytes_accessed=work * chans * 10,
            transcendentals=2 * work * weights[1].shape[2],
        ),
        name="outer",
    )(*args)


def by_circles(dec_cot, saved_conv, dec_weight, w_in, w_out, conv_taps, dilation):
    layers = w_in.shape[0]

    def home(c):
        return c + 1

    def away(c, k):
        return (home(c) + (k if c == 0 else -k)) % 4

    order = (3, 1, 2)

    def gather(value):
        found = {0: value}
        for k in order:
            found[k] = routed(
                value, lambda c, z, j: (c, home(c), j) if z == away(c, k) else None
            )
        return [found[k] for k in range(4)]

    def neighbours(c, z, j):
        if z == away(c, 1):
            return c, home(c), j
        if z == away(c, 2):
            return 1 - c, home(c), j

    def across(c, z, j):
        return (1 - c, z, j) if z == home(1 - c) else None

    cot = partner(dec_cot[0], "segment")
    conv = saved_conv[0].transpose(0, 2, 1, 3)
    early, late, top, bottom = cut_edges(GROUPS, conv, cot)
    first = gather(early)
    below = routed(top, lambda c, z, j: (c, z, j - 1))
    above = routed(bottom, lambda c, z, j: (c, z, j + 1))

    two = routed(late, lambda c, z, j: (c, home(c), j) if z == away(c, 2) else None)
    sides, above, below = lax.optimization_barrier((late, above, below))
    one = routed(sides, lambda c, z, j: (c, home(c), j) if z == away(c, 1) else None)
    three = routed(sides, lambda c, z, j: (c, home(c), j) if z == away(c, 3) else None)
    second = [late, one, two, three]

    carried, gradients, cg_edges = dec_weight, [], []
    for layer in reversed(range(layers)):
        group, place = MESSAGE[layer]
        mains = (first, second)[group]
        found = run_inner(
            layer, layers, place, dilation, mains, carried, w_in, w_out, conv_taps
        )
        if layer == layers - 1:
            carried, cg_edge, handed_edges = found
        elif layer:
            carried, cg_edge = found
        else:
            *inner, cg_edge = found
        cg_edges.append(cg_edge)
        if layer:
            gradients.append(carried)
        if layer == layers - 1:
            edges = jnp.concatenate([above, below], axis=0)
            edges, carried = lax.optimization_barrier((edges, carried))
            one = routed(edges, neighbours)
            three = routed(edges, lambda c, z, j: (c, home(c), j) if z == away(c, 3) else None)
        if layer == 1:
            one, carried = lax.optimization_barrier((one, carried))
            halos = [edges, one, routed(one, across), three]
    weights = [dec_weight, w_in, w_out, conv_taps]
    found = run_outer(
        layers, dilation, halos, (first, second), inner, handed_edges, gradients, cg_edges, weights
    )

    result = jnp.where(on_home(), found[0], 0)
    for k in (2, 3, 1):
        result = result + routed(
            found[k], lambda c, z, j: (c, away(c, k), j) if z == home(c) else None
        )
    return result.transpose(1, 0, 2)[None]


def solution(mesh):
    in_specs = (
        P("segment", "lon", "lat", None),
        P("segment", None, "lon", "lat", None),
        P(),
        P(),
        P(),
        P(),
        P(),
    )
    out_specs = P("segment", "lon", "lat", None)
    gathers = mesh.shape["lon"] == 4 and mesh.shape["segment"] == 2
    return jax.shard_map(
        by_circles if gathers else by_exchange,
        mesh=mesh,
        in_specs=in_specs,
        out_specs=out_specs,
        check_vma=False,
    )
```

```python
import functools

import jax
import jax.numpy as jnp
from jax import lax
from jax.experimental import pallas as pl
from jax.experimental.pallas import tpu as pltpu
from jax.sharding import PartitionSpec as P

AXES = ("segment", "lon", "lat")


def with_halo(cells, sides, width):
    for axis, dim in sides:
        count = lax.axis_size(axis)
        ends = count - 1
        head = lax.slice_in_dim(cells, 0, width, axis=dim)
        tail = lax.slice_in_dim(cells, cells.shape[dim] - width, cells.shape[dim], axis=dim)
        cells = jnp.concatenate(
            [
                lax.ppermute(tail, axis, [(i, (i + 1) % count) for i in range(ends)]),
                cells,
                lax.ppermute(head, axis, [((i + 1) % count, i) for i in range(ends)]),
            ],
            axis=dim,
        )
    return cells


def from_behind(value, axis, steps):
    count = lax.axis_size(axis)
    pairs = [(source, (source + steps) % count) for source in range(count)]
    return lax.ppermute(value, axis, pairs)


def partner(block, axis):
    count = lax.axis_size(axis)
    return lax.ppermute(block, axis, [(i, i ^ 1) for i in range(count) if i ^ 1 < count])


def gelu_slope(hidden):
    normal_cdf = 0.5 * (1.0 + lax.erf(hidden * 0.7071067811865476))
    density = jnp.exp(-0.5 * hidden * hidden) * 0.3989422804014327
    return normal_cdf + hidden * density


def tap_adjoint(conv_grad, taps_now, offset):
    lon_cells = conv_grad.shape[0]
    lat_padded = with_halo(conv_grad, (("lat", 1),), 1)
    meridional = taps_now[3] * lat_padded[:, 2:] + taps_now[4] * lat_padded[:, :-2]
    centre = taps_now[1] * conv_grad
    rim_width = 3 * lon_cells
    pieces = []
    for distance in (3, 2, 1, 0, -1, -2, -3):
        pieces.append(conv_grad if distance == 0 else from_behind(conv_grad, "lon", distance))
    padded = jnp.concatenate(pieces, axis=0)
    ahead_cells = lax.dynamic_slice_in_dim(padded, rim_width + offset, lon_cells, 0)
    behind = lax.dynamic_slice_in_dim(padded, rim_width - offset, lon_cells, 0)
    zonal_sum = taps_now[0] * ahead_cells + taps_now[2] * behind
    zonal_sum = lax.optimization_barrier(zonal_sum.astype(jnp.bfloat16)).astype(jnp.float32)
    return zonal_sum + centre + meridional


def by_exchange(dec_cot, saved_conv, dec_weight, w_in, w_out, conv_taps, dilation):
    lon_cells, lat_rows, chans = saved_conv.shape[2:]
    own_cot = dec_cot[0].reshape(-1, dec_cot.shape[3])
    projected = jnp.einsum(
        "nv,cv->nc", own_cot, dec_weight, preferred_element_type=jnp.float32
    ).astype(jnp.bfloat16)
    gradient = lax.optimization_barrier(partner(projected, "segment")).astype(jnp.float32)
    for layer in reversed(range(w_in.shape[0])):
        conv_out = saved_conv[0, layer].reshape(-1, chans)
        hidden = jnp.dot(conv_out, w_in[layer], preferred_element_type=jnp.float32)
        act_grad = jnp.einsum(
            "nc,hc->nh",
            gradient.astype(jnp.bfloat16),
            w_out[layer],
            preferred_element_type=jnp.float32,
        )
        pre_grad = (act_grad * gelu_slope(hidden)).astype(jnp.bfloat16)
        conv_grad = jnp.einsum(
            "nh,ch->nc", pre_grad, w_in[layer], preferred_element_type=jnp.float32
        ).astype(jnp.bfloat16)
        tapped = tap_adjoint(
            conv_grad.reshape(lon_cells, lat_rows, chans), conv_taps[layer], dilation[layer]
        )
        gradient = gradient + tapped.reshape(-1, chans)
    return gradient.reshape(1, lon_cells, lat_rows, chans).astype(jnp.bfloat16)


def routed(value, hop):
    cores, cols, rows = (lax.axis_size(a) for a in AXES)
    pairs = []
    for c in range(cores):
        for z in range(cols):
            for j in range(rows):
                to = hop(c, z, j)
                if to is not None and 0 <= to[2] < rows:
                    pairs.append(((c * cols + z) * rows + j, (to[0] * cols + to[1]) * rows + to[2]))
    return lax.ppermute(value, AXES, pairs)


def row_chunks(low, high):
    count = max(1, round((high - low) / 24))
    edges = [low + (high - low) * i // count for i in range(count + 1)]
    return list(zip(edges[:-1], edges[1:]))


def on_home():
    return lax.axis_index("lon") == lax.axis_index("segment") + 1


GROUPS = ((3, 2), (1, 0))
MESSAGE = {layer: (g, k) for g, group in enumerate(GROUPS) for k, layer in enumerate(group)}


def edge_start(layer):
    return layer * (layer + 1) // 2


def edges_kernel(layers, groups, conv, cot, *outs):
    *messages, top_ref, bottom_ref = outs
    cot = jnp.swapaxes(cot[...].astype(jnp.float32), 0, 1).astype(conv.dtype)
    rows, chans, v = cot.shape[0], conv.shape[3], cot.shape[2]
    for message, group in zip(messages, groups):
        for k, layer in enumerate(group):
            message[:, :, k * chans : (k + 1) * chans] = conv[layer]
    messages[0][:, :, len(groups[0]) * chans :] = cot
    for layer in range(layers):
        here = slice(edge_start(layer), edge_start(layer + 1))
        top_ref[here] = conv[layer, : layer + 1]
        bottom_ref[here] = conv[layer, rows - layer - 1 :]
    for k in range(layers):
        at, lanes = edge_start(layers) + k // 2, slice(k % 2 * v, (k % 2 + 1) * v)
        top_ref[at, :, lanes] = cot[k]
        bottom_ref[at, :, lanes] = cot[rows - layers + k]


def cut_edges(groups, conv, cot):
    layers, rows, cells, chans = conv.shape
    edge = jax.ShapeDtypeStruct((edge_start(layers) + layers // 2, cells, chans), conv.dtype)
    widths = [len(group) * chans for group in groups]
    widths[0] += cot.shape[2]
    messages = [jax.ShapeDtypeStruct((rows, cells, width), conv.dtype) for width in widths]
    vmem = pl.BlockSpec(memory_space=pltpu.VMEM)
    return pl.pallas_call(
        functools.partial(edges_kernel, layers, groups),
        out_shape=messages + [edge, edge],
        in_specs=[vmem, vmem],
        out_specs=[vmem] * (len(groups) + 2),
        compiler_params=pltpu.CompilerParams(vmem_limit_bytes=16 * 2**20),
        name="edges",
    )(conv, cot)


def nt(a, b):
    return lax.dot_general(a, b, (((1,), (1,)), ((), ())), preferred_element_type=jnp.float32)


def halves_of(chans):
    return [(h, slice(h * 128, (h + 1) * 128)) for h in range(chans // 128)]


def in_order(pieces):
    upward = lax.axis_index("segment") == 0
    own, one, two, three = pieces
    return [own, jnp.where(upward, one, three), two, jnp.where(upward, three, one)]


def conv_gradient(conv_out, cot_low, w_in, w_out):
    hidden = jnp.dot(conv_out, w_in, preferred_element_type=jnp.float32)
    pre = (nt(cot_low, w_out) * gelu_slope(hidden)).astype(jnp.bfloat16)
    return nt(pre, w_in)


def keep_row(cg, at, row):
    lon = row.shape[0]
    for h, lanes in halves_of(row.shape[1]):
        cg[at, h, 0:lon] = row[:, lanes]
        cg[at, h, lon : 2 * lon] = row[:, lanes]


def tapped(cg, at, h, taps, offset):
    lon = cg.shape[2] // 2
    total = taps[0] * cg[at, h, pl.ds(offset, lon)] + taps[2] * cg[at, h, pl.ds(lon - offset, lon)]
    total += taps[1] * cg[at, h, 0:lon]
    return total + taps[3] * cg[at + 1, h, 0:lon] + taps[4] * cg[at - 1, h, 0:lon]


def inner_kernel(layer, layers, place, *refs):
    pl.when(on_home())(functools.partial(inner_body, layer, layers, place, *refs))


def inner_body(layer, layers, place, *refs):
    first, last = layer == layers - 1, layer == 0
    offset_ref, mains, refs = refs[0], [refs[1 + k] for k in (3, 1, 0, 2)], refs[5:]
    carried, w_in, w_out, taps, refs = refs[0], refs[1], refs[2], refs[3], refs[4:]
    outs, refs = (refs[:4], refs[4:]) if last else (refs[:1], refs[1:])
    cg_edges, refs = refs[0], refs[1:]
    if first:
        handed_edges, cg, handed = refs
    else:
        (cg,) = refs
    lon, chans = cg_edges.shape[1:]
    cells, rows = lon // 4, cg.shape[0]
    skipped = layers - 1 - layer
    convs, cots = slice(place * chans, (place + 1) * chans), slice(len(GROUPS[0]) * chans, mains[0].shape[2])
    offset = offset_ref[layer]

    def rows_of(r0, r1, lanes):
        found = [in_order([m[skipped + r, :, lanes] for m in mains]) for r in range(r0, r1)]
        return jnp.concatenate(sum(found, []), axis=0)

    def taps_of(at):
        found = []
        for r in at:
            for h, lanes in halves_of(chans):
                total = tapped(cg, r, h, [taps[layer, k : k + 1, lanes] for k in range(5)], offset)
                before = handed[r, :, lanes].astype(jnp.float32) if first else carried[r, :, lanes]
                found.append((r, lanes, total + before))
        for r, lanes, total in found:
            if last:
                low = total.astype(jnp.bfloat16)
                quarters = in_order([low[p * cells : (p + 1) * cells] for p in range(4)])
                for p in range(4):
                    outs[p][r - 1, :, lanes] = quarters[p]
            else:
                outs[0][r - 1, :, lanes] = total

    edge_rows = (0, 1, rows - 2, rows - 1)
    for r0, r1 in row_chunks(0, rows):
        if first:
            cot_low = nt(rows_of(r0, r1, cots), carried[...]).astype(jnp.bfloat16)
        else:
            cot_low = carried[r0:r1].reshape((r1 - r0) * lon, chans).astype(jnp.bfloat16)
        conv_grad = conv_gradient(rows_of(r0, r1, convs), cot_low, w_in[layer], w_out[layer])
        conv_grad = conv_grad.reshape(r1 - r0, lon, chans)
        if first:
            handed[r0:r1] = cot_low.reshape(r1 - r0, lon, chans)
        for r in range(r0, r1):
            keep_row(cg, r, conv_grad[r - r0])
            if r in edge_rows:
                cg_edges[edge_rows.index(r)] = conv_grad[r - r0]
    half = (rows - 2) // 2

    def taps_of_half(k, carry):
        for r in range(0, half, 2):
            taps_of([1 + k * half + n for n in range(r, min(r + 2, half))])
        return carry

    lax.fori_loop(0, 2, taps_of_half, 0)
    if first:
        handed_edges[0] = handed[0].astype(jnp.float32)
        handed_edges[1] = handed[rows - 1].astype(jnp.float32)


def run_inner(layer, layers, place, offsets, mains, carried, w_in, w_out, taps):
    first, last = layer == layers - 1, layer == 0
    rows, cells = mains[0].shape[:2]
    chans = w_in.shape[1]
    lon = 4 * cells
    rows -= 2 * (layers - 1 - layer)
    smem = pl.BlockSpec(memory_space=pltpu.SMEM)
    vmem = pl.BlockSpec(memory_space=pltpu.VMEM)
    args = [offsets, *(mains[k] for k in (2, 1, 3, 0)), carried, w_in, w_out, taps]
    if last:
        out = [jax.ShapeDtypeStruct((rows - 2, cells, chans), jnp.bfloat16)] * 4
    else:
        out = [jax.ShapeDtypeStruct((rows - 2, lon, chans), jnp.float32)]
    out.append(jax.ShapeDtypeStruct((4, lon, chans), jnp.float32))
    scratch = [pltpu.VMEM((rows, chans // 128, 2 * lon, 128), jnp.float32)]
    if first:
        out.append(jax.ShapeDtypeStruct((2, lon, chans), jnp.float32))
        scratch.append(pltpu.VMEM((rows, lon, chans), jnp.bfloat16))
    work = rows * lon
    return pl.pallas_call(
        functools.partial(inner_kernel, layer, layers, place),
        out_shape=out,
        in_specs=[smem] + [vmem] * (len(args) - 1),
        out_specs=[vmem] * len(out),
        scratch_shapes=scratch,
        compiler_params=pltpu.CompilerParams(vmem_limit_bytes=24 * 2**20),
        cost_estimate=pl.CostEstimate(
            flops=6 * work * chans * w_in.shape[2],
            bytes_accessed=work * chans * 10,
            transcendentals=2 * work * w_in.shape[2],
        ),
        name=f"inner_{layer}",
    )(*args)


def outer_kernel(layers, *refs):
    pl.when(on_home())(functools.partial(outer_body, layers, *refs))


def outer_body(layers, *refs):
    offset_ref, refs = refs[0], refs[1:]
    halos, mains, refs = refs[:4], (refs[4:8], refs[8:12]), refs[12:]
    inner, refs = refs[:4], refs[4:]
    handed_edges, gradients, refs = refs[0], refs[1:layers], refs[layers:]
    cg_edges, refs = refs[:layers], refs[layers:]
    dec_weight, w_in, w_out, taps, refs = refs[0], refs[1], refs[2], refs[3], refs[4:]
    outs, cg, grad = refs[:4], refs[4:6], refs[6:8]
    rows, cells = mains[0][0].shape[:2]
    lon, chans = cg_edges[0].shape[1:]
    v = dec_weight.shape[1]
    half_halo = halos[0].shape[0] // 2
    lat = lax.axis_index("lat")
    has_above = jnp.where(lat > 0, 1.0, 0.0).astype(jnp.float32)
    has_below = jnp.where(lat < lax.axis_size("lat") - 1, 1.0, 0.0).astype(jnp.float32)

    def conv_row(layer, r):
        if 0 <= r < rows:
            group, place = MESSAGE[layer]
            return in_order([m[r, :, place * chans : (place + 1) * chans] for m in mains[group]])
        at = edge_start(layer) + (r + layer + 1 if r < 0 else half_halo + r - rows)
        return in_order([h[at] for h in halos])

    def cot_row(r):
        k = r + layers if r < 0 else r - rows
        at = edge_start(layers) + k // 2 + (0 if r < 0 else half_halo)
        return in_order([h[at, :, k % 2 * v : (k % 2 + 1) * v] for h in halos])

    def gradient_rows(layer, side):
        shift = layers - 1 - layer
        here = range(-layers + shift, shift) if side == 0 else range(rows - shift, rows - shift + layers)
        if layer == layers - 1:
            cot = jnp.concatenate(sum([cot_row(r) for r in here], []), axis=0)
            cot_low = nt(cot, dec_weight[...]).astype(jnp.bfloat16)
            grad[side][...] = cot_low.astype(jnp.float32).reshape(grad[side].shape)
        else:
            cot_low = grad[side][...].reshape(layers * lon, chans).astype(jnp.bfloat16)
        conv_out = jnp.concatenate(sum([conv_row(layer, r) for r in here], []), axis=0)
        found = conv_gradient(conv_out, cot_low, w_in[layer], w_out[layer])
        found = found.reshape(layers, lon, chans)
        edge = cg_edges[layers - 1 - layer]
        for k, r in enumerate(here):
            row = found[k]
            if r < 0:
                row = row * has_above
            if r >= rows:
                row = row * has_below
            keep_row(cg[side], k if side == 0 else k + 2, row)
        for k in range(2):
            keep_row(cg[side], layers + k if side == 0 else k, edge[k + 2 * side])

    def gradient_taps(layer, side):
        if layer == layers - 1:
            near = handed_edges[side]
        else:
            before = gradients[layers - 2 - layer]
            near = before[0 if side == 0 else before.shape[0] - 1]
        old = [grad[side][k] for k in range(layers)]
        old = [*old[1:], near] if side == 0 else [near, *old[:-1]]
        for k in range(layers):
            for h, lanes in halves_of(chans):
                tap = [taps[layer, n : n + 1, lanes] for n in range(5)]
                total = old[k][:, lanes] + tapped(cg[side], k + 1, h, tap, offset_ref[layer])
                if layer:
                    grad[side][k, :, lanes] = total
                else:
                    quarters = quarters_of(total.astype(jnp.bfloat16))
                    r = k if side == 0 else rows - layers + k
                    for p in range(4):
                        outs[p][r, :, lanes] = quarters[p]

    def quarters_of(row):
        return in_order([row[p * cells : (p + 1) * cells] for p in range(4)])

    for p in range(4):
        outs[p][layers : rows - layers] = inner[p][...]
    gradient_rows(layers - 1, 0)
    for layer in reversed(range(layers)):
        gradient_rows(layer, 1)
        gradient_taps(layer, 0)
        if layer:
            gradient_rows(layer - 1, 0)
        gradient_taps(layer, 1)


def run_outer(layers, offsets, halos, mains, inner, handed_edges, gradients, cg_edges, weights):
    rows, cells = mains[0][0].shape[:2]
    lon, chans = cg_edges[0].shape[1:]
    smem = pl.BlockSpec(memory_space=pltpu.SMEM)
    vmem = pl.BlockSpec(memory_space=pltpu.VMEM)
    args = [offsets, *halos, *mains[0], *mains[1], *inner, handed_edges, *gradients, *cg_edges]
    args += weights
    work = 2 * layers * layers * lon
    return pl.pallas_call(
        functools.partial(outer_kernel, layers),
        out_shape=[jax.ShapeDtypeStruct((rows, cells, chans), jnp.bfloat16)] * 4,
        in_specs=[smem] + [vmem] * (len(args) - 1),
        out_specs=[vmem] * 4,
        scratch_shapes=[
            *[pltpu.VMEM((layers + 2, chans // 128, 2 * lon, 128), jnp.float32)] * 2,
            *[pltpu.VMEM((layers, lon, chans), jnp.float32)] * 2,
        ],
        compiler_params=pltpu.CompilerParams(vmem_limit_bytes=24 * 2**20),
        cost_estimate=pl.CostEstimate(
            flops=6 * work * chans * weights[1].shape[2],
            bytes_accessed=work * chans * 10,
            transcendentals=2 * work * weights[1].shape[2],
        ),
        name="outer",
    )(*args)


def by_circles(dec_cot, saved_conv, dec_weight, w_in, w_out, conv_taps, dilation):
    layers = w_in.shape[0]

    def home(c):
        return c + 1

    def away(c, k):
        return (home(c) + (k if c == 0 else -k)) % 4

    order = (3, 1, 2)

    def gather(value):
        found = {0: value}
        for k in order:
            found[k] = routed(
                value, lambda c, z, j: (c, home(c), j) if z == away(c, k) else None
            )
        return [found[k] for k in range(4)]

    def neighbours(c, z, j):
        if z == away(c, 1):
            return c, home(c), j
        if z == away(c, 2):
            return 1 - c, home(c), j

    def across(c, z, j):
        return (1 - c, z, j) if z == home(1 - c) else None

    cot = partner(dec_cot[0], "segment")
    conv = saved_conv[0].transpose(0, 2, 1, 3)
    early, late, top, bottom = cut_edges(GROUPS, conv, cot)
    first = gather(early)
    below = routed(top, lambda c, z, j: (c, z, j - 1))
    above = routed(bottom, lambda c, z, j: (c, z, j + 1))

    two = routed(late, lambda c, z, j: (c, home(c), j) if z == away(c, 2) else None)
    sides, above, below = lax.optimization_barrier((late, above, below))
    one = routed(sides, lambda c, z, j: (c, home(c), j) if z == away(c, 1) else None)
    three = routed(sides, lambda c, z, j: (c, home(c), j) if z == away(c, 3) else None)
    second = [late, one, two, three]

    carried, gradients, cg_edges = dec_weight, [], []
    for layer in reversed(range(layers)):
        group, place = MESSAGE[layer]
        mains = (first, second)[group]
        found = run_inner(
            layer, layers, place, dilation, mains, carried, w_in, w_out, conv_taps
        )
        if layer == layers - 1:
            carried, cg_edge, handed_edges = found
        elif layer:
            carried, cg_edge = found
        else:
            *inner, cg_edge = found
        cg_edges.append(cg_edge)
        if layer:
            gradients.append(carried)
        if layer == layers - 1:
            edges = jnp.concatenate([above, below], axis=0)
            edges, carried = lax.optimization_barrier((edges, carried))
            one = routed(edges, neighbours)
            three = routed(edges, lambda c, z, j: (c, home(c), j) if z == away(c, 3) else None)
        if layer == 1:
            one, carried = lax.optimization_barrier((one, carried))
            halos = [edges, one, routed(one, across), three]
    weights = [dec_weight, w_in, w_out, conv_taps]
    found = run_outer(
        layers, dilation, halos, (first, second), inner, handed_edges, gradients, cg_edges, weights
    )

    result = jnp.where(on_home(), found[0], 0)
    for k in (2, 3, 1):
        result = result + routed(
            found[k], lambda c, z, j: (c, away(c, k), j) if z == home(c) else None
        )
    return result.transpose(1, 0, 2)[None]


def solution(mesh):
    in_specs = (
        P("segment", "lon", "lat", None),
        P("segment", None, "lon", "lat", None),
        P(),
        P(),
        P(),
        P(),
        P(),
    )
    out_specs = P("segment", "lon", "lat", None)
    gathers = mesh.shape["lon"] == 4 and mesh.shape["segment"] == 2
    return jax.shard_map(
        by_circles if gathers else by_exchange,
        mesh=mesh,
        in_specs=in_specs,
        out_specs=out_specs,
        check_vma=False,
    )
```
